32 devices in a mesh: chan: 16 (over z, x, core), win: 2 (over y).
Axes of the slice: x: 2, y: 2, z: 4, core: 2. Of those that a mesh axis runs over, the one named last changes fastest.
Arguments:
- records: float32 [64, 16, 8192], P('chan', 'win'), may hold values from -80 to 80, as said below
- positions: int32 [64], replicated, may hold values from 0 to 7843, as said below
Outputs:
- stacks: float32 [4, 64, 4, 2, 4096], P(None, 'chan', None, None, 'win')
The draws below stay inside these ranges and needn't reach their ends.
Inputs may be any that keep to these rules, and one draw needn't show every extreme that they name: `positions`: positions rise along the channels by 62 to 187 metres from one channel to the next; the first is 0. `records`: records of different channels and windows differ in scale.
All inputs are finite; a program needn't handle non-finite values.
Results may differ from the reference program's by a relative error of at most 0.004.
Values may be sent and summed in bfloat16 or wider, within the bound.
No kernel may reach another device: no remote copies, remote signals or barrier semaphores. Data moves between devices by JAX's collectives and lax.ppermute only.
A program may use at most 128 MiB of HBM per device.

```python
import math
import jax
import jax.numpy as jnp
from jax import lax

CH_DEV = 4
BINS = 4096
BAND = 128
ROUNDS = 4
REACH = 2000
SAMPLES = 8192
CHANNELS = 64
WINDOWS = 16


def draw_records(key, part):
    key = jax.random.fold_in(key, 11)
    key_scale, key_noise = jax.random.split(key, 2)
    row_scale = jnp.exp(jax.random.uniform(key_scale, (CHANNELS, WINDOWS, 1), jnp.float32, 0.0, math.log(10.0)))
    drawn_values = jax.random.truncated_normal(key_noise, -6.0, 6.0, (CHANNELS, WINDOWS, SAMPLES), jnp.float32) * row_scale
    return drawn_values.astype(jnp.float32)


def draw_positions(key, part):
    key = jax.random.fold_in(key, 23)
    low_step = 250 // CH_DEV
    high_step = 750 // CH_DEV
    step_total = low_step + high_step
    first_steps = jax.random.randint(key, ((CHANNELS - 2) // 2,), low_step, high_step + 1).astype(jnp.int32)
    paired = jnp.stack([first_steps, step_total - first_steps], axis=1).reshape(-1)
    spacing = jnp.concatenate([jnp.full((1,), step_total // 2, jnp.int32), paired]).astype(jnp.int32)
    rising = jnp.cumsum(spacing).astype(jnp.int32)
    return jnp.concatenate([jnp.zeros((1,), jnp.int32), rising]).astype(jnp.int32)


def setup_inputs(seed: int = 0) -> dict:
    splits = jax.random.split(jax.random.key(seed), 3)
    return {
        "records": draw_records(jax.random.fold_in(splits[2], 71), 0),
        "positions": draw_positions(jax.random.fold_in(splits[2], 71), 0),
    }


band_epsilon = 1e-06

def whiten_channel(chan_records):
    transformed = jnp.fft.rfft(chan_records, axis=-1)[:, :BINS]
    spec_real = jnp.real(transformed).astype(jnp.float32)
    spec_imag = jnp.imag(transformed).astype(jnp.float32)
    win_count = chan_records.shape[0]
    band_power = lax.optimization_barrier(jnp.mean((spec_real * spec_real + spec_imag * spec_imag).reshape(win_count, BINS // BAND, BAND), axis=-1, keepdims=True))
    whiten_scale = jnp.broadcast_to(lax.rsqrt(band_power + band_epsilon), (win_count, BINS // BAND, BAND)).reshape(win_count, BINS)
    return jnp.stack([spec_real * whiten_scale, spec_imag * whiten_scale], axis=1).astype(jnp.bfloat16)

def block_cross(pair_blocks):
    mine_block, their_block = pair_blocks
    mine_real = mine_block[:, :, 0].astype(jnp.float32)
    mine_imag = mine_block[:, :, 1].astype(jnp.float32)
    their_real = their_block[:, :, 0].astype(jnp.float32)
    their_imag = their_block[:, :, 1].astype(jnp.float32)
    cross_real = jnp.einsum('awf,bwf->abf', mine_real, their_real) + jnp.einsum('awf,bwf->abf', mine_imag, their_imag)
    cross_imag = jnp.einsum('awf,bwf->abf', mine_imag, their_real) - jnp.einsum('awf,bwf->abf', mine_real, their_imag)
    return jnp.stack([cross_real, cross_imag], axis=2)

def reference(records, positions):
    white = lax.map(whiten_channel, records)
    block_count = CHANNELS // CH_DEV
    spectra_blocks = white.reshape(block_count, CH_DEV, WINDOWS, 2, BINS)
    pos_blocks = positions.reshape(block_count, CH_DEV)
    inv_root = 1.0 / math.sqrt(WINDOWS)
    results = []
    for offset in range(1, ROUNDS + 1):
        partner_blocks = jnp.concatenate([spectra_blocks[offset:], jnp.zeros_like(spectra_blocks[:offset])], axis=0)
        partner_pos = jnp.concatenate([pos_blocks[offset:], pos_blocks[:offset]], axis=0)
        cross_sums = lax.map(block_cross, (spectra_blocks, partner_blocks))
        within = (partner_pos[:, None, :] - pos_blocks[:, :, None] <= REACH).astype(jnp.float32)
        stacked = cross_sums * inv_root * within[:, :, :, None, None]
        results.append(stacked.reshape(CHANNELS, CH_DEV, 2, BINS))
    return jnp.stack(results, axis=0)
```

```python
import functools
import math

import jax
import jax.numpy as jnp
import numpy as np
from jax import lax
from jax.experimental import pallas as pl
from jax.experimental.pallas import tpu as pltpu
from jax.sharding import PartitionSpec as P
import ml_dtypes

BINS = 4096
BAND = 128
ROUNDS = 4
REACH = 2000
LANES = 128
band_epsilon = 1e-06


def split3_np(table):
    hi = table.astype(ml_dtypes.bfloat16)
    rest = table - hi.astype(np.float64)
    mid = rest.astype(ml_dtypes.bfloat16)
    lo = (rest - mid.astype(np.float64)).astype(ml_dtypes.bfloat16)
    return hi, mid, lo


def six_np(table):
    hi, mid, lo = split3_np(table)
    return np.concatenate([hi, hi, hi, mid, mid, lo], axis=-1)


def dft_tables(samples, parts):
    first = samples // LANES
    p = np.arange(first)
    q = np.arange(LANES)
    k1 = np.arange(first)
    angle = 2.0 * np.pi * ((k1[:, None] * p[None, :]) % first) / first
    stage1 = six_np(np.concatenate([np.cos(angle), -np.sin(angle)], axis=0))
    angle = 2.0 * np.pi * ((k1[:, None] * q[None, :]) % samples) / samples
    twiddle = np.stack([np.cos(angle), np.sin(angle)]).astype(np.float32)
    bands = BINS // BAND // parts
    rows = []
    for part in range(parts):
        pieces = []
        for imag in (False, True):
            for odd in (0, 1):
                m = 2 * (part * bands + np.arange(bands)) + odd
                angle = 2.0 * np.pi * ((m[:, None] * q[None, :]) % LANES) / LANES
                cos, sin = np.cos(angle), np.sin(angle)
                pieces.append(np.concatenate([-sin, cos] if imag else [cos, sin], axis=1))
        rows.append(np.concatenate(pieces, axis=0))
    stage2 = six_np(np.stack(rows))
    half = np.arange(LANES) // first
    ones = (half[:, None] == half[None, :]).astype(ml_dtypes.bfloat16)
    return stage1, twiddle, stage2, np.concatenate([ones] * 3, axis=0)


def split3(value):
    hi = value.astype(jnp.bfloat16)
    rest = value - hi.astype(jnp.float32)
    mid = rest.astype(jnp.bfloat16)
    lo = (rest - mid.astype(jnp.float32)).astype(jnp.bfloat16)
    return hi, mid, lo


def six(value, axis):
    hi, mid, lo = split3(value)
    return jnp.concatenate([hi, mid, lo, hi, mid, hi], axis=axis)


def spectra_kernel(parts, x_ref, l1_ref, tw_ref, l2_ref, ones_ref, *out_refs):
    chans, first, wins, _ = x_ref.shape
    bands = BINS // BAND // parts
    me = lax.axis_index("win")
    cos, sin = tw_ref[0], tw_ref[1]
    l1 = l1_ref[...]
    l2 = jnp.concatenate([l2_ref[lax.rem(me + s, parts)] for s in range(parts)], axis=0)
    ones = ones_ref[...]
    left = lax.broadcasted_iota(jnp.int32, (bands, LANES), 1) < first
    group = 4
    rows_ref = x_ref.reshape(chans * first * wins, LANES)
    for chan in range(chans):
        for start in range(0, wins, group):
            base = chan * first * wins + start
            x = jnp.concatenate(
                [rows_ref[pl.ds(base + i, first, stride=wins), :] for i in range(group)], axis=1
            )
            t = jnp.dot(l1, six(x, 0), preferred_element_type=jnp.float32)
            rows = []
            for i in range(group):
                tr = t[:first, i * LANES : (i + 1) * LANES]
                ti = t[first:, i * LANES : (i + 1) * LANES]
                rows.append(jnp.concatenate([tr * cos + ti * sin, ti * cos - tr * sin], axis=1))
            rhs = six(jnp.concatenate(rows, axis=0), 1)
            spec = lax.dot_general(
                l2, rhs, (((1,), (1,)), ((), ())), preferred_element_type=jnp.float32
            )
            for pair in range(group // 2):
                part = spec[:, pair * LANES : (pair + 1) * LANES].reshape(parts, 4, bands, LANES)
                square = part * part
                power = square[:, 0] + square[:, 1] + square[:, 2] + square[:, 3]
                power = power.reshape(parts * bands, LANES)
                total = jnp.dot(
                    jnp.concatenate(split3(power), axis=1), ones, preferred_element_type=jnp.float32
                )
                scale = lax.rsqrt(total * (1.0 / BAND) + band_epsilon).reshape(parts, bands, LANES)
                for s in range(parts):
                    for imag in range(2):
                        even = part[s, 2 * imag] * scale[s]
                        odd = part[s, 2 * imag + 1] * scale[s]
                        one = jnp.where(left, even, pltpu.roll(odd, first, 1))
                        two = jnp.where(left, pltpu.roll(even, first, 1), odd)
                        win = start + 2 * pair
                        at = pl.ds(imag * bands, bands)
                        out_refs[s][chan, win, at, :] = one.astype(jnp.bfloat16)
                        out_refs[s][chan, win + 1, at, :] = two.astype(jnp.bfloat16)


def whitened_spectra(records, parts):
    chans, wins, samples = records.shape
    first = samples // LANES
    bands = BINS // BAND // parts
    tables = dft_tables(samples, parts)
    x = records.reshape(chans, wins, first, LANES).transpose(0, 2, 1, 3)
    out = jax.ShapeDtypeStruct((chans, wins, 2 * bands, LANES), jnp.bfloat16)
    return pl.pallas_call(
        functools.partial(spectra_kernel, parts),
        out_shape=[out] * parts,
        compiler_params=pltpu.CompilerParams(vmem_limit_bytes=48 * 1024 * 1024),
        cost_estimate=pl.CostEstimate(
            flops=6 * 4 * chans * wins * samples * LANES, bytes_accessed=3 * 2**20, transcendentals=0
        ),
        name="spectra",
    )(x, *tables)


def cross_kernel(pieces, inv_root, pos_ref, *refs):
    mine = refs[:pieces]
    theirs = [refs[pieces * (i + 1) : pieces * (i + 2)] for i in range(ROUNDS)]
    out_ref = refs[-1]
    chans, wins, rows, _ = mine[0].shape
    bands = rows // 2
    me = lax.axis_index("chan")
    odd = lax.rem(me, 2)
    last = pos_ref.shape[0] - 1
    rounds = [2 * odd, 1, 2 - 2 * odd, 3]
    a_group = 2
    for source in (3, 1, 0, 2):
        rnd = rounds[source]
        for a_start in range(0, chans, a_group):

            def step(piece, win, acc):
                own = [
                    [
                        mine[piece][a_start + a, win, pl.ds(i * bands, bands), :].astype(jnp.float32)
                        for i in range(2)
                    ]
                    for a in range(a_group)
                ]
                acc = list(acc)
                for c in range(chans):
                    cr, ci = [
                        theirs[source][piece][c, win, pl.ds(i * bands, bands), :].astype(jnp.float32)
                        for i in range(2)
                    ]
                    for a in range(a_group):
                        ar, ai = own[a]
                        at = 2 * (a * chans + c)
                        acc[at] = acc[at] + ar * cr + ai * ci
                        acc[at + 1] = acc[at + 1] + ai * cr - ar * ci
                return tuple(acc)

            acc = tuple(jnp.zeros((bands, LANES), jnp.float32) for _ in range(2 * a_group * chans))
            for piece in range(pieces):
                acc = lax.fori_loop(0, wins, functools.partial(step, piece), acc)
            for a in range(a_group):
                pos_a = pos_ref[me * chans + a_start + a]
                for c in range(chans):
                    pos_c = pos_ref[lax.min((me + rnd + 1) * chans + c, last)]
                    gain = jnp.where(pos_c - pos_a <= REACH, inv_root, 0.0).astype(jnp.float32)
                    at = 2 * (a * chans + c)
                    for i in range(2):
                        out_ref[rnd, a_start + a, c, pl.ds(i, bands, stride=2), :] = acc[at + i] * gain


def cross_spectra(mine, theirs, positions):
    pieces = len(mine)
    chans, wins, rows, _ = mine[0].shape
    vmem = pl.BlockSpec(memory_space=pltpu.VMEM)
    inv_root = 1.0 / math.sqrt(pieces * wins)
    operands = list(mine) + [piece for source in theirs for piece in source]
    out = pl.pallas_call(
        functools.partial(cross_kernel, pieces, inv_root),
        in_specs=[pl.BlockSpec(memory_space=pltpu.SMEM)] + [vmem] * len(operands),
        out_specs=vmem,
        out_shape=jax.ShapeDtypeStruct((ROUNDS, chans, chans, rows, LANES), jnp.float32),
        compiler_params=pltpu.CompilerParams(vmem_limit_bytes=48 * 1024 * 1024),
        name="cross",
    )(positions, *operands)
    bands = rows // 2
    out = out.reshape(ROUNDS, chans, chans, bands, 2, LANES).transpose(0, 1, 2, 4, 3, 5)
    return out.reshape(ROUNDS, chans, chans, 2, bands * LANES)


def shards(records, positions):
    parts = lax.axis_size("win")
    blocks = lax.axis_size("chan")
    me = lax.axis_index("chan")
    spectra = whitened_spectra(records, parts)
    mine = [spectra[0]]
    for s in range(1, parts):
        mine.append(lax.ppermute(spectra[s], "win", [(i, (i + s) % parts) for i in range(parts)]))
    up = [(i, i - 4) for i in range(4, blocks)]
    swap2 = [(i, i ^ 2) for i in range(blocks)]
    swap1 = [(i, i ^ 1) for i in range(blocks)]
    far, mid, one, two = [], [], [], []
    upper = lax.rem(me, 4) >= 2
    odd = lax.rem(me, 2) == 1
    for own in mine:
        by4 = lax.ppermute(own, "chan", up)
        by2 = lax.ppermute(jnp.where(upper, own, by4), "chan", swap2)
        far.append(by4)
        mid.append(by2)
        one.append(lax.ppermute(jnp.where(odd, own, by4), "chan", swap1))
        two.append(lax.ppermute(by2, "chan", swap1))
    return cross_spectra(mine, (one, mid, two, far), positions)


def solution(mesh):
    return jax.shard_map(
        shards,
        mesh=mesh,
        in_specs=(P("chan", "win", None), P()),
        out_specs=P(None, "chan", None, None, "win"),
        check_vma=False,
    )
```

```python
import functools
import math

import jax
import jax.numpy as jnp
from jax import lax
from jax.experimental import pallas as pl
from jax.experimental.pallas import tpu as pltpu
from jax.sharding import PartitionSpec as P

BINS = 4096
BAND = 128
ROUNDS = 4
REACH = 2000
LANES = 128
band_epsilon = 1e-06
VMEM = pl.BlockSpec(memory_space=pltpu.VMEM)
SMEM = pl.BlockSpec(memory_space=pltpu.SMEM)
HBM = pl.BlockSpec(memory_space=pltpu.HBM)
PARAMS = pltpu.CompilerParams(vmem_limit_bytes=40 * 1024 * 1024)


def cost(microseconds):
    return pl.CostEstimate(flops=int(microseconds * 1.1e9), bytes_accessed=0, transcendentals=0)


def split3(value):
    hi = value.astype(jnp.bfloat16)
    rest = value - hi.astype(jnp.float32)
    mid = rest.astype(jnp.bfloat16)
    lo = (rest - mid.astype(jnp.float32)).astype(jnp.bfloat16)
    return hi, mid, lo


def real_dft(values):
    n = len(values)
    if n == 2:
        return [(values[0] + values[1], None), (values[0] - values[1], None)]
    even, odd = real_dft(values[0::2]), real_dft(values[1::2])
    out = [None] * (n // 2 + 1)
    for k in range(n // 4 + 1):
        (er, ei), (dr, di) = even[k], odd[k]
        if k == 0:
            out[0] = (er + dr, None)
            out[n // 2] = (er - dr, None)
        elif 4 * k == n:
            out[k] = (er, -dr)
        else:
            c, s = math.cos(2.0 * math.pi * k / n), math.sin(2.0 * math.pi * k / n)
            tr = dr * c + di * s
            ti = di * c - dr * s
            out[k] = (er + tr, ei + ti)
            out[n // 2 - k] = (er - tr, ti - ei)
    return out


def spectra_channel(parts, chan, x, tw_ref, l2_ref, t_ref, outs):
    first = len(x)
    wins = x[0].shape[0]
    bands = BINS // BAND // parts
    terms = real_dft(x)
    for k in range(first):
        re, im = terms[min(k, first - k)]
        rows = pl.ds(k * wins, wins)
        cos, sin = tw_ref[0, pl.ds(k, 1), :], tw_ref[1, pl.ds(k, 1), :]
        if im is None:
            t_ref[chan, 0, rows, :] = re * cos
            t_ref[chan, 1, rows, :] = -(re * sin)
        elif 2 * k <= first:
            t_ref[chan, 0, rows, :] = re * cos + im * sin
            t_ref[chan, 1, rows, :] = im * cos - re * sin
        else:
            t_ref[chan, 0, rows, :] = re * cos - im * sin
            t_ref[chan, 1, rows, :] = -(im * cos + re * sin)
    rhs = []
    for win in range(wins):
        at = pl.ds(win, first, stride=wins)
        row = jnp.concatenate([t_ref[chan, 0, at, :], t_ref[chan, 1, at, :]], axis=1)
        hi, mid, lo = split3(row)
        rhs.append(jnp.concatenate([hi, mid, lo, hi, mid, hi], axis=1))
    spec = lax.dot_general(
        l2_ref[...],
        jnp.concatenate(rhs, axis=0),
        (((1,), (1,)), ((), ())),
        preferred_element_type=jnp.float32,
    )
    left = lax.broadcasted_iota(jnp.int32, (bands, LANES), 1) < first
    pairs = wins // 2
    tiles = [
        spec[:, i * LANES : (i + 1) * LANES].reshape(parts, 4, bands, LANES) for i in range(pairs)
    ]
    powers = []
    for tile in tiles:
        square = tile * tile
        power = square[:, 0] + square[:, 1] + square[:, 2] + square[:, 3]
        powers.append(power.reshape(parts * bands, LANES))
    row = lax.rem(lax.broadcasted_iota(jnp.int32, (3 * LANES, LANES), 0), LANES)
    lane = lax.broadcasted_iota(jnp.int32, (3 * LANES, LANES), 1)
    ones = ((row < first) == (lane < first)).astype(jnp.bfloat16)
    total = jnp.dot(
        jnp.concatenate(split3(jnp.concatenate(powers, axis=0)), axis=1),
        ones,
        preferred_element_type=jnp.float32,
    )
    scales = lax.rsqrt(total * (1.0 / BAND) + band_epsilon).reshape(pairs, parts, bands, LANES)
    for pair in range(pairs):
        for s in range(parts):
            scale = scales[pair, s]
            for imag in range(2):
                even = tiles[pair][s, 2 * imag] * scale
                odd = tiles[pair][s, 2 * imag + 1] * scale
                one = jnp.where(left, even, pltpu.roll(odd, first, 1)).astype(jnp.bfloat16)
                two = jnp.where(left, pltpu.roll(even, first, 1), odd).astype(jnp.bfloat16)
                at = pl.ds(imag * bands, bands)
                for out_ref, row in outs[s]:
                    out_ref[row, 2 * pair, at, :] = one
                    out_ref[row, 2 * pair + 1, at, :] = two


def turn_table(index, period):
    index = lax.rem(index, period)
    quarter = period // 4
    turn = lax.div(index + quarter // 2, quarter)
    angle = (index - turn * quarter).astype(jnp.float32) * (2.0 * math.pi / period)
    square = angle * angle

    def series(first):
        value = jnp.full_like(angle, 0.0)
        for power in range(10 + first, first - 1, -2):
            value = value * square + (-1) ** (power // 2) / math.factorial(power)
        return value

    cos, sin = series(0), series(1) * angle
    swap = lax.rem(turn, 2) == 1
    minus_cos = (turn == 1) | (turn == 2)
    minus_sin = (turn == 2) | (turn == 3)
    cos, sin = jnp.where(swap, sin, cos), jnp.where(swap, cos, sin)
    return jnp.where(minus_cos, -cos, cos), jnp.where(minus_sin, -sin, sin)


def tables_kernel(parts, samples, tw_ref, l2_ref):
    first = samples // LANES
    bands = BINS // BAND // parts
    me = lax.axis_index("win")
    k1 = lax.broadcasted_iota(jnp.int32, (first, LANES), 0)
    q = lax.broadcasted_iota(jnp.int32, (first, LANES), 1)
    tw_ref[0], tw_ref[1] = turn_table(k1 * q, samples)
    band = lax.broadcasted_iota(jnp.int32, (bands, LANES), 0)
    q = lax.broadcasted_iota(jnp.int32, (bands, LANES), 1)
    for s in range(parts):
        part = lax.rem(me + s, parts)
        tables = [turn_table((2 * (part * bands + band) + odd) * q, LANES) for odd in range(2)]
        rows = [jnp.concatenate([cos, sin], axis=1) for cos, sin in tables]
        rows += [jnp.concatenate([-sin, cos], axis=1) for cos, sin in tables]
        hi, mid, lo = split3(jnp.concatenate(rows, axis=0))
        table = jnp.concatenate([hi, hi, hi, mid, mid, lo], axis=1)
        l2_ref[pl.ds(s * 4 * bands, 4 * bands), :] = table


def spectra_kernel(parts, x_ref, tw_ref, l2_ref, *refs):
    low, high, whole, t_ref = (
        refs[:parts], refs[parts : 2 * parts], refs[2 * parts : 3 * parts - 1], refs[-1]
    )
    chans, first = x_ref.shape[:2]
    half = low[0].shape[0]
    for chan in range(chans):
        x = [x_ref[chan, p] for p in range(first)]
        chunk, row = (low, chan) if chan < half else (high, chan - half)
        targets = [[(out, row)] for out in chunk]
        for s in range(1, parts):
            targets[s].append((whole[s - 1], chan))
        spectra_channel(parts, chan, x, tw_ref, l2_ref, t_ref, targets)


def whitened_spectra(records, parts):
    chans, wins, samples = records.shape
    first = samples // LANES
    rows = 2 * (BINS // BAND // parts)
    x = records.reshape(chans, wins, first, LANES).transpose(0, 2, 1, 3)
    half = chans // 2

    def chunk(count):
        return jax.ShapeDtypeStruct((count, wins, rows, LANES), jnp.bfloat16)

    tables = pl.pallas_call(
        functools.partial(tables_kernel, parts, samples),
        out_specs=[VMEM] * 2,
        out_shape=[
            jax.ShapeDtypeStruct((2, first, LANES), jnp.float32),
            jax.ShapeDtypeStruct((2 * rows * parts, 12 * LANES), jnp.bfloat16),
        ],
        compiler_params=PARAMS,
        cost_estimate=cost(1),
        name="tables",
    )()
    out = pl.pallas_call(
        functools.partial(spectra_kernel, parts),
        in_specs=[VMEM] * 3,
        out_specs=[VMEM] * (3 * parts - 1),
        out_shape=[chunk(half)] * parts + [chunk(chans - half)] * parts + [chunk(chans)] * (parts - 1),
        scratch_shapes=[pltpu.VMEM((chans, 2, first * wins, LANES), jnp.float32)],
        compiler_params=PARAMS,
        cost_estimate=cost(4),
        name="spectra",
    )(x, *tables)
    return out[:parts], out[parts : 2 * parts], out[2 * parts :]


def cross_unit(mine, theirs, acc):
    rows = mine[0][0].shape[1]
    bands = rows // 2
    wins = mine[0][0].shape[0]
    per_step = 4 if wins % 4 == 0 else 1

    def planes(ref, win):
        return [ref[win, pl.ds(i * bands, bands), :].astype(jnp.float32) for i in range(2)]

    for own, their in zip(mine, theirs):

        def step(index, acc, own=own, their=their):
            acc = list(acc)
            for i in range(per_step):
                win = index * per_step + i
                ours = [planes(ref, win) for ref in own]
                for c, ref in enumerate(their):
                    cr, ci = planes(ref, win)
                    for a, (ar, ai) in enumerate(ours):
                        at = 2 * (a * len(their) + c)
                        acc[at] = acc[at] + ar * cr + ai * ci
                        acc[at + 1] = acc[at + 1] + ai * cr - ar * ci
            return tuple(acc)

        acc = lax.fori_loop(0, wins // per_step, step, acc)
    return acc


def cross_kernel(layout, jobs, inv_root, *refs):
    groups, at = {}, 0
    for name, count in layout:
        groups[name] = refs[at : at + count]
        at += count
    pos_ref, out_ref, buffer, sems = groups["pos"][0], groups["out"][0], groups["buffer"][0], groups["sems"][0]
    chans = out_ref.shape[1]
    me = lax.axis_index("chan")
    odd = lax.rem(me, 2)
    rounds = {"one": 2 * odd, "mid": 1, "two": 2 - 2 * odd, "far": 3}
    last = pos_ref.shape[0] - 1
    bands = buffer.shape[-2] // 2
    half = chans // 2
    own_refs = groups["mine"]

    def own_view(piece, a):
        if piece == 0:
            return own_refs[a // half].at[a % half]
        return own_refs[piece + 1].at[a]

    copies = []
    for index, (source, side, pieces, acc_in, acc_out) in enumerate(jobs):
        rnd = rounds[source]
        for a_start in range(0, chans, 2):
            a_list = list(range(a_start, min(a_start + 2, chans)))
            mine = [[own_view(piece, a) for a in a_list] for piece, _ in pieces]
            theirs = [
                [groups[name][ref_index].at[row + c] for c in range(half)]
                for _, (name, ref_index, row) in pieces
            ]
            count = 2 * len(a_list) * half
            if acc_in is None:
                acc = tuple(jnp.zeros((bands, LANES), jnp.float32) for _ in range(count))
            else:
                ref = groups["acc_in"][acc_in]
                acc = tuple(
                    ref[a, c, pl.ds(i * bands, bands), :]
                    for a in a_list for c in range(half) for i in range(2)
                )
            acc = cross_unit(mine, theirs, acc)
            for ai, a in enumerate(a_list):
                pos_a = pos_ref[me * chans + a]
                for c in range(half):
                    at = 2 * (ai * half + c)
                    if acc_out is not None:
                        for i in range(2):
                            groups["acc_out"][acc_out][a, c, pl.ds(i * bands, bands), :] = acc[at + i]
                        continue
                    other = (me + rnd + 1) * chans + side * half + c
                    pos_c = pos_ref[lax.min(other, last)]
                    gain = jnp.where(pos_c - pos_a <= REACH, inv_root, 0.0).astype(jnp.float32)
                    for i in range(2):
                        buffer[index, a, c, pl.ds(i, bands, stride=2), :] = acc[at + i] * gain
        if acc_out is None:
            copy = pltpu.make_async_copy(
                buffer.at[index], out_ref.at[rnd, :, pl.ds(side * half, half)], sems.at[index]
            )
            copy.start()
            copies.append(copy)
    for copy in copies:
        copy.wait()


def cross_call(name, jobs, inv_root, positions, mine, sources, acc_in, acc_count, out_before):
    chans = mine[0].shape[0] + mine[1].shape[0]
    rows = mine[0].shape[2]
    half = chans // 2
    layout = [("pos", 1), ("mine", len(mine))]
    operands = [positions, *mine]
    for key, arrays in sources.items():
        layout.append((key, len(arrays)))
        operands += arrays
    layout.append(("acc_in", len(acc_in)))
    operands += acc_in
    specs = [SMEM] + [VMEM] * (len(operands) - 1)
    aliases = {}
    if out_before is not None:
        layout.append(("before", 1))
        aliases = {len(operands): 0}
        operands.append(out_before)
        specs.append(HBM)
    layout += [("out", 1), ("acc_out", acc_count), ("buffer", 1), ("sems", 1)]
    acc = jax.ShapeDtypeStruct((chans, half, rows, LANES), jnp.float32)
    return pl.pallas_call(
        functools.partial(cross_kernel, layout, jobs, inv_root),
        in_specs=specs,
        out_specs=[HBM] + [VMEM] * acc_count,
        out_shape=[jax.ShapeDtypeStruct((ROUNDS, chans, chans, rows, LANES), jnp.float32)]
        + [acc] * acc_count,
        scratch_shapes=[
            pltpu.VMEM((len(jobs), chans, half, rows, LANES), jnp.float32),
            pltpu.SemaphoreType.DMA((len(jobs),)),
        ],
        input_output_aliases=aliases,
        compiler_params=PARAMS,
        cost_estimate=cost(0.3 * sum(len(job[2]) for job in jobs)),
        name=name,
    )(*operands)


def choose_body(bit, triples, out_ref):
    yes = lax.rem(lax.div(lax.axis_index("chan"), bit), 2) == 1
    start = 0
    for own_ref, row, far_ref in triples:
        rows = far_ref.shape[0]

        @pl.when(yes)
        def _(own_ref=own_ref, row=row, rows=rows, start=start):
            out_ref[pl.ds(start, rows)] = own_ref[pl.ds(row, rows)]

        @pl.when(jnp.logical_not(yes))
        def _(far_ref=far_ref, rows=rows, start=start):
            out_ref[pl.ds(start, rows)] = far_ref[...]

        start += rows


def choose(bit, pairs):
    rows = [row for _, row, _ in pairs]

    def kernel(*refs):
        triples = [(refs[2 * i], row, refs[2 * i + 1]) for i, row in enumerate(rows)]
        choose_body(bit, triples, refs[-1])

    operands = [array for own, _, far in pairs for array in (own, far)]
    shape = (sum(far.shape[0] for _, _, far in pairs),) + pairs[0][2].shape[1:]
    return pl.pallas_call(
        kernel,
        in_specs=[VMEM] * len(operands),
        out_specs=VMEM,
        out_shape=jax.ShapeDtypeStruct(shape, jnp.bfloat16),
        compiler_params=PARAMS,
        cost_estimate=cost(0.1),
        name="choose",
    )(*operands)


def shards(records, positions):
    parts = lax.axis_size("win")
    blocks = lax.axis_size("chan")
    chans, wins, _ = records.shape
    half = chans // 2
    low, high, whole = whitened_spectra(records, parts)
    turn = [[(i, (i + s) % parts) for i in range(parts)] for s in range(parts)]
    up = [
        [
            (b * parts + i, (b - 4) * parts + j)
            for b in range(4, blocks)
            for i, j in turn[s]
        ]
        for s in range(parts)
    ]
    swap2 = [(i, i ^ 2) for i in range(blocks)]
    swap1 = [(i, i ^ 1) for i in range(blocks)]
    keys = [(s, h) for s in range(parts) for h in range(2)]
    far = {}
    for at, (s, h) in enumerate(keys):
        payload = (low, high)[h][s]
        if at >= 2:
            far[keys[at - 2]], payload = lax.optimization_barrier((far[keys[at - 2]], payload))
        far[s, h] = lax.ppermute(payload, ("chan", "win"), up[s])
    others = [lax.ppermute(whole[s - 1], "win", turn[s]) for s in range(1, parts)]

    def own(s, h):
        return ((low, high)[h][0], 0) if s == 0 else (others[s - 1], h * half)

    mid, one, two = {}, [], {}
    for s in range(parts):
        for h in range(2):
            mid[s, h] = lax.ppermute(choose(2, [(*own(s, h), far[s, h])]), "chan", swap2)
            if (s, h) != keys[-1]:
                two[s, h] = lax.ppermute(mid[s, h], "chan", swap1)
        pairs = [(*own(s, h), far[s, h]) for h in range(2)]
        one.append(lax.ppermute(choose(1, pairs), "chan", swap1))

    mine = [low[0], high[0], *others]
    inv_root = 1.0 / math.sqrt(parts * wins)
    last = parts - 1
    names = {"far": far, "mid": mid, "two": two}
    jobs = []
    for name in ("far", "mid", "two"):
        for h in range(2):
            open_job = h == 1 and name != "far"
            pieces = [
                (s, (name, keys.index((s, h)), 0)) for s in range(parts) if not (open_job and s == last)
            ]
            jobs.append((name, h, pieces, None, {"mid": 0, "two": 1}[name] if open_job else None))
    for h in range(2):
        jobs.append(("one", h, [(s, ("one", s, h * half)) for s in range(parts)], None, None))
    sources = {"far": [far[k] for k in keys], "one": one}
    sources |= {name: [names[name][k] for k in keys[:-1]] for name in ("mid", "two")}
    out, acc_mid, acc_two = cross_call(
        "cross_most", jobs, inv_root, positions, mine, sources, [], 2, None
    )
    mid[keys[-1]], acc_mid = lax.optimization_barrier((mid[keys[-1]], acc_mid))
    two[keys[-1]] = lax.ppermute(mid[keys[-1]], "chan", swap1)
    for name, acc in (("mid", acc_mid), ("two", acc_two)):
        job = (name, 1, [(last, (name, 0, 0))], 0, None)
        (out,) = cross_call(
            "cross_" + name, [job], inv_root, positions, mine,
            {name: [names[name][last, 1]]}, [acc], 0, out,
        )
    bands = out.shape[3] // 2
    out = out.reshape(ROUNDS, chans, chans, bands, 2, LANES).transpose(0, 1, 2, 4, 3, 5)
    return out.reshape(ROUNDS, chans, chans, 2, bands * LANES)


def solution(mesh):
    return jax.shard_map(
        shards,
        mesh=mesh,
        in_specs=(P("chan", "win", None), P()),
        out_specs=P(None, "chan", None, None, "win"),
        check_vma=False,
    )
```

```python
import functools
import math

import jax
import jax.numpy as jnp
from jax import lax
from jax.experimental import pallas as pl
from jax.experimental.pallas import tpu as pltpu
from jax.sharding import PartitionSpec as P

BINS = 4096
BAND = 128
ROUNDS = 4
REACH = 2000
LANES = 128
band_epsilon = 1e-06
VMEM = pl.BlockSpec(memory_space=pltpu.VMEM)
SMEM = pl.BlockSpec(memory_space=pltpu.SMEM)
HBM = pl.BlockSpec(memory_space=pltpu.HBM)
PARAMS = pltpu.CompilerParams(vmem_limit_bytes=40 * 1024 * 1024)


def cost(microseconds):
    return pl.CostEstimate(flops=int(microseconds * 1.1e9), bytes_accessed=0, transcendentals=0)


def split3(value):
    hi = value.astype(jnp.bfloat16)
    rest = value - hi.astype(jnp.float32)
    mid = rest.astype(jnp.bfloat16)
    lo = (rest - mid.astype(jnp.float32)).astype(jnp.bfloat16)
    return hi, mid, lo


def real_dft(values):
    n = len(values)
    if n == 2:
        return [(values[0] + values[1], None), (values[0] - values[1], None)]
    even, odd = real_dft(values[0::2]), real_dft(values[1::2])
    out = [None] * (n // 2 + 1)
    for k in range(n // 4 + 1):
        (er, ei), (dr, di) = even[k], odd[k]
        if k == 0:
            out[0] = (er + dr, None)
            out[n // 2] = (er - dr, None)
        elif 4 * k == n:
            out[k] = (er, -dr)
        else:
            c, s = math.cos(2.0 * math.pi * k / n), math.sin(2.0 * math.pi * k / n)
            tr = dr * c + di * s
            ti = di * c - dr * s
            out[k] = (er + tr, ei + ti)
            out[n // 2 - k] = (er - tr, ti - ei)
    return out


def spectra_channel(parts, chan, x, tw_ref, l2_ref, t_ref, outs):
    first = len(x)
    wins = x[0].shape[0]
    bands = BINS // BAND // parts
    terms = real_dft(x)
    for k in range(first):
        re, im = terms[min(k, first - k)]
        rows = pl.ds(k * wins, wins)
        cos, sin = tw_ref[0, pl.ds(k, 1), :], tw_ref[1, pl.ds(k, 1), :]
        if im is None:
            t_ref[chan, 0, rows, :] = re * cos
            t_ref[chan, 1, rows, :] = -(re * sin)
        elif 2 * k <= first:
            t_ref[chan, 0, rows, :] = re * cos + im * sin
            t_ref[chan, 1, rows, :] = im * cos - re * sin
        else:
            t_ref[chan, 0, rows, :] = re * cos - im * sin
            t_ref[chan, 1, rows, :] = -(im * cos + re * sin)
    rhs = []
    for win in range(wins):
        at = pl.ds(win, first, stride=wins)
        row = jnp.concatenate([t_ref[chan, 0, at, :], t_ref[chan, 1, at, :]], axis=1)
        hi, mid, lo = split3(row)
        rhs.append(jnp.concatenate([hi, mid, lo, hi, mid, hi], axis=1))
    spec = lax.dot_general(
        l2_ref[...],
        jnp.concatenate(rhs, axis=0),
        (((1,), (1,)), ((), ())),
        preferred_element_type=jnp.float32,
    )
    left = lax.broadcasted_iota(jnp.int32, (bands, LANES), 1) < first
    pairs = wins // 2
    tiles = [
        spec[:, i * LANES : (i + 1) * LANES].reshape(parts, 4, bands, LANES) for i in range(pairs)
    ]
    powers = []
    for tile in tiles:
        square = tile * tile
        power = square[:, 0] + square[:, 1] + square[:, 2] + square[:, 3]
        powers.append(power.reshape(parts * bands, LANES))
    row = lax.rem(lax.broadcasted_iota(jnp.int32, (3 * LANES, LANES), 0), LANES)
    lane = lax.broadcasted_iota(jnp.int32, (3 * LANES, LANES), 1)
    ones = ((row < first) == (lane < first)).astype(jnp.bfloat16)
    total = jnp.dot(
        jnp.concatenate(split3(jnp.concatenate(powers, axis=0)), axis=1),
        ones,
        preferred_element_type=jnp.float32,
    )
    scales = lax.rsqrt(total * (1.0 / BAND) + band_epsilon).reshape(pairs, parts, bands, LANES)
    for pair in range(pairs):
        for s in range(parts):
            scale = scales[pair, s]
            for imag in range(2):
                even = tiles[pair][s, 2 * imag] * scale
                odd = tiles[pair][s, 2 * imag + 1] * scale
                one = jnp.where(left, even, pltpu.roll(odd, first, 1)).astype(jnp.bfloat16)
                two = jnp.where(left, pltpu.roll(even, first, 1), odd).astype(jnp.bfloat16)
                at = pl.ds(imag * bands, bands)
                outs[s][chan, 2 * pair, at, :] = one
                outs[s][chan, 2 * pair + 1, at, :] = two


def turn_table(index, period):
    index = lax.rem(index, period)
    quarter = period // 4
    turn = lax.div(index + quarter // 2, quarter)
    angle = (index - turn * quarter).astype(jnp.float32) * (2.0 * math.pi / period)
    square = angle * angle

    def series(first):
        value = jnp.full_like(angle, 0.0)
        for power in range(10 + first, first - 1, -2):
            value = value * square + (-1) ** (power // 2) / math.factorial(power)
        return value

    cos, sin = series(0), series(1) * angle
    swap = lax.rem(turn, 2) == 1
    minus_cos = (turn == 1) | (turn == 2)
    minus_sin = (turn == 2) | (turn == 3)
    cos, sin = jnp.where(swap, sin, cos), jnp.where(swap, cos, sin)
    return jnp.where(minus_cos, -cos, cos), jnp.where(minus_sin, -sin, sin)


def tables_kernel(parts, samples, tw_ref, l2_ref):
    first = samples // LANES
    bands = BINS // BAND // parts
    me = lax.axis_index("win")
    k1 = lax.broadcasted_iota(jnp.int32, (first, LANES), 0)
    q = lax.broadcasted_iota(jnp.int32, (first, LANES), 1)
    tw_ref[0], tw_ref[1] = turn_table(k1 * q, samples)
    band = lax.broadcasted_iota(jnp.int32, (bands, LANES), 0)
    q = lax.broadcasted_iota(jnp.int32, (bands, LANES), 1)
    for s in range(parts):
        part = lax.rem(me + s, parts)
        tables = [turn_table((2 * (part * bands + band) + odd) * q, LANES) for odd in range(2)]
        rows = [jnp.concatenate([cos, sin], axis=1) for cos, sin in tables]
        rows += [jnp.concatenate([-sin, cos], axis=1) for cos, sin in tables]
        hi, mid, lo = split3(jnp.concatenate(rows, axis=0))
        table = jnp.concatenate([hi, hi, hi, mid, mid, lo], axis=1)
        l2_ref[pl.ds(s * 4 * bands, 4 * bands), :] = table


def spectra_kernel(parts, x_ref, tw_ref, l2_ref, *refs):
    outs, t_ref = refs[:-1], refs[-1]
    chans, first = x_ref.shape[:2]
    for chan in range(chans):
        x = [x_ref[chan, p] for p in range(first)]
        spectra_channel(parts, chan, x, tw_ref, l2_ref, t_ref, outs)


def whitened_spectra(records, parts):
    chans, wins, samples = records.shape
    first = samples // LANES
    rows = 2 * (BINS // BAND // parts)
    x = records.reshape(chans, wins, first, LANES).transpose(0, 2, 1, 3)
    tables = pl.pallas_call(
        functools.partial(tables_kernel, parts, samples),
        out_specs=[VMEM] * 2,
        out_shape=[
            jax.ShapeDtypeStruct((2, first, LANES), jnp.float32),
            jax.ShapeDtypeStruct((2 * rows * parts, 12 * LANES), jnp.bfloat16),
        ],
        compiler_params=PARAMS,
        cost_estimate=cost(1),
        name="tables",
    )()
    return pl.pallas_call(
        functools.partial(spectra_kernel, parts),
        in_specs=[VMEM] * 3,
        out_specs=[VMEM] * parts,
        out_shape=[jax.ShapeDtypeStruct((chans, wins, rows, LANES), jnp.bfloat16)] * parts,
        scratch_shapes=[pltpu.VMEM((chans, 2, first * wins, LANES), jnp.float32)],
        compiler_params=PARAMS,
        cost_estimate=cost(4),
        name="spectra",
    )(x, *tables)


def cross_unit(mine, theirs, acc):
    rows = mine[0][0].shape[1]
    bands = rows // 2
    wins = mine[0][0].shape[0]
    per_step = 4 if wins % 4 == 0 else 1

    def planes(ref, win):
        return [ref[win, pl.ds(i * bands, bands), :].astype(jnp.float32) for i in range(2)]

    for own, their in zip(mine, theirs):

        def step(index, acc, own=own, their=their):
            acc = list(acc)
            for i in range(per_step):
                win = index * per_step + i
                ours = [planes(ref, win) for ref in own]
                for c, ref in enumerate(their):
                    cr, ci = planes(ref, win)
                    for a, (ar, ai) in enumerate(ours):
                        at = 2 * (a * len(their) + c)
                        acc[at] = acc[at] + ar * cr + ai * ci
                        acc[at + 1] = acc[at + 1] + ai * cr - ar * ci
            return tuple(acc)

        acc = lax.fori_loop(0, wins // per_step, step, acc)
    return acc


def cross_kernel(layout, jobs, inv_root, *refs):
    groups, at = {}, 0
    for name, count in layout:
        groups[name] = refs[at : at + count]
        at += count
    (pos_ref,) = groups["pos"]
    mine = groups["mine"]
    chans, _, rows, _ = mine[0].shape
    bands = rows // 2
    me = lax.axis_index("chan")
    odd = lax.rem(me, 2)
    rounds = {"one": 2 * odd, "mid": 1, "two": 2 - 2 * odd, "far": 3}
    last = pos_ref.shape[0] - 1
    step = 2
    copies = []

    def send(source, ref, a_start, count):
        (out_ref,), (sems,) = groups["out"], groups["sems"]
        part = pl.ds(a_start, count)
        copy = pltpu.make_async_copy(
            ref.at[part], out_ref.at[rounds[source], part], sems.at[len(copies)]
        )
        copy.start()
        copies.append(copy)

    for source, ref in zip(("far", "mid", "one"), groups["done"]):
        send(source, ref, 0, chans)
    for source, pieces, acc_in, final, to in jobs:
        rnd = rounds[source]
        to_ref = groups["buffer"][0] if to is None else groups["acc_out"][to]
        for a_start in range(0, chans, step):
            a_list = range(a_start, min(a_start + step, chans))
            for c_start in range(0, chans, step):
                c_list = range(c_start, min(c_start + step, chans))
                ours = [[mine[piece].at[a] for a in a_list] for piece, _ in pieces]
                theirs = [[groups[source][ref].at[c] for c in c_list] for _, ref in pieces]
                order = [(a, c, i) for a in a_list for c in c_list for i in range(2)]
                if acc_in is None:
                    acc = tuple(jnp.zeros((bands, LANES), jnp.float32) for _ in order)
                else:
                    ref = groups["acc_in"][acc_in]
                    acc = tuple(ref[a, c, pl.ds(i * bands, bands), :] for a, c, i in order)
                acc = cross_unit(ours, theirs, acc)
                for (a, c, i), value in zip(order, acc):
                    if not final:
                        to_ref[a, c, pl.ds(i * bands, bands), :] = value
                        continue
                    pos_c = pos_ref[lax.min((me + rnd + 1) * chans + c, last)]
                    near = pos_c - pos_ref[me * chans + a] <= REACH
                    gain = jnp.where(near, inv_root, 0.0).astype(jnp.float32)
                    to_ref[a, c, pl.ds(i, bands, stride=2), :] = value * gain
            if to is None:
                send(source, to_ref, a_start, len(a_list))
    for copy in copies:
        copy.wait()


def cross_call(name, jobs, inv_root, positions, mine, sources, acc_in=(), done=()):
    chans, _, rows, _ = mine[0].shape
    groups = [("pos", [positions]), ("mine", mine), *sources.items()]
    groups += [("acc_in", acc_in), ("done", done)]
    operands = [array for _, arrays in groups for array in arrays]
    layout = [(key, len(arrays)) for key, arrays in groups]
    sums = jax.ShapeDtypeStruct((chans, chans, rows, LANES), jnp.float32)
    whole = jax.ShapeDtypeStruct((ROUNDS,) + sums.shape, jnp.float32)
    acc_count = sum(job[4] is not None for job in jobs)
    ends = 1 - acc_count // len(jobs)
    layout += [("out", ends), ("acc_out", acc_count), ("buffer", ends), ("sems", ends)]
    scratch = [pltpu.VMEM(sums.shape, jnp.float32), pltpu.SemaphoreType.DMA((chans + len(done),))]
    return pl.pallas_call(
        functools.partial(cross_kernel, layout, jobs, inv_root),
        in_specs=[SMEM] + [VMEM] * (len(operands) - 1),
        out_specs=[HBM] * ends + [VMEM] * acc_count,
        out_shape=[whole] * ends + [sums] * acc_count,
        scratch_shapes=scratch * ends,
        compiler_params=PARAMS,
        cost_estimate=cost(0.6 * sum(len(job[1]) for job in jobs)),
        name=name,
    )(*operands)


def choose(bit, own, far):
    def kernel(own_ref, far_ref, out_ref):
        yes = lax.rem(lax.div(lax.axis_index("chan"), bit), 2) == 1

        @pl.when(yes)
        def _():
            out_ref[...] = own_ref[...]

        @pl.when(jnp.logical_not(yes))
        def _():
            out_ref[...] = far_ref[...]

    return pl.pallas_call(
        kernel,
        in_specs=[VMEM] * 2,
        out_specs=VMEM,
        out_shape=jax.ShapeDtypeStruct(far.shape, far.dtype),
        compiler_params=PARAMS,
        cost_estimate=cost(0.1),
        name="choose",
    )(own, far)


def after(value, *others):
    return lax.optimization_barrier((value, *others))[0]


def shards(records, positions):
    parts = lax.axis_size("win")
    blocks = lax.axis_size("chan")
    wins = records.shape[1]
    spectra = whitened_spectra(records, parts)
    up = [(b, b - 4) for b in range(4, blocks)]
    swap2 = [(b, b ^ 2) for b in range(blocks)]
    swap1 = [(b, b ^ 1) for b in range(blocks)]
    mine = [spectra[0]]
    for s in range(1, parts):
        mine.append(lax.ppermute(spectra[s], "win", [(i, (i + s) % parts) for i in range(parts)]))
    far = [lax.ppermute(own, "chan", up) for own in mine]
    last = parts - 1
    early = range(last)
    inv_root = 1.0 / math.sqrt(parts * wins)
    call = functools.partial(cross_call, inv_root=inv_root, positions=positions, mine=mine)

    (acc_far,) = call(
        "cross_far", [("far", [(s, s) for s in early], None, False, 0)], sources={"far": far[:-1]}
    )
    far[last] = after(far[last], acc_far)
    mid, one, two = [], [], []
    for s in range(parts):
        mid.append(lax.ppermute(choose(2, mine[s], far[s]), "chan", swap2))
        one.append(lax.ppermute(choose(1, mine[s], far[s]), "chan", swap1))
        if s < last:
            two.append(lax.ppermute(mid[s], "chan", swap1))
    done_far, acc_mid, acc_one = call(
        "cross_most",
        [
            ("far", [(last, 0)], 0, True, 0),
            ("mid", [(s, s) for s in early], None, False, 1),
            ("one", [(s, s) for s in early], None, False, 2),
        ],
        sources={"far": far[last:], "mid": mid[:last], "one": one[:last]},
        acc_in=[acc_far],
    )
    mid[last] = after(mid[last], acc_mid)
    two.append(lax.ppermute(mid[last], "chan", swap1))
    done_mid, done_one, acc_two = call(
        "cross_next",
        [
            ("mid", [(last, 0)], 0, True, 0),
            ("one", [(last, 0)], 1, True, 1),
            ("two", [(s, s) for s in early], None, False, 2),
        ],
        sources={"mid": mid[last:], "one": one[last:], "two": two[:last]},
        acc_in=[acc_mid, acc_one],
    )
    two[last] = after(two[last], acc_two)
    (out,) = call(
        "cross_last", [("two", [(last, 0)], 0, True, None)], sources={"two": two[last:]},
        acc_in=[acc_two], done=[done_far, done_mid, done_one],
    )
    chans, bands = out.shape[1], out.shape[3] // 2
    out = out.reshape(ROUNDS, chans, chans, bands, 2, LANES).transpose(0, 1, 2, 4, 3, 5)
    return out.reshape(ROUNDS, chans, chans, 2, bands * LANES)


def solution(mesh):
    return jax.shard_map(
        shards,
        mesh=mesh,
        in_specs=(P("chan", "win", None), P()),
        out_specs=P(None, "chan", None, None, "win"),
        check_vma=False,
    )
```

```python
import functools
import math

import jax
import jax.numpy as jnp
from jax import lax
from jax.experimental import pallas as pl
from jax.experimental.pallas import tpu as pltpu
from jax.sharding import PartitionSpec as P

BINS = 4096
BAND = 128
ROUNDS = 4
REACH = 2000
LANES = 128
band_epsilon = 1e-06
VMEM = pl.BlockSpec(memory_space=pltpu.VMEM)
SMEM = pl.BlockSpec(memory_space=pltpu.SMEM)
HBM = pl.BlockSpec(memory_space=pltpu.HBM)
PARAMS = pltpu.CompilerParams(vmem_limit_bytes=40 * 1024 * 1024)


def cost(microseconds):
    return pl.CostEstimate(flops=int(microseconds * 1.1e9), bytes_accessed=0, transcendentals=0)


def split3(value):
    hi = value.astype(jnp.bfloat16)
    rest = value - hi.astype(jnp.float32)
    mid = rest.astype(jnp.bfloat16)
    lo = (rest - mid.astype(jnp.float32)).astype(jnp.bfloat16)
    return hi, mid, lo


def real_dft(values):
    n = len(values)
    if n == 2:
        return [(values[0] + values[1], None), (values[0] - values[1], None)]
    even, odd = real_dft(values[0::2]), real_dft(values[1::2])
    out = [None] * (n // 2 + 1)
    for k in range(n // 4 + 1):
        (er, ei), (dr, di) = even[k], odd[k]
        if k == 0:
            out[0] = (er + dr, None)
            out[n // 2] = (er - dr, None)
        elif 4 * k == n:
            out[k] = (er, -dr)
        else:
            c, s = math.cos(2.0 * math.pi * k / n), math.sin(2.0 * math.pi * k / n)
            tr = dr * c + di * s
            ti = di * c - dr * s
            out[k] = (er + tr, ei + ti)
            out[n // 2 - k] = (er - tr, ti - ei)
    return out


def spectra_channel(parts, chan, x, tw_ref, l2_ref, t_ref, outs):
    first = len(x)
    wins = x[0].shape[0]
    bands = BINS // BAND // parts
    terms = real_dft(x)
    for k in range(first):
        re, im = terms[min(k, first - k)]
        rows = pl.ds(k * wins, wins)
        cos, sin = tw_ref[0, pl.ds(k, 1), :], tw_ref[1, pl.ds(k, 1), :]
        if im is None:
            t_ref[chan, 0, rows, :] = re * cos
            t_ref[chan, 1, rows, :] = -(re * sin)
        elif 2 * k <= first:
            t_ref[chan, 0, rows, :] = re * cos + im * sin
            t_ref[chan, 1, rows, :] = im * cos - re * sin
        else:
            t_ref[chan, 0, rows, :] = re * cos - im * sin
            t_ref[chan, 1, rows, :] = -(im * cos + re * sin)
    rhs = []
    for win in range(wins):
        at = pl.ds(win, first, stride=wins)
        row = jnp.concatenate([t_ref[chan, 0, at, :], t_ref[chan, 1, at, :]], axis=1)
        hi, mid, lo = split3(row)
        rhs.append(jnp.concatenate([hi, mid, lo, hi, mid, hi], axis=1))
    spec = lax.dot_general(
        l2_ref[...],
        jnp.concatenate(rhs, axis=0),
        (((1,), (1,)), ((), ())),
        preferred_element_type=jnp.float32,
    )
    left = lax.broadcasted_iota(jnp.int32, (bands, LANES), 1) < first
    pairs = wins // 2
    tiles = [
        spec[:, i * LANES : (i + 1) * LANES].reshape(parts, 4, bands, LANES) for i in range(pairs)
    ]
    powers = []
    for tile in tiles:
        square = tile * tile
        power = square[:, 0] + square[:, 1] + square[:, 2] + square[:, 3]
        powers.append(power.reshape(parts * bands, LANES))
    row = lax.rem(lax.broadcasted_iota(jnp.int32, (3 * LANES, LANES), 0), LANES)
    lane = lax.broadcasted_iota(jnp.int32, (3 * LANES, LANES), 1)
    ones = ((row < first) == (lane < first)).astype(jnp.bfloat16)
    total = jnp.dot(
        jnp.concatenate(split3(jnp.concatenate(powers, axis=0)), axis=1),
        ones,
        preferred_element_type=jnp.float32,
    )
    scales = lax.rsqrt(total * (1.0 / BAND) + band_epsilon).reshape(pairs, parts, bands, LANES)
    for pair in range(pairs):
        for s in range(parts):
            scale = scales[pair, s]
            for imag in range(2):
                even = tiles[pair][s, 2 * imag] * scale
                odd = tiles[pair][s, 2 * imag + 1] * scale
                one = jnp.where(left, even, pltpu.roll(odd, first, 1)).astype(jnp.bfloat16)
                two = jnp.where(left, pltpu.roll(even, first, 1), odd).astype(jnp.bfloat16)
                at = pl.ds(imag * bands, bands)
                outs[s][chan, 2 * pair, at, :] = one
                outs[s][chan, 2 * pair + 1, at, :] = two


def turn_table(index, period):
    index = lax.rem(index, period)
    quarter = period // 4
    turn = lax.div(index + quarter // 2, quarter)
    angle = (index - turn * quarter).astype(jnp.float32) * (2.0 * math.pi / period)
    square = angle * angle

    def series(first):
        value = jnp.full_like(angle, 0.0)
        for power in range(10 + first, first - 1, -2):
            value = value * square + (-1) ** (power // 2) / math.factorial(power)
        return value

    cos, sin = series(0), series(1) * angle
    swap = lax.rem(turn, 2) == 1
    minus_cos = (turn == 1) | (turn == 2)
    minus_sin = (turn == 2) | (turn == 3)
    cos, sin = jnp.where(swap, sin, cos), jnp.where(swap, cos, sin)
    return jnp.where(minus_cos, -cos, cos), jnp.where(minus_sin, -sin, sin)


def gains_kernel(chans, inv_root, pos_ref, gain_ref):
    block = lax.axis_index("chan")
    last = pos_ref.shape[0] - 1
    for row in range(ROUNDS * chans * chans):
        rnd, a, c = row // (chans * chans), row // chans % chans, row % chans
        pos_c = pos_ref[lax.min((block + rnd + 1) * chans + c, last)]
        near = pos_c - pos_ref[block * chans + a] <= REACH
        gain = jnp.where(near, inv_root, 0.0).astype(jnp.float32)
        gain_ref[pl.ds(row, 1), :] = jnp.full((1, LANES), gain)


def stack_gains(positions, chans, windows):
    return pl.pallas_call(
        functools.partial(gains_kernel, chans, 1.0 / math.sqrt(windows)),
        in_specs=[SMEM],
        out_specs=VMEM,
        out_shape=jax.ShapeDtypeStruct((ROUNDS * chans * chans, LANES), jnp.float32),
        compiler_params=PARAMS,
        cost_estimate=cost(0.5),
        name="gains",
    )(positions)


def tables_kernel(parts, samples, tw_ref, l2_ref):
    first = samples // LANES
    bands = BINS // BAND // parts
    me = lax.axis_index("win")
    k1 = lax.broadcasted_iota(jnp.int32, (first, LANES), 0)
    q = lax.broadcasted_iota(jnp.int32, (first, LANES), 1)
    tw_ref[0], tw_ref[1] = turn_table(k1 * q, samples)
    band = lax.broadcasted_iota(jnp.int32, (bands, LANES), 0)
    q = lax.broadcasted_iota(jnp.int32, (bands, LANES), 1)
    for s in range(parts):
        part = lax.rem(me + s, parts)
        tables = [turn_table((2 * (part * bands + band) + odd) * q, LANES) for odd in range(2)]
        rows = [jnp.concatenate([cos, sin], axis=1) for cos, sin in tables]
        rows += [jnp.concatenate([-sin, cos], axis=1) for cos, sin in tables]
        hi, mid, lo = split3(jnp.concatenate(rows, axis=0))
        table = jnp.concatenate([hi, hi, hi, mid, mid, lo], axis=1)
        l2_ref[pl.ds(s * 4 * bands, 4 * bands), :] = table


def spectra_kernel(parts, x_ref, tw_ref, l2_ref, *refs):
    outs, t_ref = refs[:-1], refs[-1]
    chans, first = x_ref.shape[:2]
    for chan in range(chans):
        x = [x_ref[chan, p] for p in range(first)]
        spectra_channel(parts, chan, x, tw_ref, l2_ref, t_ref, outs)


def whitened_spectra(records, parts):
    chans, wins, samples = records.shape
    first = samples // LANES
    rows = 2 * (BINS // BAND // parts)
    x = records.reshape(chans, wins, first, LANES).transpose(0, 2, 1, 3)
    tables = pl.pallas_call(
        functools.partial(tables_kernel, parts, samples),
        out_specs=[VMEM] * 2,
        out_shape=[
            jax.ShapeDtypeStruct((2, first, LANES), jnp.float32),
            jax.ShapeDtypeStruct((2 * rows * parts, 12 * LANES), jnp.bfloat16),
        ],
        compiler_params=PARAMS,
        cost_estimate=cost(1),
        name="tables",
    )()
    return pl.pallas_call(
        functools.partial(spectra_kernel, parts),
        in_specs=[VMEM] * 3,
        out_specs=[VMEM] * parts,
        out_shape=[jax.ShapeDtypeStruct((chans, wins, rows, LANES), jnp.bfloat16)] * parts,
        scratch_shapes=[pltpu.VMEM((chans, 2, first * wins, LANES), jnp.float32)],
        compiler_params=PARAMS,
        cost_estimate=cost(4),
        name="spectra",
    )(x, *tables)


def cross_unit(mine, theirs, acc):
    rows = mine[0][0].shape[1]
    bands = rows // 2
    wins = mine[0][0].shape[0]
    per_step = wins if wins <= 8 else 1

    def planes(ref, win):
        return [ref[win, pl.ds(i * bands, bands), :].astype(jnp.float32) for i in range(2)]

    for own, their in zip(mine, theirs):

        def step(index, acc, own=own, their=their):
            acc = list(acc)
            for i in range(per_step):
                win = index * per_step + i
                ours = [planes(ref, win) for ref in own]
                for c, ref in enumerate(their):
                    cr, ci = planes(ref, win)
                    for a, (ar, ai) in enumerate(ours):
                        at = 2 * (a * len(their) + c)
                        acc[at] = acc[at] + ar * cr + ai * ci
                        acc[at + 1] = acc[at + 1] + ai * cr - ar * ci
            return tuple(acc)

        acc = lax.fori_loop(0, wins // per_step, step, acc)
    return acc


def cross_kernel(layout, jobs, *refs):
    groups, at = {}, 0
    for name, count in layout:
        groups[name] = refs[at : at + count]
        at += count
    (gain_ref,) = groups["gains"]
    mine = groups["mine"]
    chans, _, rows, _ = mine[0].shape
    bands = rows // 2
    odd = lax.rem(lax.axis_index("chan"), 2)
    rounds = {"one": 2 * odd, "mid": 1, "two": 2 - 2 * odd, "far": 3}
    step = 2
    copies = []

    def send(source, ref, a_start, count):
        (out_ref,), (sems,) = groups["out"], groups["sems"]
        part = pl.ds(a_start, count)
        copy = pltpu.make_async_copy(
            ref.at[part], out_ref.at[rounds[source], part], sems.at[len(copies)]
        )
        copy.start()
        copies.append(copy)

    for source, ref in zip(("far", "mid", "one"), groups["done"]):
        send(source, ref, 0, chans)
    for source, pieces, acc_in, final, to in jobs:
        rnd = rounds[source]
        to_ref = groups["buffer"][0] if to is None else groups["acc_out"][to]
        for a_start in range(0, chans, step):
            a_list = range(a_start, min(a_start + step, chans))
            for c_start in range(0, chans, step):
                c_list = range(c_start, min(c_start + step, chans))
                ours = [[mine[piece].at[a] for a in a_list] for piece, _ in pieces]
                theirs = [[groups[source][ref].at[c] for c in c_list] for _, ref in pieces]
                order = [(a, c, i) for a in a_list for c in c_list for i in range(2)]
                if acc_in is None:
                    acc = tuple(jnp.zeros((bands, LANES), jnp.float32) for _ in order)
                else:
                    ref = groups["acc_in"][acc_in]
                    acc = tuple(ref[a, c, pl.ds(i * bands, bands), :] for a, c, i in order)
                acc = cross_unit(ours, theirs, acc)
                for (a, c, i), value in zip(order, acc):
                    if not final:
                        to_ref[a, c, pl.ds(i * bands, bands), :] = value
                        continue
                    gain = gain_ref[pl.ds((rnd * chans + a) * chans + c, 1), :]
                    to_ref[a, c, pl.ds(i, bands, stride=2), :] = value * gain
            if to is None:
                send(source, to_ref, a_start, len(a_list))
    for copy in copies:
        copy.wait()


def cross_call(name, jobs, gains, mine, sources, acc_in=(), done=()):
    chans, _, rows, _ = mine[0].shape
    groups = [("gains", [gains]), ("mine", mine), *sources.items()]
    groups += [("acc_in", acc_in), ("done", done)]
    groups = [(key, list(arrays)) for key, arrays in groups]
    operands = [array for _, arrays in groups for array in arrays]
    layout = [(key, len(arrays)) for key, arrays in groups]
    sums = jax.ShapeDtypeStruct((chans, chans, rows, LANES), jnp.float32)
    whole = jax.ShapeDtypeStruct((ROUNDS,) + sums.shape, jnp.float32)
    acc_count = sum(job[4] is not None for job in jobs)
    ends = 1 - acc_count // len(jobs)
    layout += [("out", ends), ("acc_out", acc_count), ("buffer", ends), ("sems", ends)]
    scratch = [pltpu.VMEM(sums.shape, jnp.float32), pltpu.SemaphoreType.DMA((chans + len(done),))]
    return pl.pallas_call(
        functools.partial(cross_kernel, layout, jobs),
        in_specs=[VMEM] * len(operands),
        out_specs=[HBM] * ends + [VMEM] * acc_count,
        out_shape=[whole] * ends + [sums] * acc_count,
        scratch_shapes=scratch * ends,
        compiler_params=PARAMS,
        cost_estimate=cost(0.6 * sum(len(job[1]) for job in jobs)),
        name=name,
    )(*operands)


def choose(bit, own, far):
    def kernel(own_ref, far_ref, out_ref):
        yes = lax.rem(lax.div(lax.axis_index("chan"), bit), 2) == 1

        @pl.when(yes)
        def _():
            out_ref[...] = own_ref[...]

        @pl.when(jnp.logical_not(yes))
        def _():
            out_ref[...] = far_ref[...]

    return pl.pallas_call(
        kernel,
        in_specs=[VMEM] * 2,
        out_specs=VMEM,
        out_shape=jax.ShapeDtypeStruct(far.shape, far.dtype),
        compiler_params=PARAMS,
        cost_estimate=cost(0.1),
        name="choose",
    )(own, far)


def after(value, *others):
    return lax.optimization_barrier((value, *others))[0]


def shards(records, positions):
    parts = lax.axis_size("win")
    blocks = lax.axis_size("chan")
    chans, wins, _ = records.shape
    spectra = whitened_spectra(records, parts)
    up = [(b, b - 4) for b in range(4, blocks)]
    swap2 = [(b, b ^ 2) for b in range(blocks)]
    swap1 = [(b, b ^ 1) for b in range(blocks)]
    mine = [spectra[0]]
    for s in range(1, parts):
        mine.append(lax.ppermute(spectra[s], "win", [(i, (i + s) % parts) for i in range(parts)]))
    far = [lax.ppermute(own, "chan", up) for own in mine]
    last = parts - 1
    early = range(last)
    gains = stack_gains(after(positions, far[0]), chans, parts * wins)
    call = functools.partial(cross_call, gains=gains, mine=mine)

    (acc_far,) = call(
        "cross_far", [("far", [(s, s) for s in early], None, False, 0)], sources={"far": far[:-1]}
    )
    far[last] = after(far[last], acc_far)
    mid, one, two = [], [], []
    for s in range(parts):
        mid.append(lax.ppermute(choose(2, mine[s], far[s]), "chan", swap2))
        one.append(lax.ppermute(choose(1, mine[s], far[s]), "chan", swap1))
        if s < last:
            two.append(lax.ppermute(mid[s], "chan", swap1))
    done_far, acc_mid, acc_one = call(
        "cross_most",
        [
            ("far", [(last, 0)], 0, True, 0),
            ("mid", [(s, s) for s in early], None, False, 1),
            ("one", [(s, s) for s in early], None, False, 2),
        ],
        sources={"far": far[last:], "mid": mid[:last], "one": one[:last]},
        acc_in=[acc_far],
    )
    mid[last] = after(mid[last], acc_mid)
    two.append(lax.ppermute(mid[last], "chan", swap1))
    done_mid, done_one, acc_two = call(
        "cross_next",
        [
            ("mid", [(last, 0)], 0, True, 0),
            ("one", [(last, 0)], 1, True, 1),
            ("two", [(s, s) for s in early], None, False, 2),
        ],
        sources={"mid": mid[last:], "one": one[last:], "two": two[:last]},
        acc_in=[acc_mid, acc_one],
    )
    two[last] = after(two[last], acc_two)
    (out,) = call(
        "cross_last", [("two", [(last, 0)], 0, True, None)], sources={"two": two[last:]},
        acc_in=[acc_two], done=[done_far, done_mid, done_one],
    )
    bands = out.shape[3] // 2
    out = out.reshape(ROUNDS, chans, chans, bands, 2, LANES).transpose(0, 1, 2, 4, 3, 5)
    return out.reshape(ROUNDS, chans, chans, 2, bands * LANES)


def solution(mesh):
    return jax.shard_map(
        shards,
        mesh=mesh,
        in_specs=(P("chan", "win", None), P()),
        out_specs=P(None, "chan", None, None, "win"),
        check_vma=False,
    )
```

```python
import functools
import math

import jax
import jax.numpy as jnp
from jax import lax
from jax.experimental import pallas as pl
from jax.experimental.pallas import tpu as pltpu
from jax.sharding import PartitionSpec as P

BINS = 4096
BAND = 128
ROUNDS = 4
REACH = 2000
LANES = 128
band_epsilon = 1e-06
VMEM = pl.BlockSpec(memory_space=pltpu.VMEM)
SMEM = pl.BlockSpec(memory_space=pltpu.SMEM)
HBM = pl.BlockSpec(memory_space=pltpu.HBM)
PARAMS = pltpu.CompilerParams(vmem_limit_bytes=40 * 1024 * 1024)


def cost(microseconds):
    return pl.CostEstimate(flops=int(microseconds * 1.1e9), bytes_accessed=0, transcendentals=0)


def split3(value):
    hi = value.astype(jnp.bfloat16)
    rest = value - hi.astype(jnp.float32)
    mid = rest.astype(jnp.bfloat16)
    lo = (rest - mid.astype(jnp.float32)).astype(jnp.bfloat16)
    return hi, mid, lo


def real_dft(values):
    n = len(values)
    if n == 2:
        return [(values[0] + values[1], None), (values[0] - values[1], None)]
    even, odd = real_dft(values[0::2]), real_dft(values[1::2])
    out = [None] * (n // 2 + 1)
    for k in range(n // 4 + 1):
        (er, ei), (dr, di) = even[k], odd[k]
        if k == 0:
            out[0] = (er + dr, None)
            out[n // 2] = (er - dr, None)
        elif 4 * k == n:
            out[k] = (er, -dr)
        else:
            c, s = math.cos(2.0 * math.pi * k / n), math.sin(2.0 * math.pi * k / n)
            tr = dr * c + di * s
            ti = di * c - dr * s
            out[k] = (er + tr, ei + ti)
            out[n // 2 - k] = (er - tr, ti - ei)
    return out


def spectra_channel(parts, chan, x, tw_ref, l2_ref, t_ref, outs):
    first = len(x)
    wins = x[0].shape[0]
    bands = BINS // BAND // parts
    terms = real_dft(x)
    for k in range(first):
        re, im = terms[min(k, first - k)]
        rows = pl.ds(k * wins, wins)
        cos, sin = tw_ref[0, pl.ds(k, 1), :], tw_ref[1, pl.ds(k, 1), :]
        if im is None:
            t_ref[chan, 0, rows, :] = re * cos
            t_ref[chan, 1, rows, :] = -(re * sin)
        elif 2 * k <= first:
            t_ref[chan, 0, rows, :] = re * cos + im * sin
            t_ref[chan, 1, rows, :] = im * cos - re * sin
        else:
            t_ref[chan, 0, rows, :] = re * cos - im * sin
            t_ref[chan, 1, rows, :] = -(im * cos + re * sin)
    rhs = []
    for win in range(wins):
        at = pl.ds(win, first, stride=wins)
        row = jnp.concatenate([t_ref[chan, 0, at, :], t_ref[chan, 1, at, :]], axis=1)
        hi, mid, lo = split3(row)
        rhs.append(jnp.concatenate([hi, mid, lo, hi, mid, hi], axis=1))
    spec = lax.dot_general(
        l2_ref[...],
        jnp.concatenate(rhs, axis=0),
        (((1,), (1,)), ((), ())),
        preferred_element_type=jnp.float32,
    )
    left = lax.broadcasted_iota(jnp.int32, (bands, LANES), 1) < first
    pairs = wins // 2
    tiles = [
        spec[:, i * LANES : (i + 1) * LANES].reshape(parts, 4, bands, LANES) for i in range(pairs)
    ]
    powers = []
    for tile in tiles:
        square = tile * tile
        power = square[:, 0] + square[:, 1] + square[:, 2] + square[:, 3]
        powers.append(power.reshape(parts * bands, LANES))
    row = lax.rem(lax.broadcasted_iota(jnp.int32, (3 * LANES, LANES), 0), LANES)
    lane = lax.broadcasted_iota(jnp.int32, (3 * LANES, LANES), 1)
    ones = ((row < first) == (lane < first)).astype(jnp.bfloat16)
    total = jnp.dot(
        jnp.concatenate(split3(jnp.concatenate(powers, axis=0)), axis=1),
        ones,
        preferred_element_type=jnp.float32,
    )
    scales = lax.rsqrt(total * (1.0 / BAND) + band_epsilon).reshape(pairs, parts, bands, LANES)
    for pair in range(pairs):
        for s in range(parts):
            scale = scales[pair, s]
            for imag in range(2):
                even = tiles[pair][s, 2 * imag] * scale
                odd = tiles[pair][s, 2 * imag + 1] * scale
                one = jnp.where(left, even, pltpu.roll(odd, first, 1)).astype(jnp.bfloat16)
                two = jnp.where(left, pltpu.roll(even, first, 1), odd).astype(jnp.bfloat16)
                at = pl.ds(imag * bands, bands)
                outs[s][chan, 2 * pair, at, :] = one
                outs[s][chan, 2 * pair + 1, at, :] = two


def turn_table(index, period):
    index = lax.rem(index, period)
    quarter = period // 4
    turn = lax.div(index + quarter // 2, quarter)
    angle = (index - turn * quarter).astype(jnp.float32) * (2.0 * math.pi / period)
    square = angle * angle

    def series(first):
        value = jnp.full_like(angle, 0.0)
        for power in range(10 + first, first - 1, -2):
            value = value * square + (-1) ** (power // 2) / math.factorial(power)
        return value

    cos, sin = series(0), series(1) * angle
    swap = lax.rem(turn, 2) == 1
    minus_cos = (turn == 1) | (turn == 2)
    minus_sin = (turn == 2) | (turn == 3)
    cos, sin = jnp.where(swap, sin, cos), jnp.where(swap, cos, sin)
    return jnp.where(minus_cos, -cos, cos), jnp.where(minus_sin, -sin, sin)


def gains_kernel(chans, inv_root, pos_ref, gain_ref):
    block = lax.axis_index("chan")
    last = pos_ref.shape[0] - 1
    for row in range(ROUNDS * chans * chans):
        rnd, a, c = row // (chans * chans), row // chans % chans, row % chans
        pos_c = pos_ref[lax.min((block + rnd + 1) * chans + c, last)]
        near = pos_c - pos_ref[block * chans + a] <= REACH
        gain = jnp.where(near, inv_root, 0.0).astype(jnp.float32)
        gain_ref[pl.ds(row, 1), :] = jnp.full((1, LANES), gain)


def stack_gains(positions, chans, windows):
    return pl.pallas_call(
        functools.partial(gains_kernel, chans, 1.0 / math.sqrt(windows)),
        in_specs=[SMEM],
        out_specs=VMEM,
        out_shape=jax.ShapeDtypeStruct((ROUNDS * chans * chans, LANES), jnp.float32),
        compiler_params=PARAMS,
        cost_estimate=cost(0.5),
        name="gains",
    )(positions)


def tables_kernel(parts, samples, tw_ref, l2_ref):
    first = samples // LANES
    bands = BINS // BAND // parts
    me = lax.axis_index("win")
    k1 = lax.broadcasted_iota(jnp.int32, (first, LANES), 0)
    q = lax.broadcasted_iota(jnp.int32, (first, LANES), 1)
    tw_ref[0], tw_ref[1] = turn_table(k1 * q, samples)
    band = lax.broadcasted_iota(jnp.int32, (bands, LANES), 0)
    q = lax.broadcasted_iota(jnp.int32, (bands, LANES), 1)
    for s in range(parts):
        part = lax.rem(me + s, parts)
        tables = [turn_table((2 * (part * bands + band) + odd) * q, LANES) for odd in range(2)]
        rows = [jnp.concatenate([cos, sin], axis=1) for cos, sin in tables]
        rows += [jnp.concatenate([-sin, cos], axis=1) for cos, sin in tables]
        hi, mid, lo = split3(jnp.concatenate(rows, axis=0))
        table = jnp.concatenate([hi, hi, hi, mid, mid, lo], axis=1)
        l2_ref[pl.ds(s * 4 * bands, 4 * bands), :] = table


def spectra_kernel(parts, x_ref, tw_ref, l2_ref, *refs):
    outs, t_ref = refs[:-1], refs[-1]
    chans, first = x_ref.shape[:2]
    for chan in range(chans):
        x = [x_ref[chan, p] for p in range(first)]
        spectra_channel(parts, chan, x, tw_ref, l2_ref, t_ref, outs)


def whitened_spectra(records, parts):
    chans, wins, samples = records.shape
    first = samples // LANES
    rows = 2 * (BINS // BAND // parts)
    x = records.reshape(chans, wins, first, LANES).transpose(0, 2, 1, 3)
    tables = pl.pallas_call(
        functools.partial(tables_kernel, parts, samples),
        out_specs=[VMEM] * 2,
        out_shape=[
            jax.ShapeDtypeStruct((2, first, LANES), jnp.float32),
            jax.ShapeDtypeStruct((2 * rows * parts, 12 * LANES), jnp.bfloat16),
        ],
        compiler_params=PARAMS,
        cost_estimate=cost(1),
        name="tables",
    )()
    return pl.pallas_call(
        functools.partial(spectra_kernel, parts),
        in_specs=[VMEM] * 3,
        out_specs=[VMEM] * parts,
        out_shape=[jax.ShapeDtypeStruct((chans, wins, rows, LANES), jnp.bfloat16)] * parts,
        scratch_shapes=[pltpu.VMEM((chans, 2, first * wins, LANES), jnp.float32)],
        compiler_params=PARAMS,
        cost_estimate=cost(4),
        name="spectra",
    )(x, *tables)


def cross_unit(mine, theirs, acc):
    rows = mine[0][0].shape[1]
    bands = rows // 2
    wins = mine[0][0].shape[0]
    per_step = wins if wins <= 8 else 1

    def planes(ref, win):
        return [ref[win, pl.ds(i * bands, bands), :].astype(jnp.float32) for i in range(2)]

    for own, their in zip(mine, theirs):

        def step(index, acc, own=own, their=their):
            acc = list(acc)
            for i in range(per_step):
                win = index * per_step + i
                ours = [planes(ref, win) for ref in own]
                for c, ref in enumerate(their):
                    cr, ci = planes(ref, win)
                    for a, (ar, ai) in enumerate(ours):
                        at = 2 * (a * len(their) + c)
                        acc[at] = acc[at] + ar * cr + ai * ci
                        acc[at + 1] = acc[at + 1] + ai * cr - ar * ci
            return tuple(acc)

        acc = lax.fori_loop(0, wins // per_step, step, acc)
    return acc


def cross_kernel(layout, jobs, *refs):
    groups, at = {}, 0
    for name, count in layout:
        groups[name] = refs[at : at + count]
        at += count
    (gain_ref,) = groups["gains"]
    mine = groups["mine"]
    chans, _, rows, _ = mine[0].shape
    bands = rows // 2
    odd = lax.rem(lax.axis_index("chan"), 2)
    rounds = {"one": 2 * odd, "mid": 1, "two": 2 - 2 * odd, "far": 3}
    step = 2
    copies = []

    def send(source, ref, a_start, count):
        (out_ref,), (sems,) = groups["out"], groups["sems"]
        part = pl.ds(a_start, count)
        copy = pltpu.make_async_copy(
            ref.at[part], out_ref.at[rounds[source], part], sems.at[len(copies)]
        )
        copy.start()
        copies.append(copy)

    for source, ref in zip(("far", "mid", "one"), groups["done"]):
        send(source, ref, 0, chans)
    for source, pieces, acc_in, final, to in jobs:
        rnd = rounds[source]
        to_ref = groups["buffer"][0] if to is None else groups["acc_out"][to]
        for a_start in range(0, chans, step):
            a_list = range(a_start, min(a_start + step, chans))
            for c_start in range(0, chans, step):
                c_list = range(c_start, min(c_start + step, chans))
                ours = [[mine[piece].at[a] for a in a_list] for piece, _ in pieces]
                theirs = [[groups[source][ref].at[c] for c in c_list] for _, ref in pieces]
                order = [(a, c, i) for a in a_list for c in c_list for i in range(2)]
                if acc_in is None:
                    acc = tuple(jnp.zeros((bands, LANES), jnp.float32) for _ in order)
                else:
                    ref = groups["acc_in"][acc_in]
                    acc = tuple(ref[a, c, pl.ds(i * bands, bands), :] for a, c, i in order)
                acc = cross_unit(ours, theirs, acc)
                for (a, c, i), value in zip(order, acc):
                    if not final:
                        to_ref[a, c, pl.ds(i * bands, bands), :] = value
                        continue
                    gain = gain_ref[pl.ds((rnd * chans + a) * chans + c, 1), :]
                    to_ref[a, c, pl.ds(i, bands, stride=2), :] = value * gain
            if to is None:
                send(source, to_ref, a_start, len(a_list))
    for copy in copies:
        copy.wait()


def cross_call(name, jobs, gains, mine, sources, acc_in=(), done=()):
    chans, _, rows, _ = mine[0].shape
    groups = [("gains", [gains]), ("mine", mine), *sources.items()]
    groups += [("acc_in", acc_in), ("done", done)]
    groups = [(key, list(arrays)) for key, arrays in groups]
    operands = [array for _, arrays in groups for array in arrays]
    layout = [(key, len(arrays)) for key, arrays in groups]
    sums = jax.ShapeDtypeStruct((chans, chans, rows, LANES), jnp.float32)
    whole = jax.ShapeDtypeStruct((ROUNDS,) + sums.shape, jnp.float32)
    acc_count = sum(job[4] is not None for job in jobs)
    ends = 1 - acc_count // len(jobs)
    layout += [("out", ends), ("acc_out", acc_count), ("buffer", ends), ("sems", ends)]
    scratch = [pltpu.VMEM(sums.shape, jnp.float32), pltpu.SemaphoreType.DMA((chans + len(done),))]
    return pl.pallas_call(
        functools.partial(cross_kernel, layout, jobs),
        in_specs=[VMEM] * len(operands),
        out_specs=[HBM] * ends + [VMEM] * acc_count,
        out_shape=[whole] * ends + [sums] * acc_count,
        scratch_shapes=scratch * ends,
        compiler_params=PARAMS,
        cost_estimate=cost(0.6 * sum(len(job[1]) for job in jobs)),
        name=name,
    )(*operands)


def choose(bit, own, far):
    def kernel(own_ref, far_ref, out_ref):
        yes = lax.rem(lax.div(lax.axis_index("chan"), bit), 2) == 1

        @pl.when(yes)
        def _():
            out_ref[...] = own_ref[...]

        @pl.when(jnp.logical_not(yes))
        def _():
            out_ref[...] = far_ref[...]

    return pl.pallas_call(
        kernel,
        in_specs=[VMEM] * 2,
        out_specs=VMEM,
        out_shape=jax.ShapeDtypeStruct(far.shape, far.dtype),
        compiler_params=PARAMS,
        cost_estimate=cost(0.1),
        name="choose",
    )(own, far)


def after(value, *others):
    return lax.optimization_barrier((value, *others))[0]


def shards(records, positions):
    parts = lax.axis_size("win")
    blocks = lax.axis_size("chan")
    chans, wins, _ = records.shape
    spectra = whitened_spectra(records, parts)
    up = [(b, b - 4) for b in range(4, blocks)]
    swap2 = [(b, b ^ 2) for b in range(blocks)]
    swap1 = [(b, b ^ 1) for b in range(blocks)]
    mine = [spectra[0]]
    for s in range(1, parts):
        mine.append(lax.ppermute(spectra[s], "win", [(i, (i + s) % parts) for i in range(parts)]))
    far = [lax.ppermute(own, "chan", up) for own in mine]
    last = parts - 1
    early = range(last)
    gains = stack_gains(after(positions, far[0]), chans, parts * wins)
    call = functools.partial(cross_call, gains=gains, mine=mine)

    (acc_far,) = call(
        "cross_far", [("far", [(s, s) for s in early], None, False, 0)], sources={"far": far[:-1]}
    )
    far[last] = after(far[last], acc_far)
    mid, one, two = [], [], []
    for s in range(parts):
        if s < last:
            mid.append(lax.ppermute(choose(2, mine[s], far[s]), "chan", swap2))
        else:
            mid.append(lax.ppermute(mine[s], "chan", [(b, b - 2) for b in range(2, blocks)]))
        one.append(lax.ppermute(choose(1, mine[s], far[s]), "chan", swap1))
        if s < last:
            two.append(lax.ppermute(mid[s], "chan", swap1))
    done_far, acc_mid, acc_one = call(
        "cross_most",
        [
            ("far", [(last, 0)], 0, True, 0),
            ("mid", [(s, s) for s in early], None, False, 1),
            ("one", [(s, s) for s in early], None, False, 2),
        ],
        sources={"far": far[last:], "mid": mid[:last], "one": one[:last]},
        acc_in=[acc_far],
    )
    mid[last] = after(mid[last], acc_mid)
    two.append(lax.ppermute(mid[last], "chan", swap1))
    done_mid, done_one, acc_two = call(
        "cross_next",
        [
            ("mid", [(last, 0)], 0, True, 0),
            ("one", [(last, 0)], 1, True, 1),
            ("two", [(s, s) for s in early], None, False, 2),
        ],
        sources={"mid": mid[last:], "one": one[last:], "two": two[:last]},
        acc_in=[acc_mid, acc_one],
    )
    two[last] = after(two[last], acc_two)
    (out,) = call(
        "cross_last", [("two", [(last, 0)], 0, True, None)], sources={"two": two[last:]},
        acc_in=[acc_two], done=[done_far, done_mid, done_one],
    )
    bands = out.shape[3] // 2
    out = out.reshape(ROUNDS, chans, chans, bands, 2, LANES).transpose(0, 1, 2, 4, 3, 5)
    return out.reshape(ROUNDS, chans, chans, 2, bands * LANES)


def solution(mesh):
    return jax.shard_map(
        shards,
        mesh=mesh,
        in_specs=(P("chan", "win", None), P()),
        out_specs=P(None, "chan", None, None, "win"),
        check_vma=False,
    )
```

```python
import functools
import math

import jax
import jax.numpy as jnp
from jax import lax
from jax.experimental import pallas as pl
from jax.experimental.pallas import tpu as pltpu
from jax.sharding import PartitionSpec as P

BINS = 4096
BAND = 128
ROUNDS = 4
REACH = 2000
LANES = 128
band_epsilon = 1e-06
VMEM = pl.BlockSpec(memory_space=pltpu.VMEM)
SMEM = pl.BlockSpec(memory_space=pltpu.SMEM)
HBM = pl.BlockSpec(memory_space=pltpu.HBM)
PARAMS = pltpu.CompilerParams(vmem_limit_bytes=40 * 1024 * 1024)


def cost(microseconds):
    return pl.CostEstimate(flops=int(microseconds * 1.1e9), bytes_accessed=0, transcendentals=0)


def split3(value):
    hi = value.astype(jnp.bfloat16)
    rest = value - hi.astype(jnp.float32)
    mid = rest.astype(jnp.bfloat16)
    lo = (rest - mid.astype(jnp.float32)).astype(jnp.bfloat16)
    return hi, mid, lo


def real_dft(values):
    n = len(values)
    if n == 2:
        return [(values[0] + values[1], None), (values[0] - values[1], None)]
    even, odd = real_dft(values[0::2]), real_dft(values[1::2])
    out = [None] * (n // 2 + 1)
    for k in range(n // 4 + 1):
        (er, ei), (dr, di) = even[k], odd[k]
        if k == 0:
            out[0] = (er + dr, None)
            out[n // 2] = (er - dr, None)
        elif 4 * k == n:
            out[k] = (er, -dr)
        else:
            c, s = math.cos(2.0 * math.pi * k / n), math.sin(2.0 * math.pi * k / n)
            tr = dr * c + di * s
            ti = di * c - dr * s
            out[k] = (er + tr, ei + ti)
            out[n // 2 - k] = (er - tr, ti - ei)
    return out


def spectra_channel(parts, chan, x, tables, t_ref, outs):
    tw_ref, main_ref, side_ref, bands_ref, pick_ref = tables
    first = len(x)
    wins = x[0].shape[0]
    bands = BINS // BAND // parts
    terms = real_dft(x)
    rows = []
    for k in range(first):
        re, im = terms[min(k, first - k)]
        cos, sin = tw_ref[0, pl.ds(k, 1), :], tw_ref[1, pl.ds(k, 1), :]
        if im is None:
            row = [re * cos, -(re * sin)]
        elif 2 * k <= first:
            row = [re * cos + im * sin, im * cos - re * sin]
        else:
            row = [re * cos - im * sin, -(im * cos + re * sin)]
        rows.append(jnp.concatenate(row, axis=1))
    hi, mid, lo = split3(jnp.concatenate(rows, axis=0))
    main = jnp.dot(
        jnp.concatenate([hi, mid], axis=1), main_ref[...], preferred_element_type=jnp.float32
    )
    side = jnp.dot(
        jnp.concatenate([hi, lo], axis=1), side_ref[...], preferred_element_type=jnp.float32
    )
    spec = (main[:, :LANES] + main[:, LANES:] + side).reshape(first, wins, LANES)
    total = jnp.dot(
        jnp.concatenate(split3(jnp.sum(spec * spec, axis=0)), axis=1),
        bands_ref[...],
        preferred_element_type=jnp.float32,
    )
    scale = lax.rsqrt(total * (1.0 / BAND) + band_epsilon)
    t_ref[chan] = (spec * scale).reshape(first * wins, LANES)
    white = jnp.concatenate(
        [t_ref[chan, pl.ds(win, first, stride=wins), :].astype(jnp.bfloat16) for win in range(wins)],
        axis=0,
    )
    spread = lax.dot_general(
        pick_ref[...], white, (((1,), (1,)), ((), ())), preferred_element_type=jnp.float32
    )
    left = lax.broadcasted_iota(jnp.int32, (bands, LANES), 1) < first
    for pair in range(wins // 2):
        tile = spread[:, pair * LANES : (pair + 1) * LANES].reshape(parts, 2, 2, bands, LANES)
        for s in range(parts):
            for imag in range(2):
                even, odd = tile[s, imag, 0], tile[s, imag, 1]
                one = jnp.where(left, even, pltpu.roll(odd, first, 1)).astype(jnp.bfloat16)
                two = jnp.where(left, pltpu.roll(even, first, 1), odd).astype(jnp.bfloat16)
                at = pl.ds(imag * bands, bands)
                outs[s][chan, 2 * pair, at, :] = one
                outs[s][chan, 2 * pair + 1, at, :] = two


def turn_table(index, period):
    index = lax.rem(index, period)
    quarter = period // 4
    turn = lax.div(index + quarter // 2, quarter)
    angle = (index - turn * quarter).astype(jnp.float32) * (2.0 * math.pi / period)
    square = angle * angle

    def series(first):
        value = jnp.full_like(angle, 0.0)
        for power in range(10 + first, first - 1, -2):
            value = value * square + (-1) ** (power // 2) / math.factorial(power)
        return value

    cos, sin = series(0), series(1) * angle
    swap = lax.rem(turn, 2) == 1
    minus_cos = (turn == 1) | (turn == 2)
    minus_sin = (turn == 2) | (turn == 3)
    cos, sin = jnp.where(swap, sin, cos), jnp.where(swap, cos, sin)
    return jnp.where(minus_cos, -cos, cos), jnp.where(minus_sin, -sin, sin)


def gains_kernel(chans, inv_root, pos_ref, gain_ref):
    block = lax.axis_index("chan")
    last = pos_ref.shape[0] - 1
    for row in range(ROUNDS * chans * chans):
        rnd, a, c = row // (chans * chans), row // chans % chans, row % chans
        pos_c = pos_ref[lax.min((block + rnd + 1) * chans + c, last)]
        near = pos_c - pos_ref[block * chans + a] <= REACH
        gain = jnp.where(near, inv_root, 0.0).astype(jnp.float32)
        gain_ref[pl.ds(row, 1), :] = jnp.full((1, LANES), gain)


def stack_gains(positions, chans, windows):
    return pl.pallas_call(
        functools.partial(gains_kernel, chans, 1.0 / math.sqrt(windows)),
        in_specs=[SMEM],
        out_specs=VMEM,
        out_shape=jax.ShapeDtypeStruct((ROUNDS * chans * chans, LANES), jnp.float32),
        compiler_params=PARAMS,
        cost_estimate=cost(0.5),
        name="gains",
    )(positions)


def tables_kernel(parts, samples, tw_ref, main_ref, side_ref, bands_ref, pick_ref):
    first = samples // LANES
    bands = BINS // BAND // parts
    me = lax.axis_index("win")
    k1 = lax.broadcasted_iota(jnp.int32, (first, LANES), 0)
    q = lax.broadcasted_iota(jnp.int32, (first, LANES), 1)
    tw_ref[0], tw_ref[1] = turn_table(k1 * q, samples)
    row = lax.broadcasted_iota(jnp.int32, (LANES, LANES), 0)
    lane = lax.broadcasted_iota(jnp.int32, (LANES, LANES), 1)
    real = lane < first
    m = lax.rem(lane, first)
    cos, sin = turn_table(row * m, LANES)
    table = jnp.concatenate([jnp.where(real, cos, -sin), jnp.where(real, sin, cos)], axis=0)
    hi, mid, lo = split3(table)
    wide = jnp.concatenate([hi, mid], axis=1)
    main_ref[...] = jnp.concatenate([wide, wide], axis=0)
    side_ref[...] = jnp.concatenate([lo, hi], axis=0)
    same = lax.div(lax.rem(row, first), 2) == lax.div(m, 2)
    bands_ref[...] = jnp.concatenate([same.astype(jnp.float32)] * 3, axis=0).astype(jnp.bfloat16)
    part = lax.rem(me + lax.div(row, 4 * bands), parts)
    imag = lax.rem(lax.div(row, 2 * bands), 2)
    odd = lax.rem(lax.div(row, bands), 2)
    source = imag * first + 2 * (part * bands + lax.rem(row, bands)) + odd
    pick_ref[...] = (lane == source).astype(jnp.float32).astype(jnp.bfloat16)


def spectra_kernel(parts, x_ref, *refs):
    tables, outs, t_ref = refs[:5], refs[5:-1], refs[-1]
    chans, first = x_ref.shape[:2]
    for chan in range(chans):
        x = [x_ref[chan, p] for p in range(first)]
        spectra_channel(parts, chan, x, tables, t_ref, outs)


def whitened_spectra(records, parts):
    chans, wins, samples = records.shape
    first = samples // LANES
    rows = 2 * (BINS // BAND // parts)
    x = records.reshape(chans, wins, first, LANES).transpose(0, 2, 1, 3)
    tables = pl.pallas_call(
        functools.partial(tables_kernel, parts, samples),
        out_specs=[VMEM] * 5,
        out_shape=[
            jax.ShapeDtypeStruct((2, first, LANES), jnp.float32),
            jax.ShapeDtypeStruct((4 * LANES, 2 * LANES), jnp.bfloat16),
            jax.ShapeDtypeStruct((4 * LANES, LANES), jnp.bfloat16),
            jax.ShapeDtypeStruct((3 * LANES, LANES), jnp.bfloat16),
            jax.ShapeDtypeStruct((LANES, LANES), jnp.bfloat16),
        ],
        compiler_params=PARAMS,
        cost_estimate=cost(1),
        name="tables",
    )()
    return pl.pallas_call(
        functools.partial(spectra_kernel, parts),
        in_specs=[VMEM] * 6,
        out_specs=[VMEM] * parts,
        out_shape=[jax.ShapeDtypeStruct((chans, wins, rows, LANES), jnp.bfloat16)] * parts,
        scratch_shapes=[pltpu.VMEM((chans, first * wins, LANES), jnp.float32)],
        compiler_params=PARAMS,
        cost_estimate=cost(4),
        name="spectra",
    )(x, *tables)


def cross_unit(mine, theirs, acc):
    rows = mine[0][0].shape[1]
    bands = rows // 2
    wins = mine[0][0].shape[0]
    per_step = wins if wins <= 8 else 1

    def planes(ref, win):
        return [ref[win, pl.ds(i * bands, bands), :].astype(jnp.float32) for i in range(2)]

    for own, their in zip(mine, theirs):

        def step(index, acc, own=own, their=their):
            acc = list(acc)
            for i in range(per_step):
                win = index * per_step + i
                ours = [planes(ref, win) for ref in own]
                for c, ref in enumerate(their):
                    cr, ci = planes(ref, win)
                    for a, (ar, ai) in enumerate(ours):
                        at = 2 * (a * len(their) + c)
                        acc[at] = acc[at] + ar * cr + ai * ci
                        acc[at + 1] = acc[at + 1] + ai * cr - ar * ci
            return tuple(acc)

        acc = lax.fori_loop(0, wins // per_step, step, acc)
    return acc


def cross_kernel(layout, jobs, *refs):
    groups, at = {}, 0
    for name, count in layout:
        groups[name] = refs[at : at + count]
        at += count
    (gain_ref,) = groups["gains"]
    mine = groups["mine"]
    chans, _, rows, _ = mine[0].shape
    bands = rows // 2
    odd = lax.rem(lax.axis_index("chan"), 2)
    rounds = {"one": 2 * odd, "mid": 1, "two": 2 - 2 * odd, "far": 3}
    step = 2
    copies = []

    def send(source, ref, a_start, count):
        (out_ref,), (sems,) = groups["out"], groups["sems"]
        part = pl.ds(a_start, count)
        copy = pltpu.make_async_copy(
            ref.at[part], out_ref.at[rounds[source], part], sems.at[len(copies)]
        )
        copy.start()
        copies.append(copy)

    for source, ref in zip(("far", "mid", "one"), groups["done"]):
        send(source, ref, 0, chans)
    for source, pieces, acc_in, final, to in jobs:
        rnd = rounds[source]
        to_ref = groups["buffer"][0] if to is None else groups["acc_out"][to]
        for a_start in range(0, chans, step):
            a_list = range(a_start, min(a_start + step, chans))
            for c_start in range(0, chans, step):
                c_list = range(c_start, min(c_start + step, chans))
                ours = [[mine[piece].at[a] for a in a_list] for piece, _ in pieces]
                theirs = [[groups[source][ref].at[c] for c in c_list] for _, ref in pieces]
                order = [(a, c, i) for a in a_list for c in c_list for i in range(2)]
                if acc_in is None:
                    acc = tuple(jnp.zeros((bands, LANES), jnp.float32) for _ in order)
                else:
                    ref = groups["acc_in"][acc_in]
                    acc = tuple(ref[a, c, pl.ds(i * bands, bands), :] for a, c, i in order)
                acc = cross_unit(ours, theirs, acc)
                for (a, c, i), value in zip(order, acc):
                    if not final:
                        to_ref[a, c, pl.ds(i * bands, bands), :] = value
                        continue
                    gain = gain_ref[pl.ds((rnd * chans + a) * chans + c, 1), :]
                    to_ref[a, c, pl.ds(i, bands, stride=2), :] = value * gain
            if to is None:
                send(source, to_ref, a_start, len(a_list))
    for copy in copies:
        copy.wait()


def cross_call(name, jobs, gains, mine, sources, acc_in=(), done=()):
    chans, _, rows, _ = mine[0].shape
    groups = [("gains", [gains]), ("mine", mine), *sources.items()]
    groups += [("acc_in", acc_in), ("done", done)]
    groups = [(key, list(arrays)) for key, arrays in groups]
    operands = [array for _, arrays in groups for array in arrays]
    layout = [(key, len(arrays)) for key, arrays in groups]
    sums = jax.ShapeDtypeStruct((chans, chans, rows, LANES), jnp.float32)
    whole = jax.ShapeDtypeStruct((ROUNDS,) + sums.shape, jnp.float32)
    acc_count = sum(job[4] is not None for job in jobs)
    ends = 1 - acc_count // len(jobs)
    layout += [("out", ends), ("acc_out", acc_count), ("buffer", ends), ("sems", ends)]
    scratch = [pltpu.VMEM(sums.shape, jnp.float32), pltpu.SemaphoreType.DMA((chans + len(done),))]
    return pl.pallas_call(
        functools.partial(cross_kernel, layout, jobs),
        in_specs=[VMEM] * len(operands),
        out_specs=[HBM] * ends + [VMEM] * acc_count,
        out_shape=[whole] * ends + [sums] * acc_count,
        scratch_shapes=scratch * ends,
        compiler_params=PARAMS,
        cost_estimate=cost(0.6 * sum(len(job[1]) for job in jobs)),
        name=name,
    )(*operands)


def choose(bit, own, far):
    def kernel(own_ref, far_ref, out_ref):
        yes = lax.rem(lax.div(lax.axis_index("chan"), bit), 2) == 1

        @pl.when(yes)
        def _():
            out_ref[...] = own_ref[...]

        @pl.when(jnp.logical_not(yes))
        def _():
            out_ref[...] = far_ref[...]

    return pl.pallas_call(
        kernel,
        in_specs=[VMEM] * 2,
        out_specs=VMEM,
        out_shape=jax.ShapeDtypeStruct(far.shape, far.dtype),
        compiler_params=PARAMS,
        cost_estimate=cost(0.1),
        name="choose",
    )(own, far)


def after(value, *others):
    return lax.optimization_barrier((value, *others))[0]


def shards(records, positions):
    parts = lax.axis_size("win")
    blocks = lax.axis_size("chan")
    chans, wins, _ = records.shape
    spectra = whitened_spectra(records, parts)
    up = [(b, b - 4) for b in range(4, blocks)]
    swap2 = [(b, b ^ 2) for b in range(blocks)]
    swap1 = [(b, b ^ 1) for b in range(blocks)]
    mine = [spectra[0]]
    for s in range(1, parts):
        mine.append(lax.ppermute(spectra[s], "win", [(i, (i + s) % parts) for i in range(parts)]))
    far = [lax.ppermute(own, "chan", up) for own in mine]
    last = parts - 1
    early = range(last)
    gains = stack_gains(after(positions, far[0]), chans, parts * wins)
    call = functools.partial(cross_call, gains=gains, mine=mine)

    (acc_far,) = call(
        "cross_far", [("far", [(s, s) for s in early], None, False, 0)], sources={"far": far[:-1]}
    )
    far[last] = after(far[last], acc_far)
    mid, one, two = [], [], []
    for s in range(parts):
        mid.append(lax.ppermute(choose(2, mine[s], far[s]), "chan", swap2))
        one.append(lax.ppermute(choose(1, mine[s], far[s]), "chan", swap1))
        if s < last:
            two.append(lax.ppermute(mid[s], "chan", swap1))
    done_far, acc_mid, acc_one = call(
        "cross_most",
        [
            ("far", [(last, 0)], 0, True, 0),
            ("mid", [(s, s) for s in early], None, False, 1),
            ("one", [(s, s) for s in early], None, False, 2),
        ],
        sources={"far": far[last:], "mid": mid[:last], "one": one[:last]},
        acc_in=[acc_far],
    )
    mid[last] = after(mid[last], acc_mid)
    two.append(lax.ppermute(mid[last], "chan", swap1))
    done_mid, done_one, acc_two = call(
        "cross_next",
        [
            ("mid", [(last, 0)], 0, True, 0),
            ("one", [(last, 0)], 1, True, 1),
            ("two", [(s, s) for s in early], None, False, 2),
        ],
        sources={"mid": mid[last:], "one": one[last:], "two": two[:last]},
        acc_in=[acc_mid, acc_one],
    )
    two[last] = after(two[last], acc_two)
    (out,) = call(
        "cross_last", [("two", [(last, 0)], 0, True, None)], sources={"two": two[last:]},
        acc_in=[acc_two], done=[done_far, done_mid, done_one],
    )
    bands = out.shape[3] // 2
    out = out.reshape(ROUNDS, chans, chans, bands, 2, LANES).transpose(0, 1, 2, 4, 3, 5)
    return out.reshape(ROUNDS, chans, chans, 2, bands * LANES)


def solution(mesh):
    return jax.shard_map(
        shards,
        mesh=mesh,
        in_specs=(P("chan", "win", None), P()),
        out_specs=P(None, "chan", None, None, "win"),
        check_vma=False,
    )
```

```python
import functools
import math

import jax
import jax.numpy as jnp
from jax import lax
from jax.experimental import pallas as pl
from jax.experimental.pallas import tpu as pltpu
from jax.sharding import PartitionSpec as P

BINS = 4096
BAND = 128
ROUNDS = 4
REACH = 2000
LANES = 128
band_epsilon = 1e-06
VMEM = pl.BlockSpec(memory_space=pltpu.VMEM)
SMEM = pl.BlockSpec(memory_space=pltpu.SMEM)
HBM = pl.BlockSpec(memory_space=pltpu.HBM)
PARAMS = pltpu.CompilerParams(vmem_limit_bytes=40 * 1024 * 1024)


def cost(microseconds):
    return pl.CostEstimate(flops=int(microseconds * 1.1e9), bytes_accessed=0, transcendentals=0)


def split3(value):
    hi = value.astype(jnp.bfloat16)
    rest = value - hi.astype(jnp.float32)
    mid = rest.astype(jnp.bfloat16)
    lo = (rest - mid.astype(jnp.float32)).astype(jnp.bfloat16)
    return hi, mid, lo


def real_dft(values):
    n = len(values)
    if n == 2:
        return [(values[0] + values[1], None), (values[0] - values[1], None)]
    even, odd = real_dft(values[0::2]), real_dft(values[1::2])
    out = [None] * (n // 2 + 1)
    for k in range(n // 4 + 1):
        (er, ei), (dr, di) = even[k], odd[k]
        if k == 0:
            out[0] = (er + dr, None)
            out[n // 2] = (er - dr, None)
        elif 4 * k == n:
            out[k] = (er, -dr)
        else:
            c, s = math.cos(2.0 * math.pi * k / n), math.sin(2.0 * math.pi * k / n)
            tr = dr * c + di * s
            ti = di * c - dr * s
            out[k] = (er + tr, ei + ti)
            out[n // 2 - k] = (er - tr, ti - ei)
    return out


def spectra_channel(parts, chan, x, tables, t_ref, outs):
    tw_ref, main_ref, side_ref, bands_ref, pick_ref = tables
    first = len(x)
    wins = x[0].shape[0]
    bands = BINS // BAND // parts
    terms = real_dft(x)
    rows = []
    for k in range(first):
        re, im = terms[min(k, first - k)]
        cos, sin = tw_ref[0, pl.ds(k, 1), :], tw_ref[1, pl.ds(k, 1), :]
        if im is None:
            row = [re * cos, -(re * sin)]
        elif 2 * k <= first:
            row = [re * cos + im * sin, im * cos - re * sin]
        else:
            row = [re * cos - im * sin, -(im * cos + re * sin)]
        rows.append(jnp.concatenate(row, axis=1))
    hi, mid, lo = split3(jnp.concatenate(rows, axis=0))
    main = jnp.dot(
        jnp.concatenate([hi, mid], axis=1), main_ref[...], preferred_element_type=jnp.float32
    )
    side = jnp.dot(
        jnp.concatenate([hi, lo], axis=1), side_ref[...], preferred_element_type=jnp.float32
    )
    spec = (main[:, :LANES] + main[:, LANES:] + side).reshape(first, wins, LANES)
    total = jnp.dot(
        jnp.concatenate(split3(jnp.sum(spec * spec, axis=0)), axis=1),
        bands_ref[...],
        preferred_element_type=jnp.float32,
    )
    scale = lax.rsqrt(total * (1.0 / BAND) + band_epsilon)
    t_ref[chan] = (spec * scale).reshape(first * wins, LANES)
    white = jnp.concatenate(
        [t_ref[chan, pl.ds(win, first, stride=wins), :].astype(jnp.bfloat16) for win in range(wins)],
        axis=0,
    )
    spread = lax.dot_general(
        pick_ref[...], white, (((1,), (1,)), ((), ())), preferred_element_type=jnp.float32
    )
    left = lax.broadcasted_iota(jnp.int32, (bands, LANES), 1) < first
    for pair in range(wins // 2):
        tile = spread[:, pair * LANES : (pair + 1) * LANES].reshape(parts, 2, 2, bands, LANES)
        for s in range(parts):
            for imag in range(2):
                even, odd = tile[s, imag, 0], tile[s, imag, 1]
                one = jnp.where(left, even, pltpu.roll(odd, first, 1)).astype(jnp.bfloat16)
                two = jnp.where(left, pltpu.roll(even, first, 1), odd).astype(jnp.bfloat16)
                at = pl.ds(imag * bands, bands)
                outs[s][chan, 2 * pair, at, :] = one
                outs[s][chan, 2 * pair + 1, at, :] = two


def turn_table(index, period):
    index = lax.rem(index, period)
    quarter = period // 4
    turn = lax.div(index + quarter // 2, quarter)
    angle = (index - turn * quarter).astype(jnp.float32) * (2.0 * math.pi / period)
    square = angle * angle

    def series(first):
        value = jnp.full_like(angle, 0.0)
        for power in range(10 + first, first - 1, -2):
            value = value * square + (-1) ** (power // 2) / math.factorial(power)
        return value

    cos, sin = series(0), series(1) * angle
    swap = lax.rem(turn, 2) == 1
    minus_cos = (turn == 1) | (turn == 2)
    minus_sin = (turn == 2) | (turn == 3)
    cos, sin = jnp.where(swap, sin, cos), jnp.where(swap, cos, sin)
    return jnp.where(minus_cos, -cos, cos), jnp.where(minus_sin, -sin, sin)


def gains_kernel(chans, inv_root, pos_ref, gain_ref):
    block = lax.axis_index("chan")
    last = pos_ref.shape[0] - 1
    for row in range(ROUNDS * chans * chans):
        rnd, a, c = row // (chans * chans), row // chans % chans, row % chans
        pos_c = pos_ref[lax.min((block + rnd + 1) * chans + c, last)]
        near = pos_c - pos_ref[block * chans + a] <= REACH
        gain = jnp.where(near, inv_root, 0.0).astype(jnp.float32)
        gain_ref[pl.ds(row, 1), :] = jnp.full((1, LANES), gain)


def stack_gains(positions, chans, windows):
    return pl.pallas_call(
        functools.partial(gains_kernel, chans, 1.0 / math.sqrt(windows)),
        in_specs=[SMEM],
        out_specs=VMEM,
        out_shape=jax.ShapeDtypeStruct((ROUNDS * chans * chans, LANES), jnp.float32),
        compiler_params=PARAMS,
        cost_estimate=cost(0.5),
        name="gains",
    )(positions)


def tables_kernel(parts, samples, tw_ref, main_ref, side_ref, bands_ref, pick_ref):
    first = samples // LANES
    bands = BINS // BAND // parts
    me = lax.axis_index("win")
    k1 = lax.broadcasted_iota(jnp.int32, (first, LANES), 0)
    q = lax.broadcasted_iota(jnp.int32, (first, LANES), 1)
    tw_ref[0], tw_ref[1] = turn_table(k1 * q, samples)
    row = lax.broadcasted_iota(jnp.int32, (LANES, LANES), 0)
    lane = lax.broadcasted_iota(jnp.int32, (LANES, LANES), 1)
    real = lane < first
    m = lax.rem(lane, first)
    cos, sin = turn_table(row * m, LANES)
    table = jnp.concatenate([jnp.where(real, cos, -sin), jnp.where(real, sin, cos)], axis=0)
    hi, mid, lo = split3(table)
    wide = jnp.concatenate([hi, mid], axis=1)
    main_ref[...] = jnp.concatenate([wide, wide], axis=0)
    side_ref[...] = jnp.concatenate([lo, hi], axis=0)
    same = lax.div(lax.rem(row, first), 2) == lax.div(m, 2)
    bands_ref[...] = jnp.concatenate([same.astype(jnp.float32)] * 3, axis=0).astype(jnp.bfloat16)
    part = lax.rem(me + lax.div(row, 4 * bands), parts)
    imag = lax.rem(lax.div(row, 2 * bands), 2)
    odd = lax.rem(lax.div(row, bands), 2)
    source = imag * first + 2 * (part * bands + lax.rem(row, bands)) + odd
    pick_ref[...] = (lane == source).astype(jnp.float32).astype(jnp.bfloat16)


def spectra_kernel(parts, x_ref, *refs):
    tables, outs, t_ref = refs[:5], refs[5:-1], refs[-1]
    chans, first = x_ref.shape[:2]
    for chan in range(chans):
        x = [x_ref[chan, p] for p in range(first)]
        spectra_channel(parts, chan, x, tables, t_ref, outs)


def whitened_spectra(records, parts):
    chans, wins, samples = records.shape
    first = samples // LANES
    rows = 2 * (BINS // BAND // parts)
    x = records.reshape(chans, wins, first, LANES).transpose(0, 2, 1, 3)
    tables = pl.pallas_call(
        functools.partial(tables_kernel, parts, samples),
        out_specs=[VMEM] * 5,
        out_shape=[
            jax.ShapeDtypeStruct((2, first, LANES), jnp.float32),
            jax.ShapeDtypeStruct((4 * LANES, 2 * LANES), jnp.bfloat16),
            jax.ShapeDtypeStruct((4 * LANES, LANES), jnp.bfloat16),
            jax.ShapeDtypeStruct((3 * LANES, LANES), jnp.bfloat16),
            jax.ShapeDtypeStruct((LANES, LANES), jnp.bfloat16),
        ],
        compiler_params=PARAMS,
        cost_estimate=cost(1),
        name="tables",
    )()
    return pl.pallas_call(
        functools.partial(spectra_kernel, parts),
        in_specs=[VMEM] * 6,
        out_specs=[VMEM] * parts,
        out_shape=[jax.ShapeDtypeStruct((chans, wins, rows, LANES), jnp.bfloat16)] * parts,
        scratch_shapes=[pltpu.VMEM((chans, first * wins, LANES), jnp.float32)],
        compiler_params=PARAMS,
        cost_estimate=cost(4),
        name="spectra",
    )(x, *tables)


def cross_unit(mine, theirs, acc):
    rows = mine[0][0].shape[1]
    bands = rows // 2
    wins = mine[0][0].shape[0]
    per_step = wins if wins <= 8 else 1

    def planes(ref, win):
        return [ref[win, pl.ds(i * bands, bands), :].astype(jnp.float32) for i in range(2)]

    for own, their in zip(mine, theirs):

        def step(index, acc, own=own, their=their):
            acc = list(acc)
            for i in range(per_step):
                win = index * per_step + i
                ours = [planes(ref, win) for ref in own]
                for c, ref in enumerate(their):
                    cr, ci = planes(ref, win)
                    for a, (ar, ai) in enumerate(ours):
                        at = 2 * (a * len(their) + c)
                        acc[at] = acc[at] + ar * cr + ai * ci
                        acc[at + 1] = acc[at + 1] + ai * cr - ar * ci
            return tuple(acc)

        acc = lax.fori_loop(0, wins // per_step, step, acc)
    return acc


def channel(refs, index, chan):
    for i in index if isinstance(index, tuple) else (index,):
        if chan < refs[i].shape[0]:
            break
        chan -= refs[i].shape[0]
    return refs[i].at[chan]


def cross_kernel(layout, jobs, *refs):
    groups, at = {}, 0
    for name, count in layout:
        groups[name] = refs[at : at + count]
        at += count
    (gain_ref,) = groups["gains"]
    mine = groups["mine"]
    chans, _, rows, _ = mine[0].shape
    bands = rows // 2
    odd = lax.rem(lax.axis_index("chan"), 2)
    rounds = {"one": 2 * odd, "mid": 1, "two": 2 - 2 * odd, "far": 3}
    step = 2
    copies = []

    def send(source, ref, a_start, count):
        (out_ref,), (sems,) = groups["out"], groups["sems"]
        part = pl.ds(a_start, count)
        copy = pltpu.make_async_copy(
            ref.at[part], out_ref.at[rounds[source], part], sems.at[len(copies)]
        )
        copy.start()
        copies.append(copy)

    for source, ref in zip(("far", "mid", "one"), groups["done"]):
        send(source, ref, 0, chans)
    for source, pieces, acc_in, final, to in jobs:
        rnd = rounds[source]
        to_ref = groups["buffer"][0] if to is None else groups["acc_out"][to]
        for a_start in range(0, chans, step):
            a_list = range(a_start, min(a_start + step, chans))
            for c_start in range(0, chans, step):
                c_list = range(c_start, min(c_start + step, chans))
                ours = [[mine[piece].at[a] for a in a_list] for piece, _ in pieces]
                theirs = [[channel(groups[source], ref, c) for c in c_list] for _, ref in pieces]
                order = [(a, c, i) for a in a_list for c in c_list for i in range(2)]
                if acc_in is None:
                    acc = tuple(jnp.zeros((bands, LANES), jnp.float32) for _ in order)
                else:
                    ref = groups["acc_in"][acc_in]
                    acc = tuple(ref[a, c, pl.ds(i * bands, bands), :] for a, c, i in order)
                acc = cross_unit(ours, theirs, acc)
                for (a, c, i), value in zip(order, acc):
                    if not final:
                        to_ref[a, c, pl.ds(i * bands, bands), :] = value
                        continue
                    gain = gain_ref[pl.ds((rnd * chans + a) * chans + c, 1), :]
                    to_ref[a, c, pl.ds(i, bands, stride=2), :] = value * gain
            if to is None:
                send(source, to_ref, a_start, len(a_list))
    for copy in copies:
        copy.wait()


def cross_call(name, jobs, gains, mine, sources, acc_in=(), done=()):
    chans, _, rows, _ = mine[0].shape
    groups = [("gains", [gains]), ("mine", mine), *sources.items()]
    groups += [("acc_in", acc_in), ("done", done)]
    groups = [(key, list(arrays)) for key, arrays in groups]
    operands = [array for _, arrays in groups for array in arrays]
    layout = [(key, len(arrays)) for key, arrays in groups]
    sums = jax.ShapeDtypeStruct((chans, chans, rows, LANES), jnp.float32)
    whole = jax.ShapeDtypeStruct((ROUNDS,) + sums.shape, jnp.float32)
    acc_count = sum(job[4] is not None for job in jobs)
    ends = 1 - acc_count // len(jobs)
    layout += [("out", ends), ("acc_out", acc_count), ("buffer", ends), ("sems", ends)]
    scratch = [pltpu.VMEM(sums.shape, jnp.float32), pltpu.SemaphoreType.DMA((chans + len(done),))]
    return pl.pallas_call(
        functools.partial(cross_kernel, layout, jobs),
        in_specs=[VMEM] * len(operands),
        out_specs=[HBM] * ends + [VMEM] * acc_count,
        out_shape=[whole] * ends + [sums] * acc_count,
        scratch_shapes=scratch * ends,
        compiler_params=PARAMS,
        cost_estimate=cost({"cross_mid": 30.0}.get(name, 0.6)),
        name=name,
    )(*operands)


def choose(bit, own, far, count=None):
    count = count or far.shape[0]

    def kernel(own_ref, far_ref, out_ref):
        yes = lax.rem(lax.div(lax.axis_index("chan"), bit), 2) == 1

        @pl.when(yes)
        def _():
            out_ref[...] = own_ref[pl.ds(0, count)]

        @pl.when(jnp.logical_not(yes))
        def _():
            out_ref[...] = far_ref[pl.ds(0, count)]

    return pl.pallas_call(
        kernel,
        in_specs=[VMEM] * 2,
        out_specs=VMEM,
        out_shape=jax.ShapeDtypeStruct((count,) + far.shape[1:], far.dtype),
        compiler_params=PARAMS,
        cost_estimate=cost(0.1),
        name="choose",
    )(own, far)


def after(value, *others):
    return lax.optimization_barrier((value, *others))[0]


def shards(records, positions):
    parts = lax.axis_size("win")
    blocks = lax.axis_size("chan")
    chans, wins, _ = records.shape
    spectra = whitened_spectra(records, parts)
    up = [(b, b - 4) for b in range(4, blocks)]
    swap2 = [(b, b ^ 2) for b in range(blocks)]
    swap1 = [(b, b ^ 1) for b in range(blocks)]
    mine = [spectra[0]]
    for s in range(1, parts):
        mine.append(lax.ppermute(spectra[s], "win", [(i, (i + s) % parts) for i in range(parts)]))
    far = [lax.ppermute(own, "chan", up) for own in mine]
    last = parts - 1
    early = range(last)
    gains = stack_gains(after(positions, far[0]), chans, parts * wins)
    call = functools.partial(cross_call, gains=gains, mine=mine)

    (acc_far,) = call(
        "cross_far", [("far", [(s, s) for s in early], None, False, 0)], sources={"far": far[:-1]}
    )
    far[last] = after(far[last], acc_far)
    mid, one, two = [], [], []
    half = chans // 2
    direct = lax.ppermute(mine[last][half:], "chan", [(b, b - 2) for b in range(2, blocks)])
    for s in range(parts):
        count = None if s < last else half
        mid.append(lax.ppermute(choose(2, mine[s], far[s], count), "chan", swap2))
        one.append(lax.ppermute(choose(1, mine[s], far[s]), "chan", swap1))
        if s < last:
            two.append(lax.ppermute(mid[s], "chan", swap1))
    done_far, acc_mid = call(
        "cross_most",
        [
            ("far", [(last, 0)], 0, True, 0),
            ("mid", [(s, s) for s in early], None, False, 1),
        ],
        sources={"far": far[last:], "mid": mid[:last]},
        acc_in=[acc_far],
    )
    direct = after(direct, acc_mid)
    two_direct = lax.ppermute(direct, "chan", swap1)
    mid[last] = after(mid[last], acc_mid)
    two.append(lax.ppermute(mid[last], "chan", swap1))
    (done_mid,) = call(
        "cross_mid", [("mid", [(last, (0, 1))], 0, True, 0)],
        sources={"mid": [mid[last], direct]}, acc_in=[acc_mid],
    )
    one[last] = after(one[last], done_mid)
    two[0] = after(two[0], done_mid)
    done_one, acc_two = call(
        "cross_next",
        [
            ("one", [(s, s) for s in range(parts)], None, True, 0),
            ("two", [(s, s) for s in early], None, False, 1),
        ],
        sources={"one": one, "two": two[:last]},
    )
    two[last] = after(two[last], acc_two)
    (out,) = call(
        "cross_last", [("two", [(last, (0, 1))], 0, True, None)],
        sources={"two": [two[last], two_direct]},
        acc_in=[acc_two], done=[done_far, done_mid, done_one],
    )
    bands = out.shape[3] // 2
    out = out.reshape(ROUNDS, chans, chans, bands, 2, LANES).transpose(0, 1, 2, 4, 3, 5)
    return out.reshape(ROUNDS, chans, chans, 2, bands * LANES)


def solution(mesh):
    return jax.shard_map(
        shards,
        mesh=mesh,
        in_specs=(P("chan", "win", None), P()),
        out_specs=P(None, "chan", None, None, "win"),
        check_vma=False,
    )
```

```python
import functools
import math

import jax
import jax.numpy as jnp
from jax import lax
from jax.experimental import pallas as pl
from jax.experimental.pallas import tpu as pltpu
from jax.sharding import PartitionSpec as P

BINS = 4096
BAND = 128
ROUNDS = 4
REACH = 2000
LANES = 128
band_epsilon = 1e-06
VMEM = pl.BlockSpec(memory_space=pltpu.VMEM)
SMEM = pl.BlockSpec(memory_space=pltpu.SMEM)
HBM = pl.BlockSpec(memory_space=pltpu.HBM)
PARAMS = pltpu.CompilerParams(vmem_limit_bytes=40 * 1024 * 1024)


def cost(microseconds):
    return pl.CostEstimate(flops=int(microseconds * 1.1e9), bytes_accessed=0, transcendentals=0)


def split3(value):
    hi = value.astype(jnp.bfloat16)
    rest = value - hi.astype(jnp.float32)
    mid = rest.astype(jnp.bfloat16)
    lo = (rest - mid.astype(jnp.float32)).astype(jnp.bfloat16)
    return hi, mid, lo


def real_dft(values):
    n = len(values)
    if n == 2:
        return [(values[0] + values[1], None), (values[0] - values[1], None)]
    even, odd = real_dft(values[0::2]), real_dft(values[1::2])
    out = [None] * (n // 2 + 1)
    for k in range(n // 4 + 1):
        (er, ei), (dr, di) = even[k], odd[k]
        if k == 0:
            out[0] = (er + dr, None)
            out[n // 2] = (er - dr, None)
        elif 4 * k == n:
            out[k] = (er, -dr)
        else:
            c, s = math.cos(2.0 * math.pi * k / n), math.sin(2.0 * math.pi * k / n)
            tr = dr * c + di * s
            ti = di * c - dr * s
            out[k] = (er + tr, ei + ti)
            out[n // 2 - k] = (er - tr, ti - ei)
    return out


def spectra_channel(parts, chan, x, tables, t_ref, outs):
    tw_ref, main_ref, side_ref, bands_ref, pick_ref = tables
    first = len(x)
    wins = x[0].shape[0]
    bands = BINS // BAND // parts
    terms = real_dft(x)
    rows = []
    for k in range(first):
        re, im = terms[min(k, first - k)]
        cos, sin = tw_ref[0, pl.ds(k, 1), :], tw_ref[1, pl.ds(k, 1), :]
        if im is None:
            row = [re * cos, -(re * sin)]
        elif 2 * k <= first:
            row = [re * cos + im * sin, im * cos - re * sin]
        else:
            row = [re * cos - im * sin, -(im * cos + re * sin)]
        rows.append(jnp.concatenate(row, axis=1))
    hi, mid, lo = split3(jnp.concatenate(rows, axis=0))
    main = jnp.dot(
        jnp.concatenate([hi, mid], axis=1), main_ref[...], preferred_element_type=jnp.float32
    )
    side = jnp.dot(
        jnp.concatenate([hi, lo], axis=1), side_ref[...], preferred_element_type=jnp.float32
    )
    spec = (main[:, :LANES] + main[:, LANES:] + side).reshape(first, wins, LANES)
    total = jnp.dot(
        jnp.concatenate(split3(jnp.sum(spec * spec, axis=0)), axis=1),
        bands_ref[...],
        preferred_element_type=jnp.float32,
    )
    scale = lax.rsqrt(total * (1.0 / BAND) + band_epsilon)
    t_ref[chan] = (spec * scale).reshape(first * wins, LANES)
    white = jnp.concatenate(
        [t_ref[chan, pl.ds(win, first, stride=wins), :].astype(jnp.bfloat16) for win in range(wins)],
        axis=0,
    )
    spread = lax.dot_general(
        pick_ref[...], white, (((1,), (1,)), ((), ())), preferred_element_type=jnp.float32
    )
    left = lax.broadcasted_iota(jnp.int32, (bands, LANES), 1) < first
    for pair in range(wins // 2):
        tile = spread[:, pair * LANES : (pair + 1) * LANES].reshape(parts, 2, 2, bands, LANES)
        for s in range(parts):
            for imag in range(2):
                even, odd = tile[s, imag, 0], tile[s, imag, 1]
                one = jnp.where(left, even, pltpu.roll(odd, first, 1)).astype(jnp.bfloat16)
                two = jnp.where(left, pltpu.roll(even, first, 1), odd).astype(jnp.bfloat16)
                at = pl.ds(imag * bands, bands)
                outs[s][chan, 2 * pair, at, :] = one
                outs[s][chan, 2 * pair + 1, at, :] = two


def turn_table(index, period):
    index = lax.rem(index, period)
    quarter = period // 4
    turn = lax.div(index + quarter // 2, quarter)
    angle = (index - turn * quarter).astype(jnp.float32) * (2.0 * math.pi / period)
    square = angle * angle

    def series(first):
        value = jnp.full_like(angle, 0.0)
        for power in range(10 + first, first - 1, -2):
            value = value * square + (-1) ** (power // 2) / math.factorial(power)
        return value

    cos, sin = series(0), series(1) * angle
    swap = lax.rem(turn, 2) == 1
    minus_cos = (turn == 1) | (turn == 2)
    minus_sin = (turn == 2) | (turn == 3)
    cos, sin = jnp.where(swap, sin, cos), jnp.where(swap, cos, sin)
    return jnp.where(minus_cos, -cos, cos), jnp.where(minus_sin, -sin, sin)


def gains_kernel(chans, inv_root, pos_ref, gain_ref):
    block = lax.axis_index("chan")
    last = pos_ref.shape[0] - 1
    for row in range(ROUNDS * chans * chans):
        rnd, a, c = row // (chans * chans), row // chans % chans, row % chans
        pos_c = pos_ref[lax.min((block + rnd + 1) * chans + c, last)]
        near = pos_c - pos_ref[block * chans + a] <= REACH
        gain = jnp.where(near, inv_root, 0.0).astype(jnp.float32)
        gain_ref[pl.ds(row, 1), :] = jnp.full((1, LANES), gain)


def stack_gains(positions, chans, windows):
    return pl.pallas_call(
        functools.partial(gains_kernel, chans, 1.0 / math.sqrt(windows)),
        in_specs=[SMEM],
        out_specs=VMEM,
        out_shape=jax.ShapeDtypeStruct((ROUNDS * chans * chans, LANES), jnp.float32),
        compiler_params=PARAMS,
        cost_estimate=cost(0.5),
        name="gains",
    )(positions)


def tables_kernel(parts, samples, tw_ref, main_ref, side_ref, bands_ref, pick_ref):
    first = samples // LANES
    bands = BINS // BAND // parts
    me = lax.axis_index("win")
    k1 = lax.broadcasted_iota(jnp.int32, (first, LANES), 0)
    q = lax.broadcasted_iota(jnp.int32, (first, LANES), 1)
    tw_ref[0], tw_ref[1] = turn_table(k1 * q, samples)
    row = lax.broadcasted_iota(jnp.int32, (LANES, LANES), 0)
    lane = lax.broadcasted_iota(jnp.int32, (LANES, LANES), 1)
    real = lane < first
    m = lax.rem(lane, first)
    cos, sin = turn_table(row * m, LANES)
    table = jnp.concatenate([jnp.where(real, cos, -sin), jnp.where(real, sin, cos)], axis=0)
    hi, mid, lo = split3(table)
    wide = jnp.concatenate([hi, mid], axis=1)
    main_ref[...] = jnp.concatenate([wide, wide], axis=0)
    side_ref[...] = jnp.concatenate([lo, hi], axis=0)
    same = lax.div(lax.rem(row, first), 2) == lax.div(m, 2)
    bands_ref[...] = jnp.concatenate([same.astype(jnp.float32)] * 3, axis=0).astype(jnp.bfloat16)
    part = lax.rem(me + lax.div(row, 4 * bands), parts)
    imag = lax.rem(lax.div(row, 2 * bands), 2)
    odd = lax.rem(lax.div(row, bands), 2)
    source = imag * first + 2 * (part * bands + lax.rem(row, bands)) + odd
    pick_ref[...] = (lane == source).astype(jnp.float32).astype(jnp.bfloat16)


def spectra_kernel(parts, x_ref, *refs):
    tables, outs, t_ref = refs[:5], refs[5:-1], refs[-1]
    chans, first = x_ref.shape[:2]
    for chan in range(chans):
        x = [x_ref[chan, p] for p in range(first)]
        spectra_channel(parts, chan, x, tables, t_ref, outs)


def whitened_spectra(records, parts):
    chans, wins, samples = records.shape
    first = samples // LANES
    rows = 2 * (BINS // BAND // parts)
    x = records.reshape(chans, wins, first, LANES).transpose(0, 2, 1, 3)
    tables = pl.pallas_call(
        functools.partial(tables_kernel, parts, samples),
        out_specs=[VMEM] * 5,
        out_shape=[
            jax.ShapeDtypeStruct((2, first, LANES), jnp.float32),
            jax.ShapeDtypeStruct((4 * LANES, 2 * LANES), jnp.bfloat16),
            jax.ShapeDtypeStruct((4 * LANES, LANES), jnp.bfloat16),
            jax.ShapeDtypeStruct((3 * LANES, LANES), jnp.bfloat16),
            jax.ShapeDtypeStruct((LANES, LANES), jnp.bfloat16),
        ],
        compiler_params=PARAMS,
        cost_estimate=cost(1),
        name="tables",
    )()
    return pl.pallas_call(
        functools.partial(spectra_kernel, parts),
        in_specs=[VMEM] * 6,
        out_specs=[VMEM] * parts,
        out_shape=[jax.ShapeDtypeStruct((chans, wins, rows, LANES), jnp.bfloat16)] * parts,
        scratch_shapes=[pltpu.VMEM((chans, first * wins, LANES), jnp.float32)],
        compiler_params=PARAMS,
        cost_estimate=cost(4),
        name="spectra",
    )(x, *tables)


def cross_unit(mine, theirs, acc):
    rows = mine[0][0].shape[1]
    bands = rows // 2
    wins = mine[0][0].shape[0]
    per_step = wins if wins <= 8 else 1

    def planes(ref, win):
        return [ref[win, pl.ds(i * bands, bands), :].astype(jnp.float32) for i in range(2)]

    for own, their in zip(mine, theirs):

        def step(index, acc, own=own, their=their):
            acc = list(acc)
            for i in range(per_step):
                win = index * per_step + i
                ours = [planes(ref, win) for ref in own]
                for c, ref in enumerate(their):
                    cr, ci = planes(ref, win)
                    for a, (ar, ai) in enumerate(ours):
                        at = 2 * (a * len(their) + c)
                        acc[at] = acc[at] + ar * cr + ai * ci
                        acc[at + 1] = acc[at + 1] + ai * cr - ar * ci
            return tuple(acc)

        acc = lax.fori_loop(0, wins // per_step, step, acc)
    return acc


def cross_kernel(layout, jobs, *refs):
    groups, at = {}, 0
    for name, count in layout:
        groups[name] = refs[at : at + count]
        at += count
    (gain_ref,) = groups["gains"]
    mine = groups["mine"]
    chans, _, rows, _ = mine[0].shape
    bands = rows // 2
    odd = lax.rem(lax.axis_index("chan"), 2)
    rounds = {"one": 2 * odd, "mid": 1, "two": 2 - 2 * odd, "far": 3}
    step = 2
    copies = []

    def send(source, ref, a_start, count):
        (out_ref,), (sems,) = groups["out"], groups["sems"]
        part = pl.ds(a_start, count)
        copy = pltpu.make_async_copy(
            ref.at[part], out_ref.at[rounds[source], part], sems.at[len(copies)]
        )
        copy.start()
        copies.append(copy)

    for source, ref in zip(("far", "mid", "one"), groups["done"]):
        send(source, ref, 0, chans)
    for source, pieces, acc_in, final, to in jobs:
        rnd = rounds[source]
        to_ref = groups["buffer"][0] if to is None else groups["acc_out"][to]
        for a_start in range(0, chans, step):
            a_list = range(a_start, min(a_start + step, chans))
            for c_start in range(0, chans, step):
                c_list = range(c_start, min(c_start + step, chans))
                ours = [[mine[piece].at[a] for a in a_list] for piece, _ in pieces]
                theirs = [[groups[source][ref].at[c] for c in c_list] for _, ref in pieces]
                order = [(a, c, i) for a in a_list for c in c_list for i in range(2)]
                if acc_in is None:
                    acc = tuple(jnp.zeros((bands, LANES), jnp.float32) for _ in order)
                else:
                    ref = groups["acc_in"][acc_in]
                    acc = tuple(ref[a, c, pl.ds(i * bands, bands), :] for a, c, i in order)
                acc = cross_unit(ours, theirs, acc)
                for (a, c, i), value in zip(order, acc):
                    if not final:
                        to_ref[a, c, pl.ds(i * bands, bands), :] = value
                        continue
                    gain = gain_ref[pl.ds((rnd * chans + a) * chans + c, 1), :]
                    to_ref[a, c, pl.ds(i, bands, stride=2), :] = value * gain
            if to is None:
                send(source, to_ref, a_start, len(a_list))
    for copy in copies:
        copy.wait()


def cross_call(name, jobs, gains, mine, sources, acc_in=(), done=()):
    chans, _, rows, _ = mine[0].shape
    groups = [("gains", [gains]), ("mine", mine), *sources.items()]
    groups += [("acc_in", acc_in), ("done", done)]
    groups = [(key, list(arrays)) for key, arrays in groups]
    operands = [array for _, arrays in groups for array in arrays]
    layout = [(key, len(arrays)) for key, arrays in groups]
    sums = jax.ShapeDtypeStruct((chans, chans, rows, LANES), jnp.float32)
    whole = jax.ShapeDtypeStruct((ROUNDS,) + sums.shape, jnp.float32)
    acc_count = sum(job[4] is not None for job in jobs)
    ends = 1 - acc_count // len(jobs)
    layout += [("out", ends), ("acc_out", acc_count), ("buffer", ends), ("sems", ends)]
    scratch = [pltpu.VMEM(sums.shape, jnp.float32), pltpu.SemaphoreType.DMA((chans + len(done),))]
    return pl.pallas_call(
        functools.partial(cross_kernel, layout, jobs),
        in_specs=[VMEM] * len(operands),
        out_specs=[HBM] * ends + [VMEM] * acc_count,
        out_shape=[whole] * ends + [sums] * acc_count,
        scratch_shapes=scratch * ends,
        compiler_params=PARAMS,
        cost_estimate=cost({"cross_mid": 30.0}.get(name, 0.6)),
        name=name,
    )(*operands)


def choose(bit, own, far, count=None):
    count = count or far.shape[0]

    def kernel(own_ref, far_ref, out_ref):
        yes = lax.rem(lax.div(lax.axis_index("chan"), bit), 2) == 1

        @pl.when(yes)
        def _():
            out_ref[...] = own_ref[pl.ds(0, count)]

        @pl.when(jnp.logical_not(yes))
        def _():
            out_ref[...] = far_ref[pl.ds(0, count)]

    return pl.pallas_call(
        kernel,
        in_specs=[VMEM] * 2,
        out_specs=VMEM,
        out_shape=jax.ShapeDtypeStruct((count,) + far.shape[1:], far.dtype),
        compiler_params=PARAMS,
        cost_estimate=cost(0.1),
        name="choose",
    )(own, far)


def join(estimate, *arrays):
    def kernel(*refs):
        start = 0
        for ref in refs[:-1]:
            refs[-1][pl.ds(start, ref.shape[0])] = ref[...]
            start += ref.shape[0]

    shape = (sum(array.shape[0] for array in arrays),) + arrays[0].shape[1:]
    return pl.pallas_call(
        kernel,
        in_specs=[VMEM] * len(arrays),
        out_specs=VMEM,
        out_shape=jax.ShapeDtypeStruct(shape, arrays[0].dtype),
        compiler_params=PARAMS,
        cost_estimate=cost(estimate),
        name="join",
    )(*arrays)


def after(value, *others):
    return lax.optimization_barrier((value, *others))[0]


def shards(records, positions):
    parts = lax.axis_size("win")
    blocks = lax.axis_size("chan")
    chans, wins, _ = records.shape
    spectra = whitened_spectra(records, parts)
    up = [(b, b - 4) for b in range(4, blocks)]
    swap2 = [(b, b ^ 2) for b in range(blocks)]
    swap1 = [(b, b ^ 1) for b in range(blocks)]
    mine = [spectra[0]]
    for s in range(1, parts):
        mine.append(lax.ppermute(spectra[s], "win", [(i, (i + s) % parts) for i in range(parts)]))
    far = [lax.ppermute(own, "chan", up) for own in mine]
    last = parts - 1
    early = range(last)
    gains = stack_gains(after(positions, far[0]), chans, parts * wins)
    call = functools.partial(cross_call, gains=gains, mine=mine)

    (acc_far,) = call(
        "cross_far", [("far", [(s, s) for s in early], None, False, 0)], sources={"far": far[:-1]}
    )
    far[last] = after(far[last], acc_far)
    mid, one, two = [], [], []
    half = chans // 2
    direct = lax.ppermute(mine[last][half:], "chan", [(b, b - 2) for b in range(2, blocks)])
    for s in range(parts):
        count = None if s < last else half
        mid.append(lax.ppermute(choose(2, mine[s], far[s], count), "chan", swap2))
        one.append(lax.ppermute(choose(1, mine[s], far[s]), "chan", swap1))
        if s < last:
            two.append(lax.ppermute(mid[s], "chan", swap1))
    done_far, acc_mid = call(
        "cross_most",
        [
            ("far", [(last, 0)], 0, True, 0),
            ("mid", [(s, s) for s in early], None, False, 1),
        ],
        sources={"far": far[last:], "mid": mid[:last]},
        acc_in=[acc_far],
    )
    direct = join(0.1, after(direct, acc_mid))
    mid[last] = join(0.1, after(mid[last], direct), direct)
    two.append(lax.ppermute(mid[last], "chan", swap1))
    (done_mid,) = call(
        "cross_mid", [("mid", [(last, 0)], 0, True, 0)],
        sources={"mid": mid[last:]}, acc_in=[acc_mid],
    )
    one[last] = after(one[last], done_mid)
    two[0] = after(two[0], done_mid)
    done_one, acc_two = call(
        "cross_next",
        [
            ("one", [(s, s) for s in range(parts)], None, True, 0),
            ("two", [(s, s) for s in early], None, False, 1),
        ],
        sources={"one": one, "two": two[:last]},
    )
    two[last] = after(two[last], acc_two)
    (out,) = call(
        "cross_last", [("two", [(last, 0)], 0, True, None)], sources={"two": two[last:]},
        acc_in=[acc_two], done=[done_far, done_mid, done_one],
    )
    bands = out.shape[3] // 2
    out = out.reshape(ROUNDS, chans, chans, bands, 2, LANES).transpose(0, 1, 2, 4, 3, 5)
    return out.reshape(ROUNDS, chans, chans, 2, bands * LANES)


def solution(mesh):
    return jax.shard_map(
        shards,
        mesh=mesh,
        in_specs=(P("chan", "win", None), P()),
        out_specs=P(None, "chan", None, None, "win"),
        check_vma=False,
    )
```

```python
import functools
import math

import jax
import jax.numpy as jnp
from jax import lax
from jax.experimental import pallas as pl
from jax.experimental.pallas import tpu as pltpu
from jax.sharding import PartitionSpec as P

BINS = 4096
BAND = 128
ROUNDS = 4
REACH = 2000
LANES = 128
band_epsilon = 1e-06
VMEM = pl.BlockSpec(memory_space=pltpu.VMEM)
SMEM = pl.BlockSpec(memory_space=pltpu.SMEM)
HBM = pl.BlockSpec(memory_space=pltpu.HBM)
PARAMS = pltpu.CompilerParams(vmem_limit_bytes=40 * 1024 * 1024)


def cost(microseconds):
    return pl.CostEstimate(flops=int(microseconds * 1.1e9), bytes_accessed=0, transcendentals=0)


def split3(value):
    hi = value.astype(jnp.bfloat16)
    rest = value - hi.astype(jnp.float32)
    mid = rest.astype(jnp.bfloat16)
    lo = (rest - mid.astype(jnp.float32)).astype(jnp.bfloat16)
    return hi, mid, lo


def real_dft(values):
    n = len(values)
    if n == 2:
        return [(values[0] + values[1], None), (values[0] - values[1], None)]
    even, odd = real_dft(values[0::2]), real_dft(values[1::2])
    out = [None] * (n // 2 + 1)
    for k in range(n // 4 + 1):
        (er, ei), (dr, di) = even[k], odd[k]
        if k == 0:
            out[0] = (er + dr, None)
            out[n // 2] = (er - dr, None)
        elif 4 * k == n:
            out[k] = (er, -dr)
        else:
            c, s = math.cos(2.0 * math.pi * k / n), math.sin(2.0 * math.pi * k / n)
            tr = dr * c + di * s
            ti = di * c - dr * s
            out[k] = (er + tr, ei + ti)
            out[n // 2 - k] = (er - tr, ti - ei)
    return out


def spectra_channel(parts, chan, x, tables, t_ref, outs):
    tw_ref, main_ref, side_ref, bands_ref, pick_ref = tables
    first = len(x)
    wins = x[0].shape[0]
    bands = BINS // BAND // parts
    terms = real_dft(x)
    rows = []
    for k in range(first):
        re, im = terms[min(k, first - k)]
        cos, sin = tw_ref[0, pl.ds(k, 1), :], tw_ref[1, pl.ds(k, 1), :]
        if im is None:
            row = [re * cos, -(re * sin)]
        elif 2 * k <= first:
            row = [re * cos + im * sin, im * cos - re * sin]
        else:
            row = [re * cos - im * sin, -(im * cos + re * sin)]
        rows.append(jnp.concatenate(row, axis=1))
    hi, mid, lo = split3(jnp.concatenate(rows, axis=0))
    main = jnp.dot(
        jnp.concatenate([hi, mid], axis=1), main_ref[...], preferred_element_type=jnp.float32
    )
    side = jnp.dot(
        jnp.concatenate([hi, lo], axis=1), side_ref[...], preferred_element_type=jnp.float32
    )
    spec = (main[:, :LANES] + main[:, LANES:] + side).reshape(first, wins, LANES)
    total = jnp.dot(
        jnp.concatenate(split3(jnp.sum(spec * spec, axis=0)), axis=1),
        bands_ref[...],
        preferred_element_type=jnp.float32,
    )
    scale = lax.rsqrt(total * (1.0 / BAND) + band_epsilon)
    t_ref[chan] = (spec * scale).reshape(first * wins, LANES)
    white = jnp.concatenate(
        [t_ref[chan, pl.ds(win, first, stride=wins), :].astype(jnp.bfloat16) for win in range(wins)],
        axis=0,
    )
    spread = lax.dot_general(
        pick_ref[...], white, (((1,), (1,)), ((), ())), preferred_element_type=jnp.float32
    )
    left = lax.broadcasted_iota(jnp.int32, (bands, LANES), 1) < first
    for pair in range(wins // 2):
        tile = spread[:, pair * LANES : (pair + 1) * LANES].reshape(parts, 2, 2, bands, LANES)
        for s in range(parts):
            for imag in range(2):
                even, odd = tile[s, imag, 0], tile[s, imag, 1]
                one = jnp.where(left, even, pltpu.roll(odd, first, 1)).astype(jnp.bfloat16)
                two = jnp.where(left, pltpu.roll(even, first, 1), odd).astype(jnp.bfloat16)
                at = pl.ds(imag * bands, bands)
                outs[s][chan, 2 * pair, at, :] = one
                outs[s][chan, 2 * pair + 1, at, :] = two


def turn_table(index, period):
    index = lax.rem(index, period)
    quarter = period // 4
    turn = lax.div(index + quarter // 2, quarter)
    angle = (index - turn * quarter).astype(jnp.float32) * (2.0 * math.pi / period)
    square = angle * angle

    def series(first):
        value = jnp.full_like(angle, 0.0)
        for power in range(10 + first, first - 1, -2):
            value = value * square + (-1) ** (power // 2) / math.factorial(power)
        return value

    cos, sin = series(0), series(1) * angle
    swap = lax.rem(turn, 2) == 1
    minus_cos = (turn == 1) | (turn == 2)
    minus_sin = (turn == 2) | (turn == 3)
    cos, sin = jnp.where(swap, sin, cos), jnp.where(swap, cos, sin)
    return jnp.where(minus_cos, -cos, cos), jnp.where(minus_sin, -sin, sin)


def gains_kernel(chans, inv_root, pos_ref, gain_ref):
    block = lax.axis_index("chan")
    last = pos_ref.shape[0] - 1
    for row in range(ROUNDS * chans * chans):
        rnd, a, c = row // (chans * chans), row // chans % chans, row % chans
        pos_c = pos_ref[lax.min((block + rnd + 1) * chans + c, last)]
        near = pos_c - pos_ref[block * chans + a] <= REACH
        gain = jnp.where(near, inv_root, 0.0).astype(jnp.float32)
        gain_ref[pl.ds(row, 1), :] = jnp.full((1, LANES), gain)


def stack_gains(positions, chans, windows):
    return pl.pallas_call(
        functools.partial(gains_kernel, chans, 1.0 / math.sqrt(windows)),
        in_specs=[SMEM],
        out_specs=VMEM,
        out_shape=jax.ShapeDtypeStruct((ROUNDS * chans * chans, LANES), jnp.float32),
        compiler_params=PARAMS,
        cost_estimate=cost(0.5),
        name="gains",
    )(positions)


def tables_kernel(parts, samples, tw_ref, main_ref, side_ref, bands_ref, pick_ref):
    first = samples // LANES
    bands = BINS // BAND // parts
    me = lax.axis_index("win")
    k1 = lax.broadcasted_iota(jnp.int32, (first, LANES), 0)
    q = lax.broadcasted_iota(jnp.int32, (first, LANES), 1)
    tw_ref[0], tw_ref[1] = turn_table(k1 * q, samples)
    row = lax.broadcasted_iota(jnp.int32, (LANES, LANES), 0)
    lane = lax.broadcasted_iota(jnp.int32, (LANES, LANES), 1)
    real = lane < first
    m = lax.rem(lane, first)
    cos, sin = turn_table(row * m, LANES)
    table = jnp.concatenate([jnp.where(real, cos, -sin), jnp.where(real, sin, cos)], axis=0)
    hi, mid, lo = split3(table)
    wide = jnp.concatenate([hi, mid], axis=1)
    main_ref[...] = jnp.concatenate([wide, wide], axis=0)
    side_ref[...] = jnp.concatenate([lo, hi], axis=0)
    same = lax.div(lax.rem(row, first), 2) == lax.div(m, 2)
    bands_ref[...] = jnp.concatenate([same.astype(jnp.float32)] * 3, axis=0).astype(jnp.bfloat16)
    part = lax.rem(me + lax.div(row, 4 * bands), parts)
    imag = lax.rem(lax.div(row, 2 * bands), 2)
    odd = lax.rem(lax.div(row, bands), 2)
    source = imag * first + 2 * (part * bands + lax.rem(row, bands)) + odd
    pick_ref[...] = (lane == source).astype(jnp.float32).astype(jnp.bfloat16)


def spectra_kernel(parts, x_ref, *refs):
    tables, outs, t_ref = refs[:5], refs[5:-1], refs[-1]
    chans, first = x_ref.shape[:2]
    for chan in range(chans):
        x = [x_ref[chan, p] for p in range(first)]
        spectra_channel(parts, chan, x, tables, t_ref, outs)


def whitened_spectra(records, parts):
    chans, wins, samples = records.shape
    first = samples // LANES
    rows = 2 * (BINS // BAND // parts)
    x = records.reshape(chans, wins, first, LANES).transpose(0, 2, 1, 3)
    tables = pl.pallas_call(
        functools.partial(tables_kernel, parts, samples),
        out_specs=[VMEM] * 5,
        out_shape=[
            jax.ShapeDtypeStruct((2, first, LANES), jnp.float32),
            jax.ShapeDtypeStruct((4 * LANES, 2 * LANES), jnp.bfloat16),
            jax.ShapeDtypeStruct((4 * LANES, LANES), jnp.bfloat16),
            jax.ShapeDtypeStruct((3 * LANES, LANES), jnp.bfloat16),
            jax.ShapeDtypeStruct((LANES, LANES), jnp.bfloat16),
        ],
        compiler_params=PARAMS,
        cost_estimate=cost(1),
        name="tables",
    )()
    return pl.pallas_call(
        functools.partial(spectra_kernel, parts),
        in_specs=[VMEM] * 6,
        out_specs=[VMEM] * parts,
        out_shape=[jax.ShapeDtypeStruct((chans, wins, rows, LANES), jnp.bfloat16)] * parts,
        scratch_shapes=[pltpu.VMEM((chans, first * wins, LANES), jnp.float32)],
        compiler_params=PARAMS,
        cost_estimate=cost(4),
        name="spectra",
    )(x, *tables)


def cross_unit(mine, theirs, acc):
    rows = mine[0][0].shape[1]
    bands = rows // 2
    wins = mine[0][0].shape[0]
    per_step = wins if wins <= 8 else 1

    def planes(ref, win):
        return [ref[win, pl.ds(i * bands, bands), :].astype(jnp.float32) for i in range(2)]

    for own, their in zip(mine, theirs):

        def step(index, acc, own=own, their=their):
            acc = list(acc)
            for i in range(per_step):
                win = index * per_step + i
                ours = [planes(ref, win) for ref in own]
                for c, ref in enumerate(their):
                    cr, ci = planes(ref, win)
                    for a, (ar, ai) in enumerate(ours):
                        at = 2 * (a * len(their) + c)
                        acc[at] = acc[at] + ar * cr + ai * ci
                        acc[at + 1] = acc[at + 1] + ai * cr - ar * ci
            return tuple(acc)

        acc = lax.fori_loop(0, wins // per_step, step, acc)
    return acc


def cross_kernel(layout, jobs, *refs):
    groups, at = {}, 0
    for name, count in layout:
        groups[name] = refs[at : at + count]
        at += count
    (gain_ref,) = groups["gains"]
    mine = groups["mine"]
    chans, _, rows, _ = mine[0].shape
    bands = rows // 2
    odd = lax.rem(lax.axis_index("chan"), 2)
    rounds = {"one": 2 * odd, "mid": 1, "two": 2 - 2 * odd, "far": 3}
    step = 2
    copies = []

    def send(source, ref, a_start, count):
        (out_ref,), (sems,) = groups["out"], groups["sems"]
        part = pl.ds(a_start, count)
        copy = pltpu.make_async_copy(
            ref.at[part], out_ref.at[rounds[source], part], sems.at[len(copies)]
        )
        copy.start()
        copies.append(copy)

    for source, ref in zip(("far", "mid", "one"), groups["done"]):
        send(source, ref, 0, chans)
    for source, pieces, acc_in, final, to in jobs:
        rnd = rounds[source]
        to_ref = groups["buffer"][0] if to is None else groups["acc_out"][to]
        for a_start in range(0, chans, step):
            a_list = range(a_start, min(a_start + step, chans))
            for c_start in range(0, chans, step):
                c_list = range(c_start, min(c_start + step, chans))
                ours = [[mine[piece].at[a] for a in a_list] for piece, _ in pieces]
                theirs = [[groups[source][ref].at[c] for c in c_list] for _, ref in pieces]
                order = [(a, c, i) for a in a_list for c in c_list for i in range(2)]
                if acc_in is None:
                    acc = tuple(jnp.zeros((bands, LANES), jnp.float32) for _ in order)
                else:
                    ref = groups["acc_in"][acc_in]
                    acc = tuple(ref[a, c, pl.ds(i * bands, bands), :] for a, c, i in order)
                acc = cross_unit(ours, theirs, acc)
                for (a, c, i), value in zip(order, acc):
                    if not final:
                        to_ref[a, c, pl.ds(i * bands, bands), :] = value
                        continue
                    gain = gain_ref[pl.ds((rnd * chans + a) * chans + c, 1), :]
                    to_ref[a, c, pl.ds(i, bands, stride=2), :] = value * gain
            if to is None:
                send(source, to_ref, a_start, len(a_list))
    for copy in copies:
        copy.wait()


def cross_call(name, jobs, gains, mine, sources, acc_in=(), done=()):
    chans, _, rows, _ = mine[0].shape
    groups = [("gains", [gains]), ("mine", mine), *sources.items()]
    groups += [("acc_in", acc_in), ("done", done)]
    groups = [(key, list(arrays)) for key, arrays in groups]
    operands = [array for _, arrays in groups for array in arrays]
    layout = [(key, len(arrays)) for key, arrays in groups]
    sums = jax.ShapeDtypeStruct((chans, chans, rows, LANES), jnp.float32)
    whole = jax.ShapeDtypeStruct((ROUNDS,) + sums.shape, jnp.float32)
    acc_count = sum(job[4] is not None for job in jobs)
    ends = 1 - acc_count // len(jobs)
    layout += [("out", ends), ("acc_out", acc_count), ("buffer", ends), ("sems", ends)]
    scratch = [pltpu.VMEM(sums.shape, jnp.float32), pltpu.SemaphoreType.DMA((chans + len(done),))]
    return pl.pallas_call(
        functools.partial(cross_kernel, layout, jobs),
        in_specs=[VMEM] * len(operands),
        out_specs=[HBM] * ends + [VMEM] * acc_count,
        out_shape=[whole] * ends + [sums] * acc_count,
        scratch_shapes=scratch * ends,
        compiler_params=PARAMS,
        cost_estimate=cost({"cross_mid": 30.0}.get(name, 0.6)),
        name=name,
    )(*operands)


def choose(bit, own, far, count=None):
    count = count or far.shape[0]

    def kernel(own_ref, far_ref, out_ref):
        yes = lax.rem(lax.div(lax.axis_index("chan"), bit), 2) == 1

        @pl.when(yes)
        def _():
            out_ref[...] = own_ref[pl.ds(0, count)]

        @pl.when(jnp.logical_not(yes))
        def _():
            out_ref[...] = far_ref[pl.ds(0, count)]

    return pl.pallas_call(
        kernel,
        in_specs=[VMEM] * 2,
        out_specs=VMEM,
        out_shape=jax.ShapeDtypeStruct((count,) + far.shape[1:], far.dtype),
        compiler_params=PARAMS,
        cost_estimate=cost(0.1),
        name="choose",
    )(own, far)


def join(estimate, *arrays):
    def kernel(*refs):
        start = 0
        for ref in refs[:-1]:
            refs[-1][pl.ds(start, ref.shape[0])] = ref[...]
            start += ref.shape[0]

    shape = (sum(array.shape[0] for array in arrays),) + arrays[0].shape[1:]
    return pl.pallas_call(
        kernel,
        in_specs=[VMEM] * len(arrays),
        out_specs=VMEM,
        out_shape=jax.ShapeDtypeStruct(shape, arrays[0].dtype),
        compiler_params=PARAMS,
        cost_estimate=cost(estimate),
        name="join",
    )(*arrays)


def after(value, *others):
    return lax.optimization_barrier((value, *others))[0]


def shards(records, positions):
    parts = lax.axis_size("win")
    blocks = lax.axis_size("chan")
    chans, wins, _ = records.shape
    spectra = whitened_spectra(records, parts)
    up = [(b, b - 4) for b in range(4, blocks)]
    swap2 = [(b, b ^ 2) for b in range(blocks)]
    swap1 = [(b, b ^ 1) for b in range(blocks)]
    mine = [spectra[0]]
    for s in range(1, parts):
        mine.append(lax.ppermute(spectra[s], "win", [(i, (i + s) % parts) for i in range(parts)]))
    far = [lax.ppermute(own, "chan", up) for own in mine]
    last = parts - 1
    early = range(last)
    gains = stack_gains(after(positions, far[0]), chans, parts * wins)
    call = functools.partial(cross_call, gains=gains, mine=mine)

    (acc_far,) = call(
        "cross_far", [("far", [(s, s) for s in early], None, False, 0)], sources={"far": far[:-1]}
    )
    far[last] = after(far[last], acc_far)
    mid, one, two = [], [], []
    half = chans - chans // 4
    direct = lax.ppermute(mine[last][half:], "chan", [(b, b - 2) for b in range(2, blocks)])
    for s in range(parts):
        count = None if s < last else half
        mid.append(lax.ppermute(choose(2, mine[s], far[s], count), "chan", swap2))
        one.append(lax.ppermute(choose(1, mine[s], far[s]), "chan", swap1))
        if s < last:
            two.append(lax.ppermute(mid[s], "chan", swap1))
    done_far, acc_mid = call(
        "cross_most",
        [
            ("far", [(last, 0)], 0, True, 0),
            ("mid", [(s, s) for s in early], None, False, 1),
        ],
        sources={"far": far[last:], "mid": mid[:last]},
        acc_in=[acc_far],
    )
    direct = join(0.1, after(direct, acc_mid))
    mid[last] = join(0.1, after(mid[last], direct), direct)
    two.append(lax.ppermute(mid[last], "chan", swap1))
    (done_mid,) = call(
        "cross_mid", [("mid", [(last, 0)], 0, True, 0)],
        sources={"mid": mid[last:]}, acc_in=[acc_mid],
    )
    one[last] = after(one[last], done_mid)
    two[0] = after(two[0], done_mid)
    done_one, acc_two = call(
        "cross_next",
        [
            ("one", [(s, s) for s in range(parts)], None, True, 0),
            ("two", [(s, s) for s in early], None, False, 1),
        ],
        sources={"one": one, "two": two[:last]},
    )
    two[last] = after(two[last], acc_two)
    (out,) = call(
        "cross_last", [("two", [(last, 0)], 0, True, None)], sources={"two": two[last:]},
        acc_in=[acc_two], done=[done_far, done_mid, done_one],
    )
    bands = out.shape[3] // 2
    out = out.reshape(ROUNDS, chans, chans, bands, 2, LANES).transpose(0, 1, 2, 4, 3, 5)
    return out.reshape(ROUNDS, chans, chans, 2, bands * LANES)


def solution(mesh):
    return jax.shard_map(
        shards,
        mesh=mesh,
        in_specs=(P("chan", "win", None), P()),
        out_specs=P(None, "chan", None, None, "win"),
        check_vma=False,
    )
```

```python
import functools
import math

import jax
import jax.numpy as jnp
from jax import lax
from jax.experimental import pallas as pl
from jax.experimental.pallas import tpu as pltpu
from jax.sharding import PartitionSpec as P

BINS = 4096
BAND = 128
ROUNDS = 4
REACH = 2000
LANES = 128
band_epsilon = 1e-06
VMEM = pl.BlockSpec(memory_space=pltpu.VMEM)
SMEM = pl.BlockSpec(memory_space=pltpu.SMEM)
HBM = pl.BlockSpec(memory_space=pltpu.HBM)
PARAMS = pltpu.CompilerParams(vmem_limit_bytes=40 * 1024 * 1024)


def cost(microseconds):
    return pl.CostEstimate(flops=int(microseconds * 1.1e9), bytes_accessed=0, transcendentals=0)


def split3(value):
    hi = value.astype(jnp.bfloat16)
    rest = value - hi.astype(jnp.float32)
    mid = rest.astype(jnp.bfloat16)
    lo = (rest - mid.astype(jnp.float32)).astype(jnp.bfloat16)
    return hi, mid, lo


def real_dft(values):
    n = len(values)
    if n == 2:
        return [(values[0] + values[1], None), (values[0] - values[1], None)]
    even, odd = real_dft(values[0::2]), real_dft(values[1::2])
    out = [None] * (n // 2 + 1)
    for k in range(n // 4 + 1):
        (er, ei), (dr, di) = even[k], odd[k]
        if k == 0:
            out[0] = (er + dr, None)
            out[n // 2] = (er - dr, None)
        elif 4 * k == n:
            out[k] = (er, -dr)
        else:
            c, s = math.cos(2.0 * math.pi * k / n), math.sin(2.0 * math.pi * k / n)
            tr = dr * c + di * s
            ti = di * c - dr * s
            out[k] = (er + tr, ei + ti)
            out[n // 2 - k] = (er - tr, ti - ei)
    return out


def spectra_channel(parts, chan, x, tables, t_ref, outs):
    tw_ref, main_ref, side_ref, bands_ref, pick_ref = tables
    first = len(x)
    wins = x[0].shape[0]
    bands = BINS // BAND // parts
    terms = real_dft(x)
    rows = []
    for k in range(first):
        re, im = terms[min(k, first - k)]
        cos, sin = tw_ref[0, pl.ds(k, 1), :], tw_ref[1, pl.ds(k, 1), :]
        if im is None:
            row = [re * cos, -(re * sin)]
        elif 2 * k <= first:
            row = [re * cos + im * sin, im * cos - re * sin]
        else:
            row = [re * cos - im * sin, -(im * cos + re * sin)]
        rows.append(jnp.concatenate(row, axis=1))
    hi, mid, lo = split3(jnp.concatenate(rows, axis=0))
    main = jnp.dot(
        jnp.concatenate([hi, mid], axis=1), main_ref[...], preferred_element_type=jnp.float32
    )
    side = jnp.dot(
        jnp.concatenate([hi, lo], axis=1), side_ref[...], preferred_element_type=jnp.float32
    )
    spec = (main[:, :LANES] + main[:, LANES:] + side).reshape(first, wins, LANES)
    total = jnp.dot(
        jnp.concatenate(split3(jnp.sum(spec * spec, axis=0)), axis=1),
        bands_ref[...],
        preferred_element_type=jnp.float32,
    )
    scale = lax.rsqrt(total * (1.0 / BAND) + band_epsilon)
    t_ref[chan] = (spec * scale).reshape(first * wins, LANES)
    white = jnp.concatenate(
        [t_ref[chan, pl.ds(win, first, stride=wins), :].astype(jnp.bfloat16) for win in range(wins)],
        axis=0,
    )
    spread = lax.dot_general(
        pick_ref[...], white, (((1,), (1,)), ((), ())), preferred_element_type=jnp.float32
    )
    left = lax.broadcasted_iota(jnp.int32, (bands, LANES), 1) < first
    for pair in range(wins // 2):
        tile = spread[:, pair * LANES : (pair + 1) * LANES].reshape(parts, 2, 2, bands, LANES)
        for s in range(parts):
            for imag in range(2):
                even, odd = tile[s, imag, 0], tile[s, imag, 1]
                one = jnp.where(left, even, pltpu.roll(odd, first, 1)).astype(jnp.bfloat16)
                two = jnp.where(left, pltpu.roll(even, first, 1), odd).astype(jnp.bfloat16)
                at = pl.ds(imag * bands, bands)
                outs[s][chan, 2 * pair, at, :] = one
                outs[s][chan, 2 * pair + 1, at, :] = two


def turn_table(index, period):
    index = lax.rem(index, period)
    quarter = period // 4
    turn = lax.div(index + quarter // 2, quarter)
    angle = (index - turn * quarter).astype(jnp.float32) * (2.0 * math.pi / period)
    square = angle * angle

    def series(first):
        value = jnp.full_like(angle, 0.0)
        for power in range(10 + first, first - 1, -2):
            value = value * square + (-1) ** (power // 2) / math.factorial(power)
        return value

    cos, sin = series(0), series(1) * angle
    swap = lax.rem(turn, 2) == 1
    minus_cos = (turn == 1) | (turn == 2)
    minus_sin = (turn == 2) | (turn == 3)
    cos, sin = jnp.where(swap, sin, cos), jnp.where(swap, cos, sin)
    return jnp.where(minus_cos, -cos, cos), jnp.where(minus_sin, -sin, sin)


def gains_kernel(chans, inv_root, pos_ref, gain_ref):
    block = lax.axis_index("chan")
    last = pos_ref.shape[0] - 1
    for row in range(ROUNDS * chans * chans):
        rnd, a, c = row // (chans * chans), row // chans % chans, row % chans
        pos_c = pos_ref[lax.min((block + rnd + 1) * chans + c, last)]
        near = pos_c - pos_ref[block * chans + a] <= REACH
        gain = jnp.where(near, inv_root, 0.0).astype(jnp.float32)
        gain_ref[pl.ds(row, 1), :] = jnp.full((1, LANES), gain)


def stack_gains(positions, chans, windows):
    return pl.pallas_call(
        functools.partial(gains_kernel, chans, 1.0 / math.sqrt(windows)),
        in_specs=[SMEM],
        out_specs=VMEM,
        out_shape=jax.ShapeDtypeStruct((ROUNDS * chans * chans, LANES), jnp.float32),
        compiler_params=PARAMS,
        cost_estimate=cost(0.5),
        name="gains",
    )(positions)


def tables_kernel(parts, samples, tw_ref, main_ref, side_ref, bands_ref, pick_ref):
    first = samples // LANES
    bands = BINS // BAND // parts
    me = lax.axis_index("win")
    k1 = lax.broadcasted_iota(jnp.int32, (first, LANES), 0)
    q = lax.broadcasted_iota(jnp.int32, (first, LANES), 1)
    tw_ref[0], tw_ref[1] = turn_table(k1 * q, samples)
    row = lax.broadcasted_iota(jnp.int32, (LANES, LANES), 0)
    lane = lax.broadcasted_iota(jnp.int32, (LANES, LANES), 1)
    real = lane < first
    m = lax.rem(lane, first)
    cos, sin = turn_table(row * m, LANES)
    table = jnp.concatenate([jnp.where(real, cos, -sin), jnp.where(real, sin, cos)], axis=0)
    hi, mid, lo = split3(table)
    wide = jnp.concatenate([hi, mid], axis=1)
    main_ref[...] = jnp.concatenate([wide, wide], axis=0)
    side_ref[...] = jnp.concatenate([lo, hi], axis=0)
    same = lax.div(lax.rem(row, first), 2) == lax.div(m, 2)
    bands_ref[...] = jnp.concatenate([same.astype(jnp.float32)] * 3, axis=0).astype(jnp.bfloat16)
    part = lax.rem(me + lax.div(row, 4 * bands), parts)
    imag = lax.rem(lax.div(row, 2 * bands), 2)
    odd = lax.rem(lax.div(row, bands), 2)
    source = imag * first + 2 * (part * bands + lax.rem(row, bands)) + odd
    pick_ref[...] = (lane == source).astype(jnp.float32).astype(jnp.bfloat16)


def spectra_kernel(parts, x_ref, *refs):
    tables, outs, t_ref = refs[:5], refs[5:-1], refs[-1]
    chans, first = x_ref.shape[:2]
    for chan in range(chans):
        x = [x_ref[chan, p] for p in range(first)]
        spectra_channel(parts, chan, x, tables, t_ref, outs)


def whitened_spectra(records, parts):
    chans, wins, samples = records.shape
    first = samples // LANES
    rows = 2 * (BINS // BAND // parts)
    x = records.reshape(chans, wins, first, LANES).transpose(0, 2, 1, 3)
    tables = pl.pallas_call(
        functools.partial(tables_kernel, parts, samples),
        out_specs=[VMEM] * 5,
        out_shape=[
            jax.ShapeDtypeStruct((2, first, LANES), jnp.float32),
            jax.ShapeDtypeStruct((4 * LANES, 2 * LANES), jnp.bfloat16),
            jax.ShapeDtypeStruct((4 * LANES, LANES), jnp.bfloat16),
            jax.ShapeDtypeStruct((3 * LANES, LANES), jnp.bfloat16),
            jax.ShapeDtypeStruct((LANES, LANES), jnp.bfloat16),
        ],
        compiler_params=PARAMS,
        cost_estimate=cost(1),
        name="tables",
    )()
    return pl.pallas_call(
        functools.partial(spectra_kernel, parts),
        in_specs=[VMEM] * 6,
        out_specs=[VMEM] * parts,
        out_shape=[jax.ShapeDtypeStruct((chans, wins, rows, LANES), jnp.bfloat16)] * parts,
        scratch_shapes=[pltpu.VMEM((chans, first * wins, LANES), jnp.float32)],
        compiler_params=PARAMS,
        cost_estimate=cost(4),
        name="spectra",
    )(x, *tables)


def cross_unit(mine, theirs, acc):
    rows = mine[0][0].shape[1]
    bands = rows // 2
    wins = mine[0][0].shape[0]
    per_step = wins if wins <= 8 else 1

    def planes(ref, win):
        return [ref[win, pl.ds(i * bands, bands), :].astype(jnp.float32) for i in range(2)]

    for own, their in zip(mine, theirs):

        def step(index, acc, own=own, their=their):
            acc = list(acc)
            for i in range(per_step):
                win = index * per_step + i
                ours = [planes(ref, win) for ref in own]
                for c, ref in enumerate(their):
                    cr, ci = planes(ref, win)
                    for a, (ar, ai) in enumerate(ours):
                        at = 2 * (a * len(their) + c)
                        acc[at] = acc[at] + ar * cr + ai * ci
                        acc[at + 1] = acc[at + 1] + ai * cr - ar * ci
            return tuple(acc)

        acc = lax.fori_loop(0, wins // per_step, step, acc)
    return acc


def cross_kernel(layout, jobs, *refs):
    groups, at = {}, 0
    for name, count in layout:
        groups[name] = refs[at : at + count]
        at += count
    (gain_ref,) = groups["gains"]
    mine = groups["mine"]
    chans, _, rows, _ = mine[0].shape
    bands = rows // 2
    odd = lax.rem(lax.axis_index("chan"), 2)
    rounds = {"one": 2 * odd, "mid": 1, "two": 2 - 2 * odd, "far": 3}
    step = 2
    copies = []

    def send(source, ref, a_start, count):
        (out_ref,), (sems,) = groups["out"], groups["sems"]
        part = pl.ds(a_start, count)
        copy = pltpu.make_async_copy(
            ref.at[part], out_ref.at[rounds[source], part], sems.at[len(copies)]
        )
        copy.start()
        copies.append(copy)

    for source, ref in zip(("far", "mid", "one"), groups["done"]):
        send(source, ref, 0, chans)
    for source, pieces, acc_in, final, to in jobs:
        rnd = rounds[source]
        to_ref = groups["buffer"][0] if to is None else groups["acc_out"][to]
        for a_start in range(0, chans, step):
            a_list = range(a_start, min(a_start + step, chans))
            for c_start in range(0, chans, step):
                c_list = range(c_start, min(c_start + step, chans))
                ours = [[mine[piece].at[a] for a in a_list] for piece, _ in pieces]
                theirs = [[groups[source][ref].at[c] for c in c_list] for _, ref in pieces]
                order = [(a, c, i) for a in a_list for c in c_list for i in range(2)]
                if acc_in is None:
                    acc = tuple(jnp.zeros((bands, LANES), jnp.float32) for _ in order)
                else:
                    ref = groups["acc_in"][acc_in]
                    acc = tuple(ref[a, c, pl.ds(i * bands, bands), :] for a, c, i in order)
                acc = cross_unit(ours, theirs, acc)
                for (a, c, i), value in zip(order, acc):
                    if not final:
                        to_ref[a, c, pl.ds(i * bands, bands), :] = value
                        continue
                    gain = gain_ref[pl.ds((rnd * chans + a) * chans + c, 1), :]
                    to_ref[a, c, pl.ds(i, bands, stride=2), :] = value * gain
            if to is None:
                send(source, to_ref, a_start, len(a_list))
    for copy in copies:
        copy.wait()


def cross_call(name, jobs, gains, mine, sources, acc_in=(), done=()):
    chans, _, rows, _ = mine[0].shape
    groups = [("gains", [gains]), ("mine", mine), *sources.items()]
    groups += [("acc_in", acc_in), ("done", done)]
    groups = [(key, list(arrays)) for key, arrays in groups]
    operands = [array for _, arrays in groups for array in arrays]
    layout = [(key, len(arrays)) for key, arrays in groups]
    sums = jax.ShapeDtypeStruct((chans, chans, rows, LANES), jnp.float32)
    whole = jax.ShapeDtypeStruct((ROUNDS,) + sums.shape, jnp.float32)
    acc_count = sum(job[4] is not None for job in jobs)
    ends = 1 - acc_count // len(jobs)
    layout += [("out", ends), ("acc_out", acc_count), ("buffer", ends), ("sems", ends)]
    scratch = [pltpu.VMEM(sums.shape, jnp.float32), pltpu.SemaphoreType.DMA((chans + len(done),))]
    return pl.pallas_call(
        functools.partial(cross_kernel, layout, jobs),
        in_specs=[VMEM] * len(operands),
        out_specs=[HBM] * ends + [VMEM] * acc_count,
        out_shape=[whole] * ends + [sums] * acc_count,
        scratch_shapes=scratch * ends,
        compiler_params=PARAMS,
        cost_estimate=cost({"cross_mid": 30.0}.get(name, 0.6)),
        name=name,
    )(*operands)


def choose(bit, own, far, count=None):
    count = count or far.shape[0]

    def kernel(own_ref, far_ref, out_ref):
        yes = lax.rem(lax.div(lax.axis_index("chan"), bit), 2) == 1

        @pl.when(yes)
        def _():
            out_ref[...] = own_ref[pl.ds(0, count)]

        @pl.when(jnp.logical_not(yes))
        def _():
            out_ref[...] = far_ref[pl.ds(0, count)]

    return pl.pallas_call(
        kernel,
        in_specs=[VMEM] * 2,
        out_specs=VMEM,
        out_shape=jax.ShapeDtypeStruct((count,) + far.shape[1:], far.dtype),
        compiler_params=PARAMS,
        cost_estimate=cost(0.1),
        name="choose",
    )(own, far)


def join(estimate, *arrays):
    def kernel(*refs):
        start = 0
        for ref in refs[:-1]:
            refs[-1][pl.ds(start, ref.shape[0])] = ref[...]
            start += ref.shape[0]

    shape = (sum(array.shape[0] for array in arrays),) + arrays[0].shape[1:]
    return pl.pallas_call(
        kernel,
        in_specs=[VMEM] * len(arrays),
        out_specs=VMEM,
        out_shape=jax.ShapeDtypeStruct(shape, arrays[0].dtype),
        compiler_params=PARAMS,
        cost_estimate=cost(estimate),
        name="join",
    )(*arrays)


def after(value, *others):
    return lax.optimization_barrier((value, *others))[0]


def shards(records, positions):
    parts = lax.axis_size("win")
    blocks = lax.axis_size("chan")
    chans, wins, _ = records.shape
    spectra = whitened_spectra(records, parts)
    up = [(b, b - 4) for b in range(4, blocks)]
    swap2 = [(b, b ^ 2) for b in range(blocks)]
    swap1 = [(b, b ^ 1) for b in range(blocks)]
    mine = [spectra[0]]
    for s in range(1, parts):
        mine.append(lax.ppermute(spectra[s], "win", [(i, (i + s) % parts) for i in range(parts)]))
    far = [lax.ppermute(own, "chan", up) for own in mine]
    last = parts - 1
    early = range(last)
    gains = stack_gains(after(positions, far[0]), chans, parts * wins)
    call = functools.partial(cross_call, gains=gains, mine=mine)

    (acc_far,) = call(
        "cross_far", [("far", [(s, s) for s in early], None, False, 0)], sources={"far": far[:-1]}
    )
    far[last] = after(far[last], acc_far)
    mid, one, two = [], [], []
    half = chans // 2
    direct = lax.ppermute(mine[last][half:], "chan", [(b, b - 2) for b in range(2, blocks)])
    for s in range(parts):
        count = None if s < last else half
        mid.append(lax.ppermute(choose(2, mine[s], far[s], count), "chan", swap2))
        one.append(lax.ppermute(choose(1, mine[s], far[s]), "chan", swap1))
        if s < last:
            two.append(lax.ppermute(mid[s], "chan", swap1))
    done_far, acc_mid = call(
        "cross_most",
        [
            ("far", [(last, 0)], 0, True, 0),
            ("mid", [(s, s) for s in early], None, False, 1),
        ],
        sources={"far": far[last:], "mid": mid[:last]},
        acc_in=[acc_far],
    )
    direct = join(5.0, after(direct, acc_mid))
    mid[last] = join(0.1, after(mid[last], direct), direct)
    two.append(lax.ppermute(mid[last], "chan", swap1))
    (done_mid,) = call(
        "cross_mid", [("mid", [(last, 0)], 0, True, 0)],
        sources={"mid": mid[last:]}, acc_in=[acc_mid],
    )
    one[last] = after(one[last], done_mid)
    two[0] = after(two[0], done_mid)
    done_one, acc_two = call(
        "cross_next",
        [
            ("one", [(s, s) for s in range(parts)], None, True, 0),
            ("two", [(s, s) for s in early], None, False, 1),
        ],
        sources={"one": one, "two": two[:last]},
    )
    two[last] = after(two[last], acc_two)
    (out,) = call(
        "cross_last", [("two", [(last, 0)], 0, True, None)], sources={"two": two[last:]},
        acc_in=[acc_two], done=[done_far, done_mid, done_one],
    )
    bands = out.shape[3] // 2
    out = out.reshape(ROUNDS, chans, chans, bands, 2, LANES).transpose(0, 1, 2, 4, 3, 5)
    return out.reshape(ROUNDS, chans, chans, 2, bands * LANES)


def solution(mesh):
    return jax.shard_map(
        shards,
        mesh=mesh,
        in_specs=(P("chan", "win", None), P()),
        out_specs=P(None, "chan", None, None, "win"),
        check_vma=False,
    )
```

```python
import functools
import math

import jax
import jax.numpy as jnp
from jax import lax
from jax.experimental import pallas as pl
from jax.experimental.pallas import tpu as pltpu
from jax.sharding import PartitionSpec as P

BINS = 4096
BAND = 128
ROUNDS = 4
REACH = 2000
LANES = 128
band_epsilon = 1e-06
VMEM = pl.BlockSpec(memory_space=pltpu.VMEM)
SMEM = pl.BlockSpec(memory_space=pltpu.SMEM)
HBM = pl.BlockSpec(memory_space=pltpu.HBM)
PARAMS = pltpu.CompilerParams(vmem_limit_bytes=40 * 1024 * 1024)


def cost(microseconds):
    return pl.CostEstimate(flops=int(microseconds * 1.1e9), bytes_accessed=0, transcendentals=0)


def split3(value):
    hi = value.astype(jnp.bfloat16)
    rest = value - hi.astype(jnp.float32)
    mid = rest.astype(jnp.bfloat16)
    lo = (rest - mid.astype(jnp.float32)).astype(jnp.bfloat16)
    return hi, mid, lo


def real_dft(values):
    n = len(values)
    if n == 2:
        return [(values[0] + values[1], None), (values[0] - values[1], None)]
    even, odd = real_dft(values[0::2]), real_dft(values[1::2])
    out = [None] * (n // 2 + 1)
    for k in range(n // 4 + 1):
        (er, ei), (dr, di) = even[k], odd[k]
        if k == 0:
            out[0] = (er + dr, None)
            out[n // 2] = (er - dr, None)
        elif 4 * k == n:
            out[k] = (er, -dr)
        else:
            c, s = math.cos(2.0 * math.pi * k / n), math.sin(2.0 * math.pi * k / n)
            tr = dr * c + di * s
            ti = di * c - dr * s
            out[k] = (er + tr, ei + ti)
            out[n // 2 - k] = (er - tr, ti - ei)
    return out


def spectra_channel(parts, chan, x, tables, t_ref, outs):
    tw_ref, main_ref, side_ref, bands_ref, pick_ref = tables
    first = len(x)
    wins = x[0].shape[0]
    bands = BINS // BAND // parts
    terms = real_dft(x)
    rows = []
    for k in range(first):
        re, im = terms[min(k, first - k)]
        cos, sin = tw_ref[0, pl.ds(k, 1), :], tw_ref[1, pl.ds(k, 1), :]
        if im is None:
            row = [re * cos, -(re * sin)]
        elif 2 * k <= first:
            row = [re * cos + im * sin, im * cos - re * sin]
        else:
            row = [re * cos - im * sin, -(im * cos + re * sin)]
        rows.append(jnp.concatenate(row, axis=1))
    hi, mid, lo = split3(jnp.concatenate(rows, axis=0))
    main = jnp.dot(
        jnp.concatenate([hi, mid], axis=1), main_ref[...], preferred_element_type=jnp.float32
    )
    side = jnp.dot(
        jnp.concatenate([hi, lo], axis=1), side_ref[...], preferred_element_type=jnp.float32
    )
    yield
    spec = (main[:, :LANES] + main[:, LANES:] + side).reshape(first, wins, LANES)
    total = jnp.dot(
        jnp.concatenate(split3(jnp.sum(spec * spec, axis=0)), axis=1),
        bands_ref[...],
        preferred_element_type=jnp.float32,
    )
    scale = lax.rsqrt(total * (1.0 / BAND) + band_epsilon)
    t_ref[chan] = (spec * scale).reshape(first * wins, LANES)
    white = jnp.concatenate(
        [t_ref[chan, pl.ds(win, first, stride=wins), :].astype(jnp.bfloat16) for win in range(wins)],
        axis=0,
    )
    spread = lax.dot_general(
        pick_ref[...], white, (((1,), (1,)), ((), ())), preferred_element_type=jnp.float32
    )
    yield
    left = lax.broadcasted_iota(jnp.int32, (bands, LANES), 1) < first
    for pair in range(wins // 2):
        tile = spread[:, pair * LANES : (pair + 1) * LANES].reshape(parts, 2, 2, bands, LANES)
        for s in range(parts):
            for imag in range(2):
                even, odd = tile[s, imag, 0], tile[s, imag, 1]
                one = jnp.where(left, even, pltpu.roll(odd, first, 1)).astype(jnp.bfloat16)
                two = jnp.where(left, pltpu.roll(even, first, 1), odd).astype(jnp.bfloat16)
                at = pl.ds(imag * bands, bands)
                outs[s][chan, 2 * pair, at, :] = one
                outs[s][chan, 2 * pair + 1, at, :] = two


def turn_table(index, period):
    index = lax.rem(index, period)
    quarter = period // 4
    turn = lax.div(index + quarter // 2, quarter)
    angle = (index - turn * quarter).astype(jnp.float32) * (2.0 * math.pi / period)
    square = angle * angle

    def series(first):
        value = jnp.full_like(angle, 0.0)
        for power in range(10 + first, first - 1, -2):
            value = value * square + (-1) ** (power // 2) / math.factorial(power)
        return value

    cos, sin = series(0), series(1) * angle
    swap = lax.rem(turn, 2) == 1
    minus_cos = (turn == 1) | (turn == 2)
    minus_sin = (turn == 2) | (turn == 3)
    cos, sin = jnp.where(swap, sin, cos), jnp.where(swap, cos, sin)
    return jnp.where(minus_cos, -cos, cos), jnp.where(minus_sin, -sin, sin)


def gains_kernel(chans, inv_root, pos_ref, gain_ref):
    block = lax.axis_index("chan")
    last = pos_ref.shape[0] - 1
    for row in range(ROUNDS * chans * chans):
        rnd, a, c = row // (chans * chans), row // chans % chans, row % chans
        pos_c = pos_ref[lax.min((block + rnd + 1) * chans + c, last)]
        near = pos_c - pos_ref[block * chans + a] <= REACH
        gain = jnp.where(near, inv_root, 0.0).astype(jnp.float32)
        gain_ref[pl.ds(row, 1), :] = jnp.full((1, LANES), gain)


def stack_gains(positions, chans, windows):
    return pl.pallas_call(
        functools.partial(gains_kernel, chans, 1.0 / math.sqrt(windows)),
        in_specs=[SMEM],
        out_specs=VMEM,
        out_shape=jax.ShapeDtypeStruct((ROUNDS * chans * chans, LANES), jnp.float32),
        compiler_params=PARAMS,
        cost_estimate=cost(0.5),
        name="gains",
    )(positions)


def tables_kernel(parts, samples, tw_ref, main_ref, side_ref, bands_ref, pick_ref):
    first = samples // LANES
    bands = BINS // BAND // parts
    me = lax.axis_index("win")
    k1 = lax.broadcasted_iota(jnp.int32, (first, LANES), 0)
    q = lax.broadcasted_iota(jnp.int32, (first, LANES), 1)
    tw_ref[0], tw_ref[1] = turn_table(k1 * q, samples)
    row = lax.broadcasted_iota(jnp.int32, (LANES, LANES), 0)
    lane = lax.broadcasted_iota(jnp.int32, (LANES, LANES), 1)
    real = lane < first
    m = lax.rem(lane, first)
    cos, sin = turn_table(row * m, LANES)
    table = jnp.concatenate([jnp.where(real, cos, -sin), jnp.where(real, sin, cos)], axis=0)
    hi, mid, lo = split3(table)
    wide = jnp.concatenate([hi, mid], axis=1)
    main_ref[...] = jnp.concatenate([wide, wide], axis=0)
    side_ref[...] = jnp.concatenate([lo, hi], axis=0)
    same = lax.div(lax.rem(row, first), 2) == lax.div(m, 2)
    bands_ref[...] = jnp.concatenate([same.astype(jnp.float32)] * 3, axis=0).astype(jnp.bfloat16)
    part = lax.rem(me + lax.div(row, 4 * bands), parts)
    imag = lax.rem(lax.div(row, 2 * bands), 2)
    odd = lax.rem(lax.div(row, bands), 2)
    source = imag * first + 2 * (part * bands + lax.rem(row, bands)) + odd
    pick_ref[...] = (lane == source).astype(jnp.float32).astype(jnp.bfloat16)


def spectra_kernel(parts, x_ref, *refs):
    tables, outs, t_ref = refs[:5], refs[5:-1], refs[-1]
    chans, first = x_ref.shape[:2]
    stages = 3
    works = []
    for turn in range(chans + stages - 1):
        if turn < chans:
            x = [x_ref[turn, p] for p in range(first)]
            works.append(spectra_channel(parts, turn, x, tables, t_ref, outs))
        for work in reversed(works[max(0, turn - stages + 1) :]):
            next(work, None)


def whitened_spectra(records, parts):
    chans, wins, samples = records.shape
    first = samples // LANES
    rows = 2 * (BINS // BAND // parts)
    x = records.reshape(chans, wins, first, LANES).transpose(0, 2, 1, 3)
    tables = pl.pallas_call(
        functools.partial(tables_kernel, parts, samples),
        out_specs=[VMEM] * 5,
        out_shape=[
            jax.ShapeDtypeStruct((2, first, LANES), jnp.float32),
            jax.ShapeDtypeStruct((4 * LANES, 2 * LANES), jnp.bfloat16),
            jax.ShapeDtypeStruct((4 * LANES, LANES), jnp.bfloat16),
            jax.ShapeDtypeStruct((3 * LANES, LANES), jnp.bfloat16),
            jax.ShapeDtypeStruct((LANES, LANES), jnp.bfloat16),
        ],
        compiler_params=PARAMS,
        cost_estimate=cost(1),
        name="tables",
    )()
    return pl.pallas_call(
        functools.partial(spectra_kernel, parts),
        in_specs=[VMEM] * 6,
        out_specs=[VMEM] * parts,
        out_shape=[jax.ShapeDtypeStruct((chans, wins, rows, LANES), jnp.bfloat16)] * parts,
        scratch_shapes=[pltpu.VMEM((chans, first * wins, LANES), jnp.float32)],
        compiler_params=PARAMS,
        cost_estimate=cost(4),
        name="spectra",
    )(x, *tables)


def cross_unit(mine, theirs, acc):
    rows = mine[0][0].shape[1]
    bands = rows // 2
    wins = mine[0][0].shape[0]
    per_step = wins if wins <= 8 else 1

    def planes(ref, win):
        return [ref[win, pl.ds(i * bands, bands), :].astype(jnp.float32) for i in range(2)]

    for own, their in zip(mine, theirs):

        def step(index, acc, own=own, their=their):
            acc = list(acc)
            for i in range(per_step):
                win = index * per_step + i
                ours = [planes(ref, win) for ref in own]
                for c, ref in enumerate(their):
                    cr, ci = planes(ref, win)
                    for a, (ar, ai) in enumerate(ours):
                        at = 2 * (a * len(their) + c)
                        acc[at] = acc[at] + ar * cr + ai * ci
                        acc[at + 1] = acc[at + 1] + ai * cr - ar * ci
            return tuple(acc)

        acc = lax.fori_loop(0, wins // per_step, step, acc)
    return acc


def channel(refs, index, chan):
    for i in index if isinstance(index, tuple) else (index,):
        if chan < refs[i].shape[0]:
            break
        chan -= refs[i].shape[0]
    return refs[i].at[chan]


def cross_kernel(layout, jobs, *refs):
    groups, at = {}, 0
    for name, count in layout:
        groups[name] = refs[at : at + count]
        at += count
    (gain_ref,) = groups["gains"]
    mine = groups["mine"]
    chans, _, rows, _ = mine[0].shape
    bands = rows // 2
    odd = lax.rem(lax.axis_index("chan"), 2)
    rounds = {"one": 2 * odd, "mid": 1, "two": 2 - 2 * odd, "far": 3}
    step = 2
    copies = []

    def send(source, ref, a_start, count):
        (out_ref,), (sems,) = groups["out"], groups["sems"]
        part = pl.ds(a_start, count)
        copy = pltpu.make_async_copy(
            ref.at[part], out_ref.at[rounds[source], part], sems.at[len(copies)]
        )
        copy.start()
        copies.append(copy)

    for source, ref in zip(("far", "mid", "one"), groups["done"]):
        send(source, ref, 0, chans)
    for source, pieces, acc_in, final, to in jobs:
        rnd = rounds[source]
        to_ref = groups["buffer"][0] if to is None else groups["acc_out"][to]
        for a_start in range(0, chans, step):
            a_list = range(a_start, min(a_start + step, chans))
            for c_start in range(0, chans, step):
                c_list = range(c_start, min(c_start + step, chans))
                ours = [[mine[piece].at[a] for a in a_list] for piece, _ in pieces]
                theirs = [[channel(groups[source], ref, c) for c in c_list] for _, ref in pieces]
                order = [(a, c, i) for a in a_list for c in c_list for i in range(2)]
                if acc_in is None:
                    acc = tuple(jnp.zeros((bands, LANES), jnp.float32) for _ in order)
                else:
                    ref = groups["acc_in"][acc_in]
                    acc = tuple(ref[a, c, pl.ds(i * bands, bands), :] for a, c, i in order)
                acc = cross_unit(ours, theirs, acc)
                for (a, c, i), value in zip(order, acc):
                    if not final:
                        to_ref[a, c, pl.ds(i * bands, bands), :] = value
                        continue
                    gain = gain_ref[pl.ds((rnd * chans + a) * chans + c, 1), :]
                    to_ref[a, c, pl.ds(i, bands, stride=2), :] = value * gain
            if to is None:
                send(source, to_ref, a_start, len(a_list))
    for copy in copies:
        copy.wait()


def cross_call(name, jobs, gains, mine, sources, acc_in=(), done=()):
    chans, _, rows, _ = mine[0].shape
    groups = [("gains", [gains]), ("mine", mine), *sources.items()]
    groups += [("acc_in", acc_in), ("done", done)]
    groups = [(key, list(arrays)) for key, arrays in groups]
    operands = [array for _, arrays in groups for array in arrays]
    layout = [(key, len(arrays)) for key, arrays in groups]
    sums = jax.ShapeDtypeStruct((chans, chans, rows, LANES), jnp.float32)
    whole = jax.ShapeDtypeStruct((ROUNDS,) + sums.shape, jnp.float32)
    acc_count = sum(job[4] is not None for job in jobs)
    ends = 1 - acc_count // len(jobs)
    layout += [("out", ends), ("acc_out", acc_count), ("buffer", ends), ("sems", ends)]
    scratch = [pltpu.VMEM(sums.shape, jnp.float32), pltpu.SemaphoreType.DMA((chans + len(done),))]
    return pl.pallas_call(
        functools.partial(cross_kernel, layout, jobs),
        in_specs=[VMEM] * len(operands),
        out_specs=[HBM] * ends + [VMEM] * acc_count,
        out_shape=[whole] * ends + [sums] * acc_count,
        scratch_shapes=scratch * ends,
        compiler_params=PARAMS,
        cost_estimate=cost({"cross_mid": 30.0}.get(name, 0.6)),
        name=name,
    )(*operands)


def choose(bit, own, far, count=None):
    count = count or far.shape[0]

    def kernel(own_ref, far_ref, out_ref):
        yes = lax.rem(lax.div(lax.axis_index("chan"), bit), 2) == 1

        @pl.when(yes)
        def _():
            out_ref[...] = own_ref[pl.ds(0, count)]

        @pl.when(jnp.logical_not(yes))
        def _():
            out_ref[...] = far_ref[pl.ds(0, count)]

    return pl.pallas_call(
        kernel,
        in_specs=[VMEM] * 2,
        out_specs=VMEM,
        out_shape=jax.ShapeDtypeStruct((count,) + far.shape[1:], far.dtype),
        compiler_params=PARAMS,
        cost_estimate=cost(0.1),
        name="choose",
    )(own, far)


def after(value, *others):
    return lax.optimization_barrier((value, *others))[0]


def shards(records, positions):
    parts = lax.axis_size("win")
    blocks = lax.axis_size("chan")
    chans, wins, _ = records.shape
    spectra = whitened_spectra(records, parts)
    up = [(b, b - 4) for b in range(4, blocks)]
    swap2 = [(b, b ^ 2) for b in range(blocks)]
    swap1 = [(b, b ^ 1) for b in range(blocks)]
    mine = [spectra[0]]
    for s in range(1, parts):
        mine.append(lax.ppermute(spectra[s], "win", [(i, (i + s) % parts) for i in range(parts)]))
    far = [lax.ppermute(own, "chan", up) for own in mine]
    last = parts - 1
    early = range(last)
    gains = stack_gains(after(positions, far[0]), chans, parts * wins)
    call = functools.partial(cross_call, gains=gains, mine=mine)

    (acc_far,) = call(
        "cross_far", [("far", [(s, s) for s in early], None, False, 0)], sources={"far": far[:-1]}
    )
    far[last] = after(far[last], acc_far)
    mid, one, two = [], [], []
    half = chans // 2
    direct = lax.ppermute(mine[last][half:], "chan", [(b, b - 2) for b in range(2, blocks)])
    for s in range(parts):
        count = None if s < last else half
        mid.append(lax.ppermute(choose(2, mine[s], far[s], count), "chan", swap2))
        one.append(lax.ppermute(choose(1, mine[s], far[s]), "chan", swap1))
        if s < last:
            two.append(lax.ppermute(mid[s], "chan", swap1))
    done_far, acc_mid = call(
        "cross_most",
        [
            ("far", [(last, 0)], 0, True, 0),
            ("mid", [(s, s) for s in early], None, False, 1),
        ],
        sources={"far": far[last:], "mid": mid[:last]},
        acc_in=[acc_far],
    )
    direct = after(direct, acc_mid)
    two_direct = lax.ppermute(direct, "chan", swap1)
    mid[last] = after(mid[last], acc_mid)
    two.append(lax.ppermute(mid[last], "chan", swap1))
    (done_mid,) = call(
        "cross_mid", [("mid", [(last, (0, 1))], 0, True, 0)],
        sources={"mid": [mid[last], direct]}, acc_in=[acc_mid],
    )
    one[last] = after(one[last], done_mid)
    two[0] = after(two[0], done_mid)
    done_one, acc_two = call(
        "cross_next",
        [
            ("one", [(s, s) for s in range(parts)], None, True, 0),
            ("two", [(s, s) for s in early], None, False, 1),
        ],
        sources={"one": one, "two": two[:last]},
    )
    two[last] = after(two[last], acc_two)
    (out,) = call(
        "cross_last", [("two", [(last, (0, 1))], 0, True, None)],
        sources={"two": [two[last], two_direct]},
        acc_in=[acc_two], done=[done_far, done_mid, done_one],
    )
    bands = out.shape[3] // 2
    out = out.reshape(ROUNDS, chans, chans, bands, 2, LANES).transpose(0, 1, 2, 4, 3, 5)
    return out.reshape(ROUNDS, chans, chans, 2, bands * LANES)


def solution(mesh):
    return jax.shard_map(
        shards,
        mesh=mesh,
        in_specs=(P("chan", "win", None), P()),
        out_specs=P(None, "chan", None, None, "win"),
        check_vma=False,
    )
```

```python
import functools
import math

import jax
import jax.numpy as jnp
from jax import lax
from jax.experimental import pallas as pl
from jax.experimental.pallas import tpu as pltpu
from jax.sharding import PartitionSpec as P

BINS = 4096
BAND = 128
ROUNDS = 4
REACH = 2000
LANES = 128
band_epsilon = 1e-06
VMEM = pl.BlockSpec(memory_space=pltpu.VMEM)
SMEM = pl.BlockSpec(memory_space=pltpu.SMEM)
HBM = pl.BlockSpec(memory_space=pltpu.HBM)
PARAMS = pltpu.CompilerParams(vmem_limit_bytes=40 * 1024 * 1024)


def cost(microseconds):
    return pl.CostEstimate(flops=int(microseconds * 1.1e9), bytes_accessed=0, transcendentals=0)


def split3(value):
    hi = value.astype(jnp.bfloat16)
    rest = value - hi.astype(jnp.float32)
    mid = rest.astype(jnp.bfloat16)
    lo = (rest - mid.astype(jnp.float32)).astype(jnp.bfloat16)
    return hi, mid, lo


def real_dft(values):
    n = len(values)
    if n == 2:
        return [(values[0] + values[1], None), (values[0] - values[1], None)]
    even, odd = real_dft(values[0::2]), real_dft(values[1::2])
    out = [None] * (n // 2 + 1)
    for k in range(n // 4 + 1):
        (er, ei), (dr, di) = even[k], odd[k]
        if k == 0:
            out[0] = (er + dr, None)
            out[n // 2] = (er - dr, None)
        elif 4 * k == n:
            out[k] = (er, -dr)
        else:
            c, s = math.cos(2.0 * math.pi * k / n), math.sin(2.0 * math.pi * k / n)
            tr = dr * c + di * s
            ti = di * c - dr * s
            out[k] = (er + tr, ei + ti)
            out[n // 2 - k] = (er - tr, ti - ei)
    return out


def spectra_channel(parts, chan, x, tables, t_ref, outs):
    tw_ref, main_ref, side_ref, bands_ref, pick_ref = tables
    first = len(x)
    wins = x[0].shape[0]
    bands = BINS // BAND // parts
    terms = real_dft(x)
    rows = []
    for k in range(first):
        re, im = terms[min(k, first - k)]
        cos, sin = tw_ref[0, pl.ds(k, 1), :], tw_ref[1, pl.ds(k, 1), :]
        if im is None:
            row = [re * cos, -(re * sin)]
        elif 2 * k <= first:
            row = [re * cos + im * sin, im * cos - re * sin]
        else:
            row = [re * cos - im * sin, -(im * cos + re * sin)]
        rows.append(jnp.concatenate(row, axis=1))
    hi, mid, lo = split3(jnp.concatenate(rows, axis=0))
    yield
    main = jnp.dot(
        jnp.concatenate([hi, mid], axis=1), main_ref[...], preferred_element_type=jnp.float32
    )
    side = jnp.dot(
        jnp.concatenate([hi, lo], axis=1), side_ref[...], preferred_element_type=jnp.float32
    )
    yield
    spec = (main[:, :LANES] + main[:, LANES:] + side).reshape(first, wins, LANES)
    total = jnp.dot(
        jnp.concatenate(split3(jnp.sum(spec * spec, axis=0)), axis=1),
        bands_ref[...],
        preferred_element_type=jnp.float32,
    )
    scale = lax.rsqrt(total * (1.0 / BAND) + band_epsilon)
    t_ref[chan] = (spec * scale).reshape(first * wins, LANES)
    white = jnp.concatenate(
        [t_ref[chan, pl.ds(win, first, stride=wins), :].astype(jnp.bfloat16) for win in range(wins)],
        axis=0,
    )
    spread = lax.dot_general(
        pick_ref[...], white, (((1,), (1,)), ((), ())), preferred_element_type=jnp.float32
    )
    yield
    left = lax.broadcasted_iota(jnp.int32, (bands, LANES), 1) < first
    for pair in range(wins // 2):
        tile = spread[:, pair * LANES : (pair + 1) * LANES].reshape(parts, 2, 2, bands, LANES)
        for s in range(parts):
            for imag in range(2):
                even, odd = tile[s, imag, 0], tile[s, imag, 1]
                one = jnp.where(left, even, pltpu.roll(odd, first, 1)).astype(jnp.bfloat16)
                two = jnp.where(left, pltpu.roll(even, first, 1), odd).astype(jnp.bfloat16)
                at = pl.ds(imag * bands, bands)
                outs[s][chan, 2 * pair, at, :] = one
                outs[s][chan, 2 * pair + 1, at, :] = two


def turn_table(index, period):
    index = lax.rem(index, period)
    quarter = period // 4
    turn = lax.div(index + quarter // 2, quarter)
    angle = (index - turn * quarter).astype(jnp.float32) * (2.0 * math.pi / period)
    square = angle * angle

    def series(first):
        value = jnp.full_like(angle, 0.0)
        for power in range(10 + first, first - 1, -2):
            value = value * square + (-1) ** (power // 2) / math.factorial(power)
        return value

    cos, sin = series(0), series(1) * angle
    swap = lax.rem(turn, 2) == 1
    minus_cos = (turn == 1) | (turn == 2)
    minus_sin = (turn == 2) | (turn == 3)
    cos, sin = jnp.where(swap, sin, cos), jnp.where(swap, cos, sin)
    return jnp.where(minus_cos, -cos, cos), jnp.where(minus_sin, -sin, sin)


def gains_kernel(chans, inv_root, pos_ref, gain_ref):
    block = lax.axis_index("chan")
    last = pos_ref.shape[0] - 1
    for row in range(ROUNDS * chans * chans):
        rnd, a, c = row // (chans * chans), row // chans % chans, row % chans
        pos_c = pos_ref[lax.min((block + rnd + 1) * chans + c, last)]
        near = pos_c - pos_ref[block * chans + a] <= REACH
        gain = jnp.where(near, inv_root, 0.0).astype(jnp.float32)
        gain_ref[pl.ds(row, 1), :] = jnp.full((1, LANES), gain)


def stack_gains(positions, chans, windows):
    return pl.pallas_call(
        functools.partial(gains_kernel, chans, 1.0 / math.sqrt(windows)),
        in_specs=[SMEM],
        out_specs=VMEM,
        out_shape=jax.ShapeDtypeStruct((ROUNDS * chans * chans, LANES), jnp.float32),
        compiler_params=PARAMS,
        cost_estimate=cost(0.5),
        name="gains",
    )(positions)


def tables_kernel(parts, samples, tw_ref, main_ref, side_ref, bands_ref, pick_ref):
    first = samples // LANES
    bands = BINS // BAND // parts
    me = lax.axis_index("win")
    k1 = lax.broadcasted_iota(jnp.int32, (first, LANES), 0)
    q = lax.broadcasted_iota(jnp.int32, (first, LANES), 1)
    tw_ref[0], tw_ref[1] = turn_table(k1 * q, samples)
    row = lax.broadcasted_iota(jnp.int32, (LANES, LANES), 0)
    lane = lax.broadcasted_iota(jnp.int32, (LANES, LANES), 1)
    real = lane < first
    m = lax.rem(lane, first)
    cos, sin = turn_table(row * m, LANES)
    table = jnp.concatenate([jnp.where(real, cos, -sin), jnp.where(real, sin, cos)], axis=0)
    hi, mid, lo = split3(table)
    wide = jnp.concatenate([hi, mid], axis=1)
    main_ref[...] = jnp.concatenate([wide, wide], axis=0)
    side_ref[...] = jnp.concatenate([lo, hi], axis=0)
    same = lax.div(lax.rem(row, first), 2) == lax.div(m, 2)
    bands_ref[...] = jnp.concatenate([same.astype(jnp.float32)] * 3, axis=0).astype(jnp.bfloat16)
    part = lax.rem(me + lax.div(row, 4 * bands), parts)
    imag = lax.rem(lax.div(row, 2 * bands), 2)
    odd = lax.rem(lax.div(row, bands), 2)
    source = imag * first + 2 * (part * bands + lax.rem(row, bands)) + odd
    pick_ref[...] = (lane == source).astype(jnp.float32).astype(jnp.bfloat16)


def spectra_kernel(parts, x_ref, *refs):
    tables, outs, t_ref = refs[:5], refs[5:-1], refs[-1]
    chans, first = x_ref.shape[:2]
    stages = 4
    works = []
    for turn in range(chans + stages - 1):
        if turn < chans:
            x = [x_ref[turn, p] for p in range(first)]
            works.append(spectra_channel(parts, turn, x, tables, t_ref, outs))
        for work in reversed(works[max(0, turn - stages + 1) :]):
            next(work, None)


def whitened_spectra(records, parts):
    chans, wins, samples = records.shape
    first = samples // LANES
    rows = 2 * (BINS // BAND // parts)
    x = records.reshape(chans, wins, first, LANES).transpose(0, 2, 1, 3)
    tables = pl.pallas_call(
        functools.partial(tables_kernel, parts, samples),
        out_specs=[VMEM] * 5,
        out_shape=[
            jax.ShapeDtypeStruct((2, first, LANES), jnp.float32),
            jax.ShapeDtypeStruct((4 * LANES, 2 * LANES), jnp.bfloat16),
            jax.ShapeDtypeStruct((4 * LANES, LANES), jnp.bfloat16),
            jax.ShapeDtypeStruct((3 * LANES, LANES), jnp.bfloat16),
            jax.ShapeDtypeStruct((LANES, LANES), jnp.bfloat16),
        ],
        compiler_params=PARAMS,
        cost_estimate=cost(1),
        name="tables",
    )()
    return pl.pallas_call(
        functools.partial(spectra_kernel, parts),
        in_specs=[VMEM] * 6,
        out_specs=[VMEM] * parts,
        out_shape=[jax.ShapeDtypeStruct((chans, wins, rows, LANES), jnp.bfloat16)] * parts,
        scratch_shapes=[pltpu.VMEM((chans, first * wins, LANES), jnp.float32)],
        compiler_params=PARAMS,
        cost_estimate=cost(4),
        name="spectra",
    )(x, *tables)


def cross_unit(mine, theirs, acc):
    rows = mine[0][0].shape[1]
    bands = rows // 2
    wins = mine[0][0].shape[0]
    per_step = wins if wins <= 8 else 1

    def planes(ref, win):
        return [ref[win, pl.ds(i * bands, bands), :].astype(jnp.float32) for i in range(2)]

    for own, their in zip(mine, theirs):

        def step(index, acc, own=own, their=their):
            acc = list(acc)
            for i in range(per_step):
                win = index * per_step + i
                ours = [planes(ref, win) for ref in own]
                for c, ref in enumerate(their):
                    cr, ci = planes(ref, win)
                    for a, (ar, ai) in enumerate(ours):
                        at = 2 * (a * len(their) + c)
                        acc[at] = acc[at] + ar * cr + ai * ci
                        acc[at + 1] = acc[at + 1] + ai * cr - ar * ci
            return tuple(acc)

        acc = lax.fori_loop(0, wins // per_step, step, acc)
    return acc


def channel(refs, index, chan):
    for i in index if isinstance(index, tuple) else (index,):
        if chan < refs[i].shape[0]:
            break
        chan -= refs[i].shape[0]
    return refs[i].at[chan]


def cross_kernel(layout, jobs, *refs):
    groups, at = {}, 0
    for name, count in layout:
        groups[name] = refs[at : at + count]
        at += count
    (gain_ref,) = groups["gains"]
    mine = groups["mine"]
    chans, _, rows, _ = mine[0].shape
    bands = rows // 2
    odd = lax.rem(lax.axis_index("chan"), 2)
    rounds = {"one": 2 * odd, "mid": 1, "two": 2 - 2 * odd, "far": 3}
    step = 2
    copies = []

    def send(source, ref, a_start, count):
        (out_ref,), (sems,) = groups["out"], groups["sems"]
        part = pl.ds(a_start, count)
        copy = pltpu.make_async_copy(
            ref.at[part], out_ref.at[rounds[source], part], sems.at[len(copies)]
        )
        copy.start()
        copies.append(copy)

    for source, ref in zip(("far", "mid", "one"), groups["done"]):
        send(source, ref, 0, chans)
    for source, pieces, acc_in, final, to in jobs:
        rnd = rounds[source]
        to_ref = groups["buffer"][0] if to is None else groups["acc_out"][to]
        for a_start in range(0, chans, step):
            a_list = range(a_start, min(a_start + step, chans))
            for c_start in range(0, chans, step):
                c_list = range(c_start, min(c_start + step, chans))
                ours = [[mine[piece].at[a] for a in a_list] for piece, _ in pieces]
                theirs = [[channel(groups[source], ref, c) for c in c_list] for _, ref in pieces]
                order = [(a, c, i) for a in a_list for c in c_list for i in range(2)]
                if acc_in is None:
                    acc = tuple(jnp.zeros((bands, LANES), jnp.float32) for _ in order)
                else:
                    ref = groups["acc_in"][acc_in]
                    acc = tuple(ref[a, c, pl.ds(i * bands, bands), :] for a, c, i in order)
                acc = cross_unit(ours, theirs, acc)
                for (a, c, i), value in zip(order, acc):
                    if not final:
                        to_ref[a, c, pl.ds(i * bands, bands), :] = value
                        continue
                    gain = gain_ref[pl.ds((rnd * chans + a) * chans + c, 1), :]
                    to_ref[a, c, pl.ds(i, bands, stride=2), :] = value * gain
            if to is None:
                send(source, to_ref, a_start, len(a_list))
    for copy in copies:
        copy.wait()


def cross_call(name, jobs, gains, mine, sources, acc_in=(), done=()):
    chans, _, rows, _ = mine[0].shape
    groups = [("gains", [gains]), ("mine", mine), *sources.items()]
    groups += [("acc_in", acc_in), ("done", done)]
    groups = [(key, list(arrays)) for key, arrays in groups]
    operands = [array for _, arrays in groups for array in arrays]
    layout = [(key, len(arrays)) for key, arrays in groups]
    sums = jax.ShapeDtypeStruct((chans, chans, rows, LANES), jnp.float32)
    whole = jax.ShapeDtypeStruct((ROUNDS,) + sums.shape, jnp.float32)
    acc_count = sum(job[4] is not None for job in jobs)
    ends = 1 - acc_count // len(jobs)
    layout += [("out", ends), ("acc_out", acc_count), ("buffer", ends), ("sems", ends)]
    scratch = [pltpu.VMEM(sums.shape, jnp.float32), pltpu.SemaphoreType.DMA((chans + len(done),))]
    return pl.pallas_call(
        functools.partial(cross_kernel, layout, jobs),
        in_specs=[VMEM] * len(operands),
        out_specs=[HBM] * ends + [VMEM] * acc_count,
        out_shape=[whole] * ends + [sums] * acc_count,
        scratch_shapes=scratch * ends,
        compiler_params=PARAMS,
        cost_estimate=cost({"cross_mid": 30.0}.get(name, 0.6)),
        name=name,
    )(*operands)


def choose(bit, own, far, count=None):
    count = count or far.shape[0]

    def kernel(own_ref, far_ref, out_ref):
        yes = lax.rem(lax.div(lax.axis_index("chan"), bit), 2) == 1

        @pl.when(yes)
        def _():
            out_ref[...] = own_ref[pl.ds(0, count)]

        @pl.when(jnp.logical_not(yes))
        def _():
            out_ref[...] = far_ref[pl.ds(0, count)]

    return pl.pallas_call(
        kernel,
        in_specs=[VMEM] * 2,
        out_specs=VMEM,
        out_shape=jax.ShapeDtypeStruct((count,) + far.shape[1:], far.dtype),
        compiler_params=PARAMS,
        cost_estimate=cost(0.1),
        name="choose",
    )(own, far)


def after(value, *others):
    return lax.optimization_barrier((value, *others))[0]


def shards(records, positions):
    parts = lax.axis_size("win")
    blocks = lax.axis_size("chan")
    chans, wins, _ = records.shape
    spectra = whitened_spectra(records, parts)
    up = [(b, b - 4) for b in range(4, blocks)]
    swap2 = [(b, b ^ 2) for b in range(blocks)]
    swap1 = [(b, b ^ 1) for b in range(blocks)]
    mine = [spectra[0]]
    for s in range(1, parts):
        mine.append(lax.ppermute(spectra[s], "win", [(i, (i + s) % parts) for i in range(parts)]))
    far = [lax.ppermute(own, "chan", up) for own in mine]
    last = parts - 1
    early = range(last)
    gains = stack_gains(after(positions, far[0]), chans, parts * wins)
    call = functools.partial(cross_call, gains=gains, mine=mine)

    (acc_far,) = call(
        "cross_far", [("far", [(s, s) for s in early], None, False, 0)], sources={"far": far[:-1]}
    )
    far[last] = after(far[last], acc_far)
    mid, one, two = [], [], []
    half = chans // 2
    direct = lax.ppermute(mine[last][half:], "chan", [(b, b - 2) for b in range(2, blocks)])
    for s in range(parts):
        count = None if s < last else half
        mid.append(lax.ppermute(choose(2, mine[s], far[s], count), "chan", swap2))
        one.append(lax.ppermute(choose(1, mine[s], far[s]), "chan", swap1))
        if s < last:
            two.append(lax.ppermute(mid[s], "chan", swap1))
    done_far, acc_mid = call(
        "cross_most",
        [
            ("far", [(last, 0)], 0, True, 0),
            ("mid", [(s, s) for s in early], None, False, 1),
        ],
        sources={"far": far[last:], "mid": mid[:last]},
        acc_in=[acc_far],
    )
    direct = after(direct, acc_mid)
    two_direct = lax.ppermute(direct, "chan", swap1)
    mid[last] = after(mid[last], acc_mid)
    two.append(lax.ppermute(mid[last], "chan", swap1))
    (done_mid,) = call(
        "cross_mid", [("mid", [(last, (0, 1))], 0, True, 0)],
        sources={"mid": [mid[last], direct]}, acc_in=[acc_mid],
    )
    one[last] = after(one[last], done_mid)
    two[0] = after(two[0], done_mid)
    done_one, acc_two = call(
        "cross_next",
        [
            ("one", [(s, s) for s in range(parts)], None, True, 0),
            ("two", [(s, s) for s in early], None, False, 1),
        ],
        sources={"one": one, "two": two[:last]},
    )
    two[last] = after(two[last], acc_two)
    (out,) = call(
        "cross_last", [("two", [(last, (0, 1))], 0, True, None)],
        sources={"two": [two[last], two_direct]},
        acc_in=[acc_two], done=[done_far, done_mid, done_one],
    )
    bands = out.shape[3] // 2
    out = out.reshape(ROUNDS, chans, chans, bands, 2, LANES).transpose(0, 1, 2, 4, 3, 5)
    return out.reshape(ROUNDS, chans, chans, 2, bands * LANES)


def solution(mesh):
    return jax.shard_map(
        shards,
        mesh=mesh,
        in_specs=(P("chan", "win", None), P()),
        out_specs=P(None, "chan", None, None, "win"),
        check_vma=False,
    )
```
